32 devices in a mesh: fib: 16 (over z, x, core), pln: 2 (over y).
Axes of the slice: x: 2, y: 2, z: 4, core: 2. Of those that a mesh axis runs over, the one named last changes fastest.
Arguments:
- nodal_values: float32 [2, 16, 288, 1000], P('pln', 'fib'), may hold values from -6 to 6
- interp_matrix: float32 [1000, 512], replicated, may hold values from -0.1875 to 0.1875
- count_table: int32 [2, 16, 3], P('pln'), may hold values from 1 to 96, as said below
- slot_order: int32 [2, 16, 192], P('pln', 'fib'), may hold values from 0 to 191, each once within a row
- start_basis: float32 [768, 128], replicated, may hold values from -6 to 6
Outputs:
- core_values: float32 [2, 16, 128, 128], P('pln', 'fib')
The draws below stay inside these ranges and needn't reach their ends.
Inputs may be any that keep to these rules, and one draw needn't show every extreme that they name: count_table[j, o, d] elements of owner o come from the source d places before it along fib, cyclically; for every owner the 3 entries sum to 192 and one equals 96. `slot_order`: each owner's row is a permutation.
All inputs are finite; a program needn't handle non-finite values.
Results may differ from the reference program's by a relative error of at most 0.0003.
Values sent between devices are 32-bit elements; how exact they have to be, the bound alone decides.
No kernel may reach another device: no remote copies, remote signals or barrier semaphores. Data moves between devices by JAX's collectives and lax.ppermute only.
A program may use at most 64 MiB of HBM per device.

```python
import jax
import jax.numpy as jnp
from jax import lax

NX = 768
Q = 1000
TILE = 128
RANK = 128
WINDOW = 3
GRID_PTS = 512
OWNERS = 16
SLABS = 2
XB = 48
TT = 16
R_ELEM = 192
CAP = 96
E_SLOTS = 288


def draw_count_table(key, part):
    first_share = jax.random.randint(jax.random.fold_in(key, 11), (SLABS, OWNERS), 1, CAP)
    shares = jnp.stack([jnp.full((SLABS, OWNERS), CAP, jnp.int32), first_share, CAP - first_share], axis=-1)
    rotation = jax.random.randint(jax.random.fold_in(key, 12), (SLABS, OWNERS, 1), 0, WINDOW)
    ordering = (jnp.arange(WINDOW, dtype=jnp.int32)[None, None, :] + rotation) % WINDOW
    return jnp.take_along_axis(shares, ordering, axis=-1).astype(jnp.int32)


def shard_levels(own_key, dims, pieces, least, largest):
    gain = 1.0
    for axis_at, shards_of in pieces:
        heights = jax.random.uniform(jax.random.fold_in(jax.random.fold_in(own_key, 6), axis_at), (shards_of,), jnp.float32, least / len(pieces), largest / len(pieces))
        gain = gain * jnp.repeat(jnp.exp(heights), dims[axis_at] // shards_of).reshape((-1,) + (1,) * (len(dims) - 1 - axis_at))
    return gain


def noise(stream_key, extent, scale, reach, split=(), kind=jnp.bfloat16):
    gain = shard_levels(stream_key, extent, split, -0.22, 0.18) if split else 1.0
    drawn = jax.random.normal(stream_key, extent, jnp.float32) * scale * gain
    return jnp.minimum(jnp.maximum(drawn, -reach), reach).astype(kind)


def setup_inputs(seed: int = 0) -> dict:
    splits = jax.random.split(jax.random.key(seed), 6)
    nodal_values = noise(splits[0], (SLABS, OWNERS, E_SLOTS, Q), 1.0, 6.0, ((0, 2), (1, 16)), jnp.float32)
    interp_matrix = noise(splits[1], (Q, GRID_PTS), Q ** -0.5, 0.1875, (), jnp.float32)
    count_table = draw_count_table(jax.random.fold_in(splits[5], 71), 0)
    slot_order = jax.vmap(lambda own: jax.random.permutation(own, R_ELEM))(jax.random.split(splits[3], SLABS * OWNERS)).reshape((SLABS, OWNERS, R_ELEM)).astype(jnp.int32)
    start_basis = noise(splits[4], (NX, RANK), 1.0, 6.0, (), jnp.float32)
    return {"nodal_values": nodal_values, "interp_matrix": interp_matrix, "count_table": count_table, "slot_order": slot_order, "start_basis": start_basis}


def arrival_index(owner_table):
    sent_counts = jnp.stack([jnp.roll(owner_table[:, distance], -distance) for distance in range(WINDOW)], axis=1)
    starts = jnp.cumsum(sent_counts, axis=1) - sent_counts
    positions = jnp.arange(R_ELEM, dtype=jnp.int32)[None, :]
    owner_ids = jnp.arange(OWNERS, dtype=jnp.int32)[:, None]
    source_id = jnp.zeros((OWNERS, R_ELEM), jnp.int32)
    slot_id = jnp.zeros((OWNERS, R_ELEM), jnp.int32)
    offset = jnp.zeros((OWNERS, 1), jnp.int32)
    for distance in range(WINDOW - 1, -1, -1):
        taken_count = owner_table[:, distance:distance + 1].astype(jnp.int32)
        slot_begin = jnp.roll(starts[:, distance], distance)[:, None].astype(jnp.int32)
        inside = (positions >= offset) & (positions < offset + taken_count)
        source_id = jnp.where(inside, (owner_ids - distance) % OWNERS, source_id)
        slot_id = jnp.where(inside, slot_begin + positions - offset, slot_id)
        offset = offset + taken_count
    return (source_id.astype(jnp.int32), slot_id.astype(jnp.int32))

def reference(nodal_values, interp_matrix, count_table, slot_order, start_basis):
    full_precision = lax.Precision.HIGHEST

    def slab_field(operands):
        slab_nodes, owner_table, brick_order = operands
        source_id, slot_id = arrival_index(owner_table)
        gathered = slab_nodes[source_id, slot_id]
        grid_values = jnp.dot(gathered.reshape(-1, Q).astype(jnp.float32), interp_matrix.astype(jnp.float32), precision=full_precision, preferred_element_type=jnp.float32).reshape(OWNERS, R_ELEM, GRID_PTS)
        owner_ids = jnp.arange(OWNERS, dtype=jnp.int32)[:, None]
        brick_values = jnp.zeros_like(grid_values).at[owner_ids, brick_order].set(grid_values)
        fibre_field = brick_values.reshape(OWNERS, TT, XB, TILE).transpose(1, 0, 2, 3).reshape(TT, NX, TILE)
        gram_part = jnp.einsum('txf,tyf->xy', fibre_field, fibre_field, precision=full_precision)
        return (fibre_field, gram_part)
    fields, grams = lax.map(slab_field, (nodal_values, count_table, slot_order))
    gram_matrix = jnp.sum(grams, axis=0)
    image_matrix = jnp.dot(gram_matrix, start_basis, precision=full_precision)
    normal_matrix = jnp.dot(image_matrix.T, image_matrix, precision=full_precision)
    lower_factor = jnp.linalg.cholesky(normal_matrix)
    new_basis = jax.scipy.linalg.solve_triangular(lower_factor, image_matrix.T, lower=True).T
    core_values = jnp.einsum('xk,jtxf->jtkf', new_basis, fields, precision=full_precision)
    return core_values
```

```python
import functools

import jax
import jax.numpy as jnp
from jax import lax
from jax.experimental import pallas as pl
from jax.experimental.pallas import tpu as pltpu
from jax.sharding import PartitionSpec as P

F32 = jnp.float32
BF16 = jnp.bfloat16
SLAB = 8
VMEM = pl.BlockSpec(memory_space=pltpu.VMEM)
SMEM = pl.BlockSpec(memory_space=pltpu.SMEM)
BIG = pltpu.CompilerParams(vmem_limit_bytes=32 * 1024 * 1024)


def halves(value):
    high = value.astype(BF16)
    return high, (value - high.astype(F32)).astype(BF16)


def dot3(left, right, contract):
    dims = (contract, ((), ()))
    lh, ll = left
    rh, rl = right
    out = lax.dot_general(lh, rl, dims, preferred_element_type=F32)
    out += lax.dot_general(ll, rh, dims, preferred_element_type=F32)
    return out + lax.dot_general(lh, rh, dims, preferred_element_type=F32)


def interp_kernel(owners, table_ref, node_ref, interp_ref, *refs):
    outs, grid_scr = refs[:-1], refs[-1]
    window = len(outs)
    rows = outs[0].shape[0]
    slots = node_ref.shape[0]
    own = lax.axis_index("fib")
    grid_scr[:slots, :] = dot3(halves(node_ref[...]), halves(interp_ref[...]), ((1,), (0,)))
    outs[0][...] = grid_scr[:rows, :]
    start = table_ref[0, own]
    for distance in range(1, window):
        shift = lax.rem(start, SLAB)
        at = pl.multiple_of(start - shift, SLAB)
        wide = grid_scr[pl.ds(at, rows + SLAB), :]
        outs[distance][...] = pltpu.roll(wide, lax.rem(rows + SLAB - shift, rows + SLAB), 0)[:rows, :]
        start = start + table_ref[distance, lax.rem(own + distance, owners)]


def pick_kernel(rows, table_ref, order_ref, out_ref):
    elements, slots = out_ref.shape
    window = slots // rows
    own = lax.axis_index("fib")
    rank_at = lax.broadcasted_iota(jnp.int32, (elements, slots), 0)
    slot_at = lax.broadcasted_iota(jnp.int32, (elements, slots), 1)
    from_slot = jnp.zeros((elements, slots), jnp.bool_)
    start = 0
    for distance in range(window - 1, -1, -1):
        count = table_ref[distance, own]
        inside = (rank_at >= start) & (rank_at < start + count)
        from_slot = from_slot | (inside & (slot_at - distance * rows == rank_at - start))
        start = start + count
    place = jnp.broadcast_to(order_ref[...], (elements, elements))
    row = lax.broadcasted_iota(jnp.int32, (elements, elements), 0)
    to_place = jnp.where(place == row, 1.0, 0.0).astype(BF16)
    out_ref[...] = jnp.dot(
        to_place, jnp.where(from_slot, 1.0, 0.0).astype(BF16), preferred_element_type=F32
    )


def order_kernel(pick_ref, *refs):
    pieces, out_ref = refs[:-1], refs[-1]
    pick = pick_ref[...].astype(BF16)
    line = jnp.concatenate([piece[...] for piece in pieces], axis=0)
    high = line.astype(BF16)
    rest = line - high.astype(F32)
    mid = rest.astype(BF16)
    low = (rest - mid.astype(F32)).astype(BF16)
    out = jnp.dot(pick, low, preferred_element_type=F32)
    out += jnp.dot(pick, mid, preferred_element_type=F32)
    out_ref[...] = out + jnp.dot(pick, high, preferred_element_type=F32)


def plane_index(inner):
    return lax.rem(lax.axis_index("fib"), inner) * lax.axis_size("pln") + lax.axis_index("pln")


def image_kernel(inner, field_ref, start_ref, *refs):
    outs, image_scr = refs[:-1], refs[-1]
    rows = outs[0].shape[0]
    field = halves(field_ref[...])
    mixed = dot3(field, halves(start_ref[...]), ((0,), (0,)))
    image_scr[...] = dot3(field, halves(mixed), ((1,), (0,)))
    mine = plane_index(inner)
    for step, out in enumerate(outs):
        at = pl.multiple_of((mine ^ step) * rows, rows)
        out[...] = image_scr[pl.ds(at, rows), :]


def factor_kernel(inner, field_ref, *refs):
    chunks, out_ref, image_scr, work, line_scr = refs[:-4], refs[-4], refs[-3], refs[-2], refs[-1]
    rows = chunks[0].shape[0]
    rank = out_ref.shape[0]
    mine = plane_index(inner)
    for step, chunk in enumerate(chunks):
        at = pl.multiple_of((mine ^ step) * rows, rows)
        image_scr[pl.ds(at, rows), :] = chunk[...]
    image = halves(image_scr[...])
    work[:, :rank] = dot3(image, image, ((0,), (0,)))
    work[:, rank:] = dot3(image, halves(field_ref[...]), ((0,), (0,)))
    shape = (1, rank)
    for base in range(0, rank, SLAB):
        left = [work[base + k : base + k + 1, :rank] for k in range(SLAB)]
        right = [work[base + k : base + k + 1, rank:] for k in range(SLAB)]
        entry = [
            [jnp.broadcast_to(left[k][:, base + i : base + i + 1], shape) for i in range(SLAB)]
            for k in range(SLAB)
        ]
        for k in range(SLAB):
            scale = lax.rsqrt(entry[k][k])
            left[k] = left[k] * scale
            right[k] = right[k] * scale
            factor = {i: entry[k][i] * scale for i in range(k + 1, SLAB)}
            for i in range(k + 1, SLAB):
                for j in range(i, SLAB):
                    entry[i][j] = entry[i][j] - factor[i] * factor[j]
                left[i] = left[i] - factor[i] * left[k]
                right[i] = right[i] - factor[i] * right[k]
            out_ref[base + k : base + k + 1, :] = right[k]
            line_scr[k : k + 1, :rank] = left[k]
            line_scr[k : k + 1, rank:] = right[k]
        after = base + SLAB
        if after < rank:
            line = line_scr[...]
            high = line.astype(BF16).astype(F32)
            rest = line - high
            mid = rest.astype(BF16).astype(F32)
            low = rest - mid
            first = jnp.concatenate([high, high, mid, high, low, mid], axis=0).astype(BF16)
            second = jnp.concatenate([high, mid, high, low, high, mid], axis=0).astype(BF16)
            drop = lax.dot_general(
                first[:, :rank], second, (((0,), (0,)), ((), ())), preferred_element_type=F32
            )
            work[after:, :] = work[after:, :] - drop[after:, :]


def pairs_by(sizes, move):
    owners, planes = sizes
    out = []
    for fib in range(owners):
        for pln in range(planes):
            to_fib, to_pln = move(fib, pln)
            out.append((fib * planes + pln, to_fib * planes + to_pln))
    return out


def per_device(nodal_values, interp_matrix, count_table, slot_order, start_basis):
    nodes = nodal_values[0, 0]
    table = count_table[0].T
    owners = lax.axis_size("fib")
    planes = lax.axis_size("pln")
    sizes = (owners, planes)
    both = ("fib", "pln")
    window = table.shape[0]
    capacity = nodes.shape[0] // window
    points = interp_matrix.shape[1]
    elements = slot_order.shape[2]
    length, rank = start_basis.shape
    tile = points * elements // length
    piece = jax.ShapeDtypeStruct((capacity, points), F32)

    pieces = pl.pallas_call(
        functools.partial(interp_kernel, owners),
        out_shape=[piece] * window,
        in_specs=[SMEM, VMEM, VMEM],
        out_specs=[VMEM] * window,
        scratch_shapes=[pltpu.VMEM((nodes.shape[0] + SLAB, points), F32)],
        compiler_params=BIG,
        name="interp",
    )(table, nodes, interp_matrix)
    received = [pieces[0]] + [
        lax.ppermute(pieces[d], "fib", [(i, (i + d) % owners) for i in range(owners)])
        for d in range(1, window)
    ]
    pick = pl.pallas_call(
        functools.partial(pick_kernel, capacity),
        out_shape=jax.ShapeDtypeStruct((elements, capacity * window), F32),
        in_specs=[SMEM, VMEM],
        out_specs=VMEM,
        compiler_params=BIG,
        name="pick",
    )(table, slot_order[0])
    brick = pl.pallas_call(
        order_kernel,
        out_shape=jax.ShapeDtypeStruct((elements, points), F32),
        in_specs=[VMEM] * (1 + window),
        out_specs=VMEM,
        compiler_params=BIG,
        name="order",
    )(pick, *received)
    brick = brick.reshape(owners, length // owners, tile)
    field = lax.all_to_all(brick, "fib", split_axis=0, concat_axis=0, tiled=True)
    field = field.reshape(length, tile)

    inner = 4
    group = inner * planes
    rows = length // group
    steps = range(group)

    def plane_move(step):
        def move(fib, pln):
            to = ((fib % inner) * planes + pln) ^ step
            return fib - fib % inner + to // planes, to % planes

        return pairs_by(sizes, move)

    chunk = jax.ShapeDtypeStruct((rows, rank), F32)
    chunks = pl.pallas_call(
        functools.partial(image_kernel, inner),
        out_shape=[chunk] * group,
        in_specs=[VMEM] * 2,
        out_specs=[VMEM] * group,
        scratch_shapes=[pltpu.VMEM((length, rank), F32)],
        compiler_params=BIG,
        name="image",
    )(field, start_basis)
    total = chunks[0]
    for step in steps[1:]:
        total = total + lax.ppermute(chunks[step], both, plane_move(step))
    own_sum = total
    for step in range(1, owners // inner):
        moves = pairs_by(sizes, lambda fib, pln: ((fib + step * inner) % owners, pln))
        total = total + lax.ppermute(own_sum, both, moves)
    gathered = [total] + [lax.ppermute(total, both, plane_move(step)) for step in steps[1:]]
    core_values = pl.pallas_call(
        functools.partial(factor_kernel, inner),
        out_shape=jax.ShapeDtypeStruct((rank, tile), F32),
        in_specs=[VMEM] * (1 + group),
        out_specs=VMEM,
        scratch_shapes=[
            pltpu.VMEM((length, rank), F32),
            pltpu.VMEM((rank, rank + tile), F32),
            pltpu.VMEM((SLAB, rank + tile), F32),
        ],
        compiler_params=BIG,
        name="factor",
    )(field, *gathered)
    return core_values[None, None]


def solution(mesh):
    placed = (P("pln", "fib", None, None), P(), P("pln", None, None), P("pln", "fib", None), P())
    return jax.shard_map(
        per_device,
        mesh=mesh,
        in_specs=placed,
        out_specs=P("pln", "fib", None, None),
        check_vma=False,
    )
```

```python
import functools

import jax
import jax.numpy as jnp
from jax import lax
from jax.experimental import pallas as pl
from jax.experimental.pallas import tpu as pltpu
from jax.sharding import PartitionSpec as P

F32 = jnp.float32
BF16 = jnp.bfloat16
SLAB = 8
VMEM = pl.BlockSpec(memory_space=pltpu.VMEM)
SMEM = pl.BlockSpec(memory_space=pltpu.SMEM)
BIG = pltpu.CompilerParams(vmem_limit_bytes=32 * 1024 * 1024)


def halves(value):
    high = value.astype(BF16)
    return high, (value - high.astype(F32)).astype(BF16)


def dot3(left, right, contract):
    dims = (contract, ((), ()))
    lh, ll = left
    rh, rl = right
    out = lax.dot_general(lh, rl, dims, preferred_element_type=F32)
    out += lax.dot_general(ll, rh, dims, preferred_element_type=F32)
    return out + lax.dot_general(lh, rh, dims, preferred_element_type=F32)


def interp_kernel(owners, table_ref, node_ref, interp_ref, *refs):
    outs, grid_scr = refs[:-1], refs[-1]
    window = len(outs)
    rows = outs[0].shape[0]
    slots = node_ref.shape[0]
    own = lax.axis_index("fib")
    grid_scr[:slots, :] = dot3(halves(node_ref[...]), halves(interp_ref[...]), ((1,), (0,)))
    outs[0][...] = grid_scr[:rows, :]
    start = table_ref[0, 0, own]
    for distance in range(1, window):
        shift = lax.rem(start, SLAB)
        at = pl.multiple_of(start - shift, SLAB)
        wide = grid_scr[pl.ds(at, rows + SLAB), :]
        outs[distance][...] = pltpu.roll(wide, lax.rem(rows + SLAB - shift, rows + SLAB), 0)[:rows, :]
        start = start + table_ref[distance, 0, lax.rem(own + distance, owners)]


def pick_kernel(rows, table_ref, order_ref, out_ref):
    elements, slots = out_ref.shape
    window = slots // rows
    own = lax.axis_index("fib")
    rank_at = lax.broadcasted_iota(jnp.int32, (elements, slots), 0)
    slot_at = lax.broadcasted_iota(jnp.int32, (elements, slots), 1)
    from_slot = jnp.zeros((elements, slots), jnp.bool_)
    start = 0
    for distance in range(window - 1, -1, -1):
        count = table_ref[distance, 0, own]
        inside = (rank_at >= start) & (rank_at < start + count)
        from_slot = from_slot | (inside & (slot_at - distance * rows == rank_at - start))
        start = start + count
    place = jnp.broadcast_to(order_ref[...], (elements, elements))
    row = lax.broadcasted_iota(jnp.int32, (elements, elements), 0)
    to_place = jnp.where(place == row, 1.0, 0.0).astype(BF16)
    out_ref[...] = jnp.dot(
        to_place, jnp.where(from_slot, 1.0, 0.0).astype(BF16), preferred_element_type=F32
    )


def order_kernel(pick_ref, *refs):
    pieces, out_ref = refs[:-1], refs[-1]
    pick = pick_ref[...].astype(BF16)
    line = jnp.concatenate([piece[...] for piece in pieces], axis=0)
    high = line.astype(BF16)
    rest = line - high.astype(F32)
    mid = rest.astype(BF16)
    low = (rest - mid.astype(F32)).astype(BF16)
    out = jnp.dot(pick, low, preferred_element_type=F32)
    out += jnp.dot(pick, mid, preferred_element_type=F32)
    out_ref[...] = out + jnp.dot(pick, high, preferred_element_type=F32)


def image_kernel(field_ref, start_ref, out_ref):
    field = halves(field_ref[...])
    mixed = dot3(field, halves(start_ref[...]), ((0,), (0,)))
    out_ref[...] = dot3(field, halves(mixed), ((1,), (0,)))


def factor_kernel(field_ref, image_ref, out_ref, work, line_scr):
    rank = out_ref.shape[0]
    image = halves(image_ref[...])
    work[:, :rank] = dot3(image, image, ((0,), (0,)))
    work[:, rank:] = dot3(image, halves(field_ref[...]), ((0,), (0,)))
    shape = (1, rank)
    for base in range(0, rank, SLAB):
        left = [work[base + k : base + k + 1, :rank] for k in range(SLAB)]
        right = [work[base + k : base + k + 1, rank:] for k in range(SLAB)]
        entry = [
            [jnp.broadcast_to(left[k][:, base + i : base + i + 1], shape) for i in range(SLAB)]
            for k in range(SLAB)
        ]
        for k in range(SLAB):
            scale = lax.rsqrt(entry[k][k])
            left[k] = left[k] * scale
            right[k] = right[k] * scale
            factor = {i: entry[k][i] * scale for i in range(k + 1, SLAB)}
            for i in range(k + 1, SLAB):
                for j in range(i, SLAB):
                    entry[i][j] = entry[i][j] - factor[i] * factor[j]
                left[i] = left[i] - factor[i] * left[k]
                right[i] = right[i] - factor[i] * right[k]
            out_ref[base + k : base + k + 1, :] = right[k]
            line_scr[k : k + 1, :rank] = left[k]
            line_scr[k : k + 1, rank:] = right[k]
        after = base + SLAB
        if after < rank:
            line = line_scr[...]
            high = line.astype(BF16).astype(F32)
            rest = line - high
            mid = rest.astype(BF16).astype(F32)
            low = rest - mid
            first = jnp.concatenate([high, high, mid, high, low, mid], axis=0).astype(BF16)
            second = jnp.concatenate([high, mid, high, low, high, mid], axis=0).astype(BF16)
            drop = lax.dot_general(
                first[:, :rank], second, (((0,), (0,)), ((), ())), preferred_element_type=F32
            )
            work[after:, :] = work[after:, :] - drop[after:, :]


def pairs_by(sizes, move):
    owners, planes = sizes
    out = []
    for fib in range(owners):
        for pln in range(planes):
            to_fib, to_pln = move(fib, pln)
            out.append((fib * planes + pln, to_fib * planes + to_pln))
    return out


def per_device(nodal_values, interp_matrix, count_table, slot_order, start_basis):
    nodes = nodal_values[0, 0]
    table = jnp.transpose(count_table, (2, 0, 1))
    owners = lax.axis_size("fib")
    planes = lax.axis_size("pln")
    sizes = (owners, planes)
    both = ("fib", "pln")
    window = table.shape[0]
    capacity = nodes.shape[0] // window
    points = interp_matrix.shape[1]
    elements = slot_order.shape[2]
    length, rank = start_basis.shape
    tile = points * elements // length
    piece = jax.ShapeDtypeStruct((capacity, points), F32)

    pieces = pl.pallas_call(
        functools.partial(interp_kernel, owners),
        out_shape=[piece] * window,
        in_specs=[SMEM, VMEM, VMEM],
        out_specs=[VMEM] * window,
        scratch_shapes=[pltpu.VMEM((nodes.shape[0] + SLAB, points), F32)],
        compiler_params=BIG,
        name="interp",
    )(table, nodes, interp_matrix)
    received = [pieces[0]] + [
        lax.ppermute(pieces[d], "fib", [(i, (i + d) % owners) for i in range(owners)])
        for d in range(1, window)
    ]
    pick = pl.pallas_call(
        functools.partial(pick_kernel, capacity),
        out_shape=jax.ShapeDtypeStruct((elements, capacity * window), F32),
        in_specs=[SMEM, VMEM],
        out_specs=VMEM,
        compiler_params=BIG,
        name="pick",
    )(table, slot_order[0])
    brick = pl.pallas_call(
        order_kernel,
        out_shape=jax.ShapeDtypeStruct((elements, points), F32),
        in_specs=[VMEM] * (1 + window),
        out_specs=VMEM,
        compiler_params=BIG,
        name="order",
    )(pick, *received)
    brick = brick.reshape(owners, length // owners, tile)
    field = lax.all_to_all(brick, "fib", split_axis=0, concat_axis=0, tiled=True)
    field = field.reshape(length, tile)

    inner = 4
    group = inner * planes
    rows = length // group
    planes_of = [
        [
            (base + i // planes) * planes + i % planes
            for i in range(group)
        ]
        for base in range(0, owners, inner)
    ]

    def plane_exchange(value):
        return lax.all_to_all(
            value, both, split_axis=0, concat_axis=0, axis_index_groups=planes_of, tiled=True
        )

    image = pl.pallas_call(
        image_kernel,
        out_shape=jax.ShapeDtypeStruct((length, rank), F32),
        in_specs=[VMEM] * 2,
        out_specs=VMEM,
        compiler_params=BIG,
        name="image",
    )(field, start_basis)
    own_sum = jnp.sum(plane_exchange(image).reshape(group, rows, rank), axis=0)
    total = own_sum
    for step in range(1, owners // inner):
        moves = pairs_by(sizes, lambda fib, pln: ((fib + step * inner) % owners, pln))
        total = total + lax.ppermute(own_sum, both, moves)
    image = plane_exchange(jnp.tile(total, (group, 1)))
    core_values = pl.pallas_call(
        factor_kernel,
        out_shape=jax.ShapeDtypeStruct((rank, tile), F32),
        in_specs=[VMEM] * 2,
        out_specs=VMEM,
        scratch_shapes=[
            pltpu.VMEM((rank, rank + tile), F32),
            pltpu.VMEM((SLAB, rank + tile), F32),
        ],
        compiler_params=BIG,
        name="factor",
    )(field, image)
    return core_values[None, None]


def solution(mesh):
    placed = (P("pln", "fib", None, None), P(), P("pln", None, None), P("pln", "fib", None), P())
    return jax.shard_map(
        per_device,
        mesh=mesh,
        in_specs=placed,
        out_specs=P("pln", "fib", None, None),
        check_vma=False,
    )
```

```python
import functools

import jax
import jax.numpy as jnp
from jax import lax
from jax.experimental import pallas as pl
from jax.experimental.pallas import tpu as pltpu
from jax.sharding import PartitionSpec as P

F32 = jnp.float32
BF16 = jnp.bfloat16
SLAB = 8
VMEM = pl.BlockSpec(memory_space=pltpu.VMEM)
SMEM = pl.BlockSpec(memory_space=pltpu.SMEM)
BIG = pltpu.CompilerParams(vmem_limit_bytes=32 * 1024 * 1024)


def halves(value):
    high = value.astype(BF16)
    return high, (value - high.astype(F32)).astype(BF16)


def dot3(left, right, contract):
    dims = (contract, ((), ()))
    lh, ll = left
    rh, rl = right
    out = lax.dot_general(lh, rl, dims, preferred_element_type=F32)
    out += lax.dot_general(ll, rh, dims, preferred_element_type=F32)
    return out + lax.dot_general(lh, rh, dims, preferred_element_type=F32)


def interp_kernel(owners, table_ref, node_ref, interp_ref, *refs):
    outs, grid_scr = refs[:-1], refs[-1]
    window = len(outs)
    rows = outs[0].shape[0]
    slots = node_ref.shape[0]
    own = lax.axis_index("fib")
    grid_scr[:slots, :] = dot3(halves(node_ref[...]), halves(interp_ref[...]), ((1,), (0,)))
    outs[0][...] = grid_scr[:rows, :]
    start = table_ref[0, 0, own]
    for distance in range(1, window):
        shift = lax.rem(start, SLAB)
        at = pl.multiple_of(start - shift, SLAB)
        wide = grid_scr[pl.ds(at, rows + SLAB), :]
        outs[distance][...] = pltpu.roll(wide, lax.rem(rows + SLAB - shift, rows + SLAB), 0)[:rows, :]
        start = start + table_ref[distance, 0, lax.rem(own + distance, owners)]


def pick_kernel(rows, table_ref, order_ref, out_ref):
    elements, slots = out_ref.shape
    window = slots // rows
    own = lax.axis_index("fib")
    rank_at = lax.broadcasted_iota(jnp.int32, (elements, slots), 0)
    slot_at = lax.broadcasted_iota(jnp.int32, (elements, slots), 1)
    from_slot = jnp.zeros((elements, slots), jnp.bool_)
    start = 0
    for distance in range(window - 1, -1, -1):
        count = table_ref[distance, 0, own]
        inside = (rank_at >= start) & (rank_at < start + count)
        from_slot = from_slot | (inside & (slot_at - distance * rows == rank_at - start))
        start = start + count
    place = jnp.broadcast_to(order_ref[...], (elements, elements))
    row = lax.broadcasted_iota(jnp.int32, (elements, elements), 0)
    to_place = jnp.where(place == row, 1.0, 0.0).astype(BF16)
    out_ref[...] = jnp.dot(
        to_place, jnp.where(from_slot, 1.0, 0.0).astype(BF16), preferred_element_type=F32
    )


def order_kernel(pick_ref, *refs):
    pieces, out_ref = refs[:-1], refs[-1]
    pick = pick_ref[...].astype(BF16)
    line = jnp.concatenate([piece[...] for piece in pieces], axis=0)
    high = line.astype(BF16)
    rest = line - high.astype(F32)
    mid = rest.astype(BF16)
    low = (rest - mid.astype(F32)).astype(BF16)
    out = jnp.dot(pick, low, preferred_element_type=F32)
    out += jnp.dot(pick, mid, preferred_element_type=F32)
    out_ref[...] = out + jnp.dot(pick, high, preferred_element_type=F32)


def bit_place(order):
    index = 0
    for axis, mask in order:
        index = index * 2 + lax.rem(lax.div(lax.axis_index(axis), mask), 2)
    return index


def image_kernel(orders, field_ref, start_ref, *refs):
    outs, image_scr = refs[:-1], refs[-1]
    length = field_ref.shape[0]
    field = halves(field_ref[...])
    mixed = dot3(field, halves(start_ref[...]), ((0,), (0,)))
    image_scr[...] = dot3(field, halves(mixed), ((1,), (0,)))
    share = length // len(orders)
    for chain, order in enumerate(orders):
        count = 2 ** len(order)
        rows = share // count
        mine = bit_place(order)
        for step in range(count):
            at = pl.multiple_of(chain * share + (mine ^ step) * rows, rows)
            half, place = divmod(step, count // 2)
            outs[2 * chain + half][place * rows : (place + 1) * rows, :] = image_scr[pl.ds(at, rows), :]


def factor_kernel(orders, field_ref, *refs):
    parts, out_ref, image_scr, work, line_scr = refs[:-4], refs[-4], refs[-3], refs[-2], refs[-1]
    length, rank = image_scr.shape
    share = length // len(orders)
    for chain, order in enumerate(orders):
        count = 2 ** len(order)
        rows = share // count
        mine = bit_place(order)
        for step in range(count):
            at = pl.multiple_of(chain * share + (mine ^ step) * rows, rows)
            half, place = divmod(step, count // 2)
            image_scr[pl.ds(at, rows), :] = parts[2 * chain + half][place * rows : (place + 1) * rows, :]
    image = halves(image_scr[...])
    work[:, :rank] = dot3(image, image, ((0,), (0,)))
    work[:, rank:] = dot3(image, halves(field_ref[...]), ((0,), (0,)))
    shape = (1, rank)
    for base in range(0, rank, SLAB):
        left = [work[base + k : base + k + 1, :rank] for k in range(SLAB)]
        right = [work[base + k : base + k + 1, rank:] for k in range(SLAB)]
        entry = [
            [jnp.broadcast_to(left[k][:, base + i : base + i + 1], shape) for i in range(SLAB)]
            for k in range(SLAB)
        ]
        for k in range(SLAB):
            scale = lax.rsqrt(entry[k][k])
            left[k] = left[k] * scale
            right[k] = right[k] * scale
            factor = {i: entry[k][i] * scale for i in range(k + 1, SLAB)}
            for i in range(k + 1, SLAB):
                for j in range(i, SLAB):
                    entry[i][j] = entry[i][j] - factor[i] * factor[j]
                left[i] = left[i] - factor[i] * left[k]
                right[i] = right[i] - factor[i] * right[k]
            out_ref[base + k : base + k + 1, :] = right[k]
            line_scr[k : k + 1, :rank] = left[k]
            line_scr[k : k + 1, rank:] = right[k]
        after = base + SLAB
        if after < rank:
            line = line_scr[...]
            high = line.astype(BF16).astype(F32)
            rest = line - high
            mid = rest.astype(BF16).astype(F32)
            low = rest - mid
            first = jnp.concatenate([high, high, mid, high, low, mid], axis=0).astype(BF16)
            second = jnp.concatenate([high, mid, high, low, high, mid], axis=0).astype(BF16)
            drop = lax.dot_general(
                first[:, :rank], second, (((0,), (0,)), ((), ())), preferred_element_type=F32
            )
            work[after:, :] = work[after:, :] - drop[after:, :]


def swapped(value, bit):
    axis, mask = bit
    return lax.ppermute(value, axis, [(i, i ^ mask) for i in range(lax.axis_size(axis))])


def masks(axis, low, high):
    out = []
    while low < high:
        out.append((axis, low))
        low *= 2
    return out


def per_device(nodal_values, interp_matrix, count_table, slot_order, start_basis):
    nodes = nodal_values[0, 0]
    table = jnp.transpose(count_table, (2, 0, 1))
    owners = lax.axis_size("fib")
    planes = lax.axis_size("pln")
    window = table.shape[0]
    capacity = nodes.shape[0] // window
    points = interp_matrix.shape[1]
    elements = slot_order.shape[2]
    length, rank = start_basis.shape
    tile = points * elements // length
    piece = jax.ShapeDtypeStruct((capacity, points), F32)

    pieces = pl.pallas_call(
        functools.partial(interp_kernel, owners),
        out_shape=[piece] * window,
        in_specs=[SMEM, VMEM, VMEM],
        out_specs=[VMEM] * window,
        scratch_shapes=[pltpu.VMEM((nodes.shape[0] + SLAB, points), F32)],
        compiler_params=BIG,
        name="interp",
    )(table, nodes, interp_matrix)
    received = [pieces[0]] + [
        lax.ppermute(pieces[d], "fib", [(i, (i + d) % owners) for i in range(owners)])
        for d in range(1, window)
    ]
    pick = pl.pallas_call(
        functools.partial(pick_kernel, capacity),
        out_shape=jax.ShapeDtypeStruct((elements, capacity * window), F32),
        in_specs=[SMEM, VMEM],
        out_specs=VMEM,
        compiler_params=BIG,
        name="pick",
    )(table, slot_order[0])
    brick = pl.pallas_call(
        order_kernel,
        out_shape=jax.ShapeDtypeStruct((elements, points), F32),
        in_specs=[VMEM] * (1 + window),
        out_specs=VMEM,
        compiler_params=BIG,
        name="order",
    )(pick, *received)
    brick = brick.reshape(owners, length // owners, tile)
    field = lax.all_to_all(brick, "fib", split_axis=0, concat_axis=0, tiled=True)
    field = field.reshape(length, tile)

    inner = 4
    near = masks("fib", 1, inner)
    across = masks("pln", 1, planes)
    far = masks("fib", inner, owners)
    orders = [near + across, near[:1] + across + near[1:]]
    if length % (16 * inner * planes) != 0:
        orders = orders[:1]
    half = jax.ShapeDtypeStruct((length // len(orders) // 2, rank), F32)
    halves_out = pl.pallas_call(
        functools.partial(image_kernel, orders),
        out_shape=[half] * (2 * len(orders)),
        in_specs=[VMEM] * 2,
        out_specs=[VMEM] * (2 * len(orders)),
        scratch_shapes=[pltpu.VMEM((length, rank), F32)],
        compiler_params=BIG,
        name="image",
    )(field, start_basis)
    keep = list(halves_out[0::2])
    send = list(halves_out[1::2])
    chains = range(len(orders))
    depth = len(orders[0])
    for level in range(depth):
        got = [swapped(send[c], orders[c][level]) for c in chains]
        for c in chains:
            total = keep[c] + got[c]
            if level + 1 < depth:
                middle = total.shape[0] // 2
                keep[c], send[c] = total[:middle], total[middle:]
            else:
                keep[c] = total
    for bit in far:
        got = [swapped(keep[c], bit) for c in chains]
        keep = [keep[c] + got[c] for c in chains]
    for level in range(depth - 1, -1, -1):
        got = [swapped(keep[c], orders[c][level]) for c in chains]
        if level:
            keep = [jnp.concatenate([keep[c], got[c]], axis=0) for c in chains]
    parts = [part for c in chains for part in (keep[c], got[c])]
    core_values = pl.pallas_call(
        functools.partial(factor_kernel, orders),
        out_shape=jax.ShapeDtypeStruct((rank, tile), F32),
        in_specs=[VMEM] * (1 + len(parts)),
        out_specs=VMEM,
        scratch_shapes=[
            pltpu.VMEM((length, rank), F32),
            pltpu.VMEM((rank, rank + tile), F32),
            pltpu.VMEM((SLAB, rank + tile), F32),
        ],
        compiler_params=BIG,
        name="factor",
    )(field, *parts)
    return core_values[None, None]


def solution(mesh):
    placed = (P("pln", "fib", None, None), P(), P("pln", None, None), P("pln", "fib", None), P())
    return jax.shard_map(
        per_device,
        mesh=mesh,
        in_specs=placed,
        out_specs=P("pln", "fib", None, None),
        check_vma=False,
    )
```

```python
import functools

import jax
import jax.numpy as jnp
from jax import lax
from jax.experimental import pallas as pl
from jax.experimental.pallas import tpu as pltpu
from jax.sharding import PartitionSpec as P

F32 = jnp.float32
BF16 = jnp.bfloat16
SLAB = 8
VMEM = pl.BlockSpec(memory_space=pltpu.VMEM)
SMEM = pl.BlockSpec(memory_space=pltpu.SMEM)
BIG = pltpu.CompilerParams(vmem_limit_bytes=32 * 1024 * 1024)


def halves(value):
    high = value.astype(BF16)
    return high, (value - high.astype(F32)).astype(BF16)


def dot3(left, right, contract):
    dims = (contract, ((), ()))
    lh, ll = left
    rh, rl = right
    out = lax.dot_general(lh, rl, dims, preferred_element_type=F32)
    out += lax.dot_general(ll, rh, dims, preferred_element_type=F32)
    return out + lax.dot_general(lh, rh, dims, preferred_element_type=F32)


def interp_kernel(owners, table_ref, node_ref, interp_ref, *refs):
    outs, grid_scr = refs[:-1], refs[-1]
    window = len(outs)
    rows = outs[0].shape[0]
    slots = node_ref.shape[0]
    own = lax.axis_index("fib")
    grid_scr[:slots, :] = dot3(halves(node_ref[...]), halves(interp_ref[...]), ((1,), (0,)))
    outs[0][...] = grid_scr[:rows, :]
    start = table_ref[0, 0, own]
    for distance in range(1, window):
        shift = lax.rem(start, SLAB)
        at = pl.multiple_of(start - shift, SLAB)
        wide = grid_scr[pl.ds(at, rows + SLAB), :]
        outs[distance][...] = pltpu.roll(wide, lax.rem(rows + SLAB - shift, rows + SLAB), 0)[:rows, :]
        start = start + table_ref[distance, 0, lax.rem(own + distance, owners)]


def pick_kernel(rows, per_tile, relative, table_ref, order_ref, out_ref):
    elements, slots = out_ref.shape
    window = slots // rows
    own = lax.axis_index("fib")
    rank_at = lax.broadcasted_iota(jnp.int32, (elements, slots), 0)
    slot_at = lax.broadcasted_iota(jnp.int32, (elements, slots), 1)
    from_slot = jnp.zeros((elements, slots), jnp.bool_)
    start = 0
    for distance in range(window - 1, -1, -1):
        count = table_ref[distance, 0, own]
        inside = (rank_at >= start) & (rank_at < start + count)
        from_slot = from_slot | (inside & (slot_at - distance * rows == rank_at - start))
        start = start + count
    place = order_ref[...]
    if relative:
        tile = lax.div(place, jnp.full_like(place, per_tile))
        inside = place - tile * per_tile
        apart = tile ^ own
        place = ((apart & 1) * (elements // per_tile // 2) + (apart >> 1)) * per_tile + inside
    place = jnp.broadcast_to(place, (elements, elements))
    row = lax.broadcasted_iota(jnp.int32, (elements, elements), 0)
    to_place = jnp.where(place == row, 1.0, 0.0).astype(BF16)
    out_ref[...] = jnp.dot(
        to_place, jnp.where(from_slot, 1.0, 0.0).astype(BF16), preferred_element_type=F32
    )


def order_kernel(pick_ref, *refs):
    pieces, outs = refs[:-2], refs[-2:]
    pick = pick_ref[...].astype(BF16)
    line = jnp.concatenate([piece[...] for piece in pieces], axis=0)
    high = line.astype(BF16)
    rest = line - high.astype(F32)
    mid = rest.astype(BF16)
    low = (rest - mid.astype(F32)).astype(BF16)
    out = jnp.dot(pick, low, preferred_element_type=F32)
    out += jnp.dot(pick, mid, preferred_element_type=F32)
    out += jnp.dot(pick, high, preferred_element_type=F32)
    half = out.shape[0] // 2
    outs[0][...] = out[:half]
    outs[1][...] = out[half:]


def bit_place(order):
    index = 0
    for axis, mask in order:
        index = index * 2 + lax.rem(lax.div(lax.axis_index(axis), mask), 2)
    return index


def image_kernel(near, mid, blocks, *refs):
    block_refs, start_ref, keep_ref, send_ref, field_ref, image_scr = refs[:blocks], *refs[blocks:]
    length = field_ref.shape[0]
    if blocks > 1:
        own = lax.axis_index("fib")
        each = length // (2 * blocks)
        for step, block in enumerate(block_refs):
            for core in range(2):
                at = pl.multiple_of((own ^ (2 * step + core)) * each, each)
                field_ref[pl.ds(at, each), :] = block[core * each : (core + 1) * each, :]
    else:
        field_ref[...] = block_refs[0][...]
    field = halves(field_ref[...])
    mixed = dot3(field, halves(start_ref[...]), ((0,), (0,)))
    image_scr[...] = dot3(field, halves(mixed), ((1,), (0,)))
    count = 2 ** len(mid)
    rows = length // (2 * count)
    core, place = bit_place(near), bit_place(mid)
    for step in range(count):
        at = pl.multiple_of((core * count + (place ^ step)) * rows, rows)
        keep_ref[step * rows : (step + 1) * rows, :] = image_scr[pl.ds(at, rows), :]
        at = pl.multiple_of(((1 - core) * count + (place ^ step)) * rows, rows)
        send_ref[step * rows : (step + 1) * rows, :] = image_scr[pl.ds(at, rows), :]


def factor_kernel(near, mid, field_ref, own_ref, other_ref, out_ref, image_scr, work, line_scr):
    length, rank = image_scr.shape
    count = 2 ** len(mid)
    rows = length // (2 * count)
    core, place = bit_place(near), bit_place(mid)
    for step in range(count):
        at = pl.multiple_of((core * count + (place ^ step)) * rows, rows)
        image_scr[pl.ds(at, rows), :] = own_ref[step * rows : (step + 1) * rows, :]
        at = pl.multiple_of(((1 - core) * count + (place ^ step)) * rows, rows)
        image_scr[pl.ds(at, rows), :] = other_ref[step * rows : (step + 1) * rows, :]
    image = halves(image_scr[...])
    work[:, :rank] = dot3(image, image, ((0,), (0,)))
    work[:, rank:] = dot3(image, halves(field_ref[...]), ((0,), (0,)))
    shape = (1, rank)
    for base in range(0, rank, SLAB):
        left = [work[base + k : base + k + 1, :rank] for k in range(SLAB)]
        right = [work[base + k : base + k + 1, rank:] for k in range(SLAB)]
        entry = [
            [jnp.broadcast_to(left[k][:, base + i : base + i + 1], shape) for i in range(SLAB)]
            for k in range(SLAB)
        ]
        for k in range(SLAB):
            scale = lax.rsqrt(entry[k][k])
            left[k] = left[k] * scale
            right[k] = right[k] * scale
            factor = {i: entry[k][i] * scale for i in range(k + 1, SLAB)}
            for i in range(k + 1, SLAB):
                for j in range(i, SLAB):
                    entry[i][j] = entry[i][j] - factor[i] * factor[j]
                left[i] = left[i] - factor[i] * left[k]
                right[i] = right[i] - factor[i] * right[k]
            out_ref[base + k : base + k + 1, :] = right[k]
            line_scr[k : k + 1, :rank] = left[k]
            line_scr[k : k + 1, rank:] = right[k]
        after = base + SLAB
        if after < rank:
            line = line_scr[...]
            high = line.astype(BF16).astype(F32)
            rest = line - high
            mid = rest.astype(BF16).astype(F32)
            low = rest - mid
            first = jnp.concatenate([high, high, mid, high, low, mid], axis=0).astype(BF16)
            second = jnp.concatenate([high, mid, high, low, high, mid], axis=0).astype(BF16)
            drop = lax.dot_general(
                first[:, :rank], second, (((0,), (0,)), ((), ())), preferred_element_type=F32
            )
            work[after:, :] = work[after:, :] - drop[after:, :]


def swapped(value, bits, step=1):
    apart = [bit for at, bit in enumerate(reversed(bits)) if step >> at & 1]
    peers = {axis: sum(mask for name, mask in apart if name == axis) for axis in ("fib", "pln")}
    owners, planes = lax.axis_size("fib"), lax.axis_size("pln")
    pairs = []
    for i in range(owners * planes):
        fib, pln = divmod(i, planes)
        pairs.append((i, (fib ^ peers["fib"]) * planes + (pln ^ peers["pln"])))
    return lax.ppermute(value, ("fib", "pln"), pairs)


def masks(axis, low, high):
    out = []
    while low < high:
        out.append((axis, low))
        low *= 2
    return out


def per_device(nodal_values, interp_matrix, count_table, slot_order, start_basis):
    nodes = nodal_values[0, 0]
    table = jnp.transpose(count_table, (2, 0, 1))
    owners = lax.axis_size("fib")
    planes = lax.axis_size("pln")
    window = table.shape[0]
    capacity = nodes.shape[0] // window
    points = interp_matrix.shape[1]
    elements = slot_order.shape[2]
    length, rank = start_basis.shape
    tile = points * elements // length
    piece = jax.ShapeDtypeStruct((capacity, points), F32)
    direct = length // owners % SLAB == 0

    pieces = pl.pallas_call(
        functools.partial(interp_kernel, owners),
        out_shape=[piece] * window,
        in_specs=[SMEM, VMEM, VMEM],
        out_specs=[VMEM] * window,
        scratch_shapes=[pltpu.VMEM((nodes.shape[0] + SLAB, points), F32)],
        compiler_params=BIG,
        name="interp",
    )(table, nodes, interp_matrix)
    received = [pieces[0]] + [
        lax.ppermute(pieces[d], "fib", [(i, (i + d) % owners) for i in range(owners)])
        for d in range(1, window)
    ]
    pick = pl.pallas_call(
        functools.partial(pick_kernel, capacity, elements // owners, direct),
        out_shape=jax.ShapeDtypeStruct((elements, capacity * window), F32),
        in_specs=[SMEM, VMEM],
        out_specs=VMEM,
        compiler_params=BIG,
        name="pick",
    )(table, slot_order[0])
    brick = pl.pallas_call(
        order_kernel,
        out_shape=[jax.ShapeDtypeStruct((elements // 2, points), F32)] * 2,
        in_specs=[VMEM] * (1 + window),
        out_specs=[VMEM] * 2,
        compiler_params=BIG,
        name="order",
    )(pick, *received)
    near = masks("fib", 1, 2)
    mid = masks("fib", 2, 4) + masks("pln", 1, planes)
    far = masks("fib", 4, owners)
    if direct:
        chips = masks("fib", 2, owners)[::-1]
        blocks = owners // 2
        shape = (blocks, length // owners, tile)
        own, other = (half.reshape(shape) for half in brick)
        both = jnp.concatenate([own, swapped(other, near)], axis=1)
        order = sorted(range(1, blocks), reverse=True)
        got = {step: swapped(both[step], chips, step) for step in order}
        got[0] = both[0]
        field_parts = [got[step] for step in range(blocks)]
    else:
        whole = jnp.concatenate(brick, axis=0).reshape(owners, length // owners, tile)
        whole = lax.all_to_all(whole, "fib", split_axis=0, concat_axis=0, tiled=True)
        field_parts = [whole.reshape(length, tile)]

    half = jax.ShapeDtypeStruct((length // 2, rank), F32)
    keep, send, field = pl.pallas_call(
        functools.partial(image_kernel, near, mid, len(field_parts)),
        out_shape=[half, half, jax.ShapeDtypeStruct((length, tile), F32)],
        in_specs=[VMEM] * (len(field_parts) + 1),
        out_specs=[VMEM] * 3,
        scratch_shapes=[pltpu.VMEM((length, rank), F32)],
        compiler_params=BIG,
        name="image",
    )(*field_parts, start_basis)
    count = 2 ** len(mid)
    chunks = (keep + swapped(send, near)).reshape(count, length // (2 * count), rank)
    total = chunks[0]
    for got in [swapped(chunks[step], mid, step) for step in range(count - 1, 0, -1)]:
        total = total + got
    own = total
    for got in [swapped(own, far, step) for step in range(2 ** len(far) - 1, 0, -1)]:
        total = total + got
    own = jnp.concatenate([total] + [swapped(total, mid, step) for step in range(1, count)], axis=0)
    other = swapped(own, near)
    core_values = pl.pallas_call(
        functools.partial(factor_kernel, near, mid),
        out_shape=jax.ShapeDtypeStruct((rank, tile), F32),
        in_specs=[VMEM] * 3,
        out_specs=VMEM,
        scratch_shapes=[
            pltpu.VMEM((length, rank), F32),
            pltpu.VMEM((rank, rank + tile), F32),
            pltpu.VMEM((SLAB, rank + tile), F32),
        ],
        compiler_params=BIG,
        name="factor",
    )(field, own, other)
    return core_values[None, None]


def solution(mesh):
    placed = (P("pln", "fib", None, None), P(), P("pln", None, None), P("pln", "fib", None), P())
    return jax.shard_map(
        per_device,
        mesh=mesh,
        in_specs=placed,
        out_specs=P("pln", "fib", None, None),
        check_vma=False,
    )
```

```python
import functools

import jax
import jax.numpy as jnp
from jax import lax
from jax.experimental import pallas as pl
from jax.experimental.pallas import tpu as pltpu
from jax.sharding import PartitionSpec as P

F32 = jnp.float32
BF16 = jnp.bfloat16
SLAB = 8
VMEM = pl.BlockSpec(memory_space=pltpu.VMEM)
SMEM = pl.BlockSpec(memory_space=pltpu.SMEM)
BIG = pltpu.CompilerParams(vmem_limit_bytes=32 * 1024 * 1024)


def halves(value):
    high = value.astype(BF16)
    return high, (value - high.astype(F32)).astype(BF16)


def dot3(left, right, contract):
    dims = (contract, ((), ()))
    lh, ll = left
    rh, rl = right
    out = lax.dot_general(lh, rl, dims, preferred_element_type=F32)
    out += lax.dot_general(ll, rh, dims, preferred_element_type=F32)
    return out + lax.dot_general(lh, rh, dims, preferred_element_type=F32)


def interp_kernel(owners, table_ref, node_ref, interp_ref, near_ref, far_ref, last_ref, grid_scr):
    rows = last_ref.shape[0]
    slots = node_ref.shape[0]
    own = lax.axis_index("fib")
    grid_scr[:slots, :] = dot3(halves(node_ref[...]), halves(interp_ref[...]), ((1,), (0,)))
    near_ref[:rows, :] = grid_scr[:rows, :]
    start = table_ref[0, 0, own]
    for distance in range(1, 3):
        shift = lax.rem(start, SLAB)
        at = pl.multiple_of(start - shift, SLAB)
        wide = grid_scr[pl.ds(at, rows + SLAB), :]
        piece = pltpu.roll(wide, lax.rem(rows + SLAB - shift, rows + SLAB), 0)[:rows, :]
        if distance == 1:
            near_ref[rows:, :] = piece
            far_ref[:rows, :] = piece
        else:
            far_ref[rows:, :] = piece
            last_ref[...] = piece
        start = start + table_ref[distance, 0, lax.rem(own + distance, owners)]


def pick_kernel(rows, per_tile, table_ref, order_ref, order_own_ref, out_ref):
    elements = order_ref.shape[1]
    slots = out_ref.shape[1]
    chip = lax.div(lax.axis_index("fib"), 2)
    rank_at = lax.broadcasted_iota(jnp.int32, (elements, slots), 0)
    slot_at = lax.broadcasted_iota(jnp.int32, (elements, slots), 1)
    row = lax.broadcasted_iota(jnp.int32, (elements, elements), 0)
    for core, order in enumerate((order_ref, order_own_ref)):
        from_slot = jnp.zeros((elements, slots), jnp.bool_)
        start = 0
        for distance in range(slots // rows - 1, -1, -1):
            count = table_ref[distance, 0, 2 * chip + core]
            inside = (rank_at >= start) & (rank_at < start + count)
            from_slot = from_slot | (inside & (slot_at - distance * rows == rank_at - start))
            start = start + count
        place = order[...]
        tile = lax.div(place, jnp.full_like(place, per_tile))
        place = place - tile * per_tile + (tile ^ (2 * chip)) * per_tile
        place = jnp.broadcast_to(place, (elements, elements))
        to_place = jnp.where(place == row, 1.0, 0.0).astype(BF16)
        out_ref[core * elements : (core + 1) * elements, :] = jnp.dot(
            to_place, jnp.where(from_slot, 1.0, 0.0).astype(BF16), preferred_element_type=F32
        )


def order_kernel(pick_ref, own_ref, near_ref, far_ref, last_ref, *outs):
    rows = last_ref.shape[0]
    elements = outs[0].shape[0]
    sources = (
        (near_ref[:rows, :], far_ref[:rows, :], last_ref[...]),
        (own_ref[:rows, :], near_ref[rows:, :], far_ref[rows:, :]),
    )
    for core, pieces in enumerate(sources):
        pick = pick_ref[core * elements : (core + 1) * elements, :].astype(BF16)
        line = jnp.concatenate(pieces, axis=0)
        high = line.astype(BF16)
        rest = line - high.astype(F32)
        mid = rest.astype(BF16)
        low = (rest - mid.astype(F32)).astype(BF16)
        out = jnp.dot(pick, low, preferred_element_type=F32)
        out += jnp.dot(pick, mid, preferred_element_type=F32)
        outs[core][...] = out + jnp.dot(pick, high, preferred_element_type=F32)


def bit_place(order):
    index = 0
    for axis, mask in order:
        index = index * 2 + lax.rem(lax.div(lax.axis_index(axis), mask), 2)
    return index


def image_kernel(mid, *refs):
    field_ref, image_scr = refs[-2:]
    count = 2 ** len(mid)
    outs = refs[-2 - count : -2]
    *block_refs, start_ref = refs[: -2 - count]
    length, width = field_ref.shape
    tile = width // 2
    chip = lax.div(lax.axis_index("fib"), 2)
    each = length // (2 * len(block_refs))
    if len(block_refs) == 1:
        field_ref[...] = block_refs[0][...]
        block_refs = []
    for step, block in enumerate(block_refs):
        for owner in range(2):
            at = pl.multiple_of((2 * (chip ^ step) + owner) * each, each)
            for core in range(2):
                part = (2 * owner + core) * each
                field_ref[pl.ds(at, each), core * tile : (core + 1) * tile] = block[part : part + each, :]
    field = halves(field_ref[...])
    mixed = dot3(field, halves(start_ref[...]), ((0,), (0,)))
    image_scr[...] = dot3(field, halves(mixed), ((1,), (0,)))
    place = bit_place(mid)
    for step, out in enumerate(outs):
        rows = out.shape[0]
        at = pl.multiple_of((place ^ step) * rows, rows)
        out[...] = image_scr[pl.ds(at, rows), :]


def factor_kernel(mid, field_ref, *refs):
    chunk_refs, out_refs, image_scr, work, line_scr = refs[:-5], refs[-5:-3], refs[-3], refs[-2], refs[-1]
    rank = image_scr.shape[1]
    place = bit_place(mid)
    for step, chunk in enumerate(chunk_refs):
        rows = chunk.shape[0]
        at = pl.multiple_of((place ^ step) * rows, rows)
        image_scr[pl.ds(at, rows), :] = chunk[...]
    image = halves(image_scr[...])
    work[:, :rank] = dot3(image, image, ((0,), (0,)))
    work[:, rank:] = dot3(image, halves(field_ref[...]), ((0,), (0,)))
    shape = (1, rank)
    for base in range(0, rank, SLAB):
        left = [work[base + k : base + k + 1, :rank] for k in range(SLAB)]
        right = [work[base + k : base + k + 1, rank:] for k in range(SLAB)]
        entry = [
            [jnp.broadcast_to(left[k][:, base + i : base + i + 1], shape) for i in range(SLAB)]
            for k in range(SLAB)
        ]
        for k in range(SLAB):
            scale = lax.rsqrt(entry[k][k])
            left[k] = left[k] * scale
            right[k] = right[k] * jnp.concatenate([scale] * 2, axis=1)
            factor = {i: entry[k][i] * scale for i in range(k + 1, SLAB)}
            for i in range(k + 1, SLAB):
                for j in range(i, SLAB):
                    entry[i][j] = entry[i][j] - factor[i] * factor[j]
                left[i] = left[i] - factor[i] * left[k]
                right[i] = right[i] - jnp.concatenate([factor[i]] * 2, axis=1) * right[k]
            out_refs[0][base + k : base + k + 1, :] = right[k][:, :rank]
            out_refs[1][base + k : base + k + 1, :] = right[k][:, rank:]
            line_scr[k : k + 1, :rank] = left[k]
            line_scr[k : k + 1, rank:] = right[k]
        after = base + SLAB
        if after < rank:
            line = line_scr[...]
            high = line.astype(BF16).astype(F32)
            rest = line - high
            mid = rest.astype(BF16).astype(F32)
            low = rest - mid
            first = jnp.concatenate([high, high, mid, high, low, mid], axis=0).astype(BF16)
            second = jnp.concatenate([high, mid, high, low, high, mid], axis=0).astype(BF16)
            drop = lax.dot_general(
                first[:, :rank], second, (((0,), (0,)), ((), ())), preferred_element_type=F32
            )
            work[after:, :] = work[after:, :] - drop[after:, :]


def swapped(value, bits, step=1):
    apart = [bit for at, bit in enumerate(reversed(bits)) if step >> at & 1]
    peers = {axis: sum(mask for name, mask in apart if name == axis) for axis in ("fib", "pln")}
    owners, planes = lax.axis_size("fib"), lax.axis_size("pln")
    pairs = []
    for i in range(owners * planes):
        fib, pln = divmod(i, planes)
        if fib % 2:
            pairs.append((i, (fib ^ peers["fib"]) * planes + (pln ^ peers["pln"])))
    return lax.ppermute(value, ("fib", "pln"), pairs)


def masks(axis, low, high):
    out = []
    while low < high:
        out.append((axis, low))
        low *= 2
    return out


def per_device(nodal_values, interp_matrix, count_table, slot_order, start_basis):
    nodes = nodal_values[0, 0]
    table = jnp.transpose(count_table, (2, 0, 1))
    owners = lax.axis_size("fib")
    planes = lax.axis_size("pln")
    window = table.shape[0]
    capacity = nodes.shape[0] // window
    points = interp_matrix.shape[1]
    elements = slot_order.shape[2]
    length, rank = start_basis.shape
    tile = points * elements // length
    odd = range(1, owners, 2)

    order_first = lax.ppermute(slot_order[0], "fib", [(i - 1, i) for i in odd])
    near, far, last = pl.pallas_call(
        functools.partial(interp_kernel, owners),
        out_shape=[jax.ShapeDtypeStruct((n * capacity, points), F32) for n in (2, 2, 1)],
        in_specs=[SMEM, VMEM, VMEM],
        out_specs=[VMEM] * 3,
        scratch_shapes=[pltpu.VMEM((nodes.shape[0] + SLAB, points), F32)],
        compiler_params=BIG,
        name="interp",
    )(table, nodes, interp_matrix)
    far_got = lax.ppermute(far, "fib", [(i, (i + 2) % owners) for i in odd])
    last_got = lax.ppermute(last, "fib", [(i - 1, (i + 2) % owners) for i in odd])
    near_got = lax.ppermute(near, "fib", [(i - 1, i) for i in odd])
    pick = pl.pallas_call(
        functools.partial(pick_kernel, capacity, elements // owners),
        out_shape=jax.ShapeDtypeStruct((2 * elements, capacity * window), F32),
        in_specs=[SMEM, VMEM, VMEM],
        out_specs=VMEM,
        compiler_params=BIG,
        name="pick",
    )(table, order_first, slot_order[0])
    bricks = pl.pallas_call(
        order_kernel,
        out_shape=[jax.ShapeDtypeStruct((elements, points), F32)] * 2,
        in_specs=[VMEM] * 5,
        out_specs=[VMEM] * 2,
        compiler_params=BIG,
        name="order",
    )(pick, near, near_got, far_got, last_got)

    blocks = owners // 2
    chips = masks("fib", 2, owners)[::-1]
    both = jnp.concatenate([b.reshape(blocks, 2 * length // owners, tile) for b in bricks], axis=1)
    got = {step: swapped(both[step], chips, step) for step in range(blocks - 1, 0, -1)}
    got[0] = both[0]
    parts = [got[step] for step in range(blocks)]
    if length // owners % SLAB:
        at = lax.axis_index("fib") // 2 ^ jnp.arange(blocks)
        whole = jnp.stack(parts)[at].reshape(blocks, 2, 2, length // owners, tile)
        parts = [whole.transpose(0, 1, 3, 2, 4).reshape(length, 2 * tile)]

    mid = masks("fib", 2, 4) + masks("pln", 1, planes)
    distant = masks("fib", 4, owners)
    count = 2 ** len(mid)
    chunk = jax.ShapeDtypeStruct((length // count, rank), F32)
    *chunks, field = pl.pallas_call(
        functools.partial(image_kernel, mid),
        out_shape=[chunk] * count + [jax.ShapeDtypeStruct((length, 2 * tile), F32)],
        in_specs=[VMEM] * (len(parts) + 1),
        out_specs=[VMEM] * (count + 1),
        scratch_shapes=[pltpu.VMEM((length, rank), F32)],
        compiler_params=BIG,
        name="image",
    )(*parts, start_basis)
    total = chunks[0]
    for arrived in [swapped(chunks[step], mid, step) for step in range(count - 1, 0, -1)]:
        total = total + arrived
    share = total
    for arrived in [swapped(share, distant, step) for step in range(2 ** len(distant) - 1, 0, -1)]:
        total = total + arrived
    chunks = [total] + [swapped(total, mid, step) for step in range(1, count)]
    first, second = pl.pallas_call(
        functools.partial(factor_kernel, mid),
        out_shape=[jax.ShapeDtypeStruct((rank, tile), F32)] * 2,
        in_specs=[VMEM] * (1 + count),
        out_specs=[VMEM] * 2,
        scratch_shapes=[
            pltpu.VMEM((length, rank), F32),
            pltpu.VMEM((rank, rank + 2 * tile), F32),
            pltpu.VMEM((SLAB, rank + 2 * tile), F32),
        ],
        compiler_params=BIG,
        name="factor",
    )(field, *chunks)
    first_got = lax.ppermute(first, "fib", [(i, i - 1) for i in odd])
    core_values = jnp.where(lax.axis_index("fib") % 2 == 1, second, first_got)
    return core_values[None, None]


def solution(mesh):
    placed = (P("pln", "fib", None, None), P(), P("pln", None, None), P("pln", "fib", None), P())
    return jax.shard_map(
        per_device,
        mesh=mesh,
        in_specs=placed,
        out_specs=P("pln", "fib", None, None),
        check_vma=False,
    )
```

```python
import functools

import jax
import jax.numpy as jnp
from jax import lax
from jax.experimental import pallas as pl
from jax.experimental.pallas import tpu as pltpu
from jax.sharding import PartitionSpec as P

F32 = jnp.float32
BF16 = jnp.bfloat16
SLAB = 8
VMEM = pl.BlockSpec(memory_space=pltpu.VMEM)
SMEM = pl.BlockSpec(memory_space=pltpu.SMEM)
BIG = pltpu.CompilerParams(vmem_limit_bytes=32 * 1024 * 1024)


def halves(value):
    high = value.astype(BF16)
    return high, (value - high.astype(F32)).astype(BF16)


def dot3(left, right, contract):
    dims = (contract, ((), ()))
    lh, ll = left
    rh, rl = right
    out = lax.dot_general(lh, rl, dims, preferred_element_type=F32)
    out += lax.dot_general(ll, rh, dims, preferred_element_type=F32)
    return out + lax.dot_general(lh, rh, dims, preferred_element_type=F32)


def interp_kernel(owners, table_ref, node_ref, interp_ref, near_ref, far_ref, last_ref, grid_scr):
    rows = last_ref.shape[0]
    slots = node_ref.shape[0]
    own = lax.axis_index("fib")
    grid_scr[:slots, :] = dot3(halves(node_ref[...]), halves(interp_ref[...]), ((1,), (0,)))
    near_ref[:rows, :] = grid_scr[:rows, :]
    start = table_ref[0, 0, own]
    for distance in range(1, 3):
        shift = lax.rem(start, SLAB)
        at = pl.multiple_of(start - shift, SLAB)
        wide = grid_scr[pl.ds(at, rows + SLAB), :]
        piece = pltpu.roll(wide, lax.rem(rows + SLAB - shift, rows + SLAB), 0)[:rows, :]
        if distance == 1:
            near_ref[rows:, :] = piece
            far_ref[:rows, :] = piece
        else:
            far_ref[rows:, :] = piece
            last_ref[...] = piece
        start = start + table_ref[distance, 0, lax.rem(own + distance, owners)]


def pick_kernel(rows, per_tile, table_ref, order_ref, order_own_ref, out_ref):
    elements = order_ref.shape[1]
    slots = out_ref.shape[1]
    chip = lax.div(lax.axis_index("fib"), 2)
    rank_at = lax.broadcasted_iota(jnp.int32, (elements, slots), 0)
    slot_at = lax.broadcasted_iota(jnp.int32, (elements, slots), 1)
    row = lax.broadcasted_iota(jnp.int32, (elements, elements), 0)
    for core, order in enumerate((order_ref, order_own_ref)):
        from_slot = jnp.zeros((elements, slots), jnp.bool_)
        start = 0
        for distance in range(slots // rows - 1, -1, -1):
            count = table_ref[distance, 0, 2 * chip + core]
            inside = (rank_at >= start) & (rank_at < start + count)
            from_slot = from_slot | (inside & (slot_at - distance * rows == rank_at - start))
            start = start + count
        place = order[...]
        tile = lax.div(place, jnp.full_like(place, per_tile))
        place = place - tile * per_tile + (tile ^ (2 * chip)) * per_tile
        place = jnp.broadcast_to(place, (elements, elements))
        to_place = jnp.where(place == row, 1.0, 0.0).astype(BF16)
        out_ref[core * elements : (core + 1) * elements, :] = jnp.dot(
            to_place, jnp.where(from_slot, 1.0, 0.0).astype(BF16), preferred_element_type=F32
        )


def order_kernel(pick_ref, own_ref, near_ref, far_ref, last_ref, *outs):
    rows = last_ref.shape[0]
    elements = outs[0].shape[0]
    sources = (
        (near_ref[:rows, :], far_ref[:rows, :], last_ref[...]),
        (own_ref[:rows, :], near_ref[rows:, :], far_ref[rows:, :]),
    )
    for core, pieces in enumerate(sources):
        pick = pick_ref[core * elements : (core + 1) * elements, :].astype(BF16)
        line = jnp.concatenate(pieces, axis=0)
        high = line.astype(BF16)
        rest = line - high.astype(F32)
        mid = rest.astype(BF16)
        low = (rest - mid.astype(F32)).astype(BF16)
        out = jnp.dot(pick, low, preferred_element_type=F32)
        out += jnp.dot(pick, mid, preferred_element_type=F32)
        outs[core][...] = out + jnp.dot(pick, high, preferred_element_type=F32)


def bit_place(order):
    index = 0
    for axis, mask in order:
        index = index * 2 + lax.rem(lax.div(lax.axis_index(axis), mask), 2)
    return index


def image_kernel(mid, *refs):
    field_ref, image_scr = refs[-2:]
    count = 2 ** len(mid)
    outs = refs[-2 - count : -2]
    *block_refs, start_ref = refs[: -2 - count]
    length, width = field_ref.shape
    tile = width // 2
    chip = lax.div(lax.axis_index("fib"), 2)
    each = length // (2 * len(block_refs))
    if len(block_refs) == 1:
        field_ref[...] = block_refs[0][...]
        block_refs = []
    for step, block in enumerate(block_refs):
        for owner in range(2):
            at = pl.multiple_of((2 * (chip ^ step) + owner) * each, each)
            for core in range(2):
                part = (2 * owner + core) * each
                field_ref[pl.ds(at, each), core * tile : (core + 1) * tile] = block[part : part + each, :]
    field = halves(field_ref[...])
    mixed = dot3(field, halves(start_ref[...]), ((0,), (0,)))
    image_scr[...] = dot3(field, halves(mixed), ((1,), (0,)))
    place = bit_place(mid)
    for step, out in enumerate(outs):
        rows = out.shape[0]
        at = pl.multiple_of((place ^ step) * rows, rows)
        out[...] = image_scr[pl.ds(at, rows), :]


def factor_kernel(mid, field_ref, *refs):
    chunk_refs, out_refs, image_scr, work, line_scr = refs[:-5], refs[-5:-3], refs[-3], refs[-2], refs[-1]
    rank = image_scr.shape[1]
    place = bit_place(mid)
    for step, chunk in enumerate(chunk_refs):
        rows = chunk.shape[0]
        at = pl.multiple_of((place ^ step) * rows, rows)
        image_scr[pl.ds(at, rows), :] = chunk[...]
    image = halves(image_scr[...])
    work[:, :rank] = dot3(image, image, ((0,), (0,)))
    work[:, rank:] = dot3(image, halves(field_ref[...]), ((0,), (0,)))
    shape = (1, rank)
    for base in range(0, rank, SLAB):
        left = [work[base + k : base + k + 1, :rank] for k in range(SLAB)]
        right = [work[base + k : base + k + 1, rank:] for k in range(SLAB)]
        entry = [
            [jnp.broadcast_to(left[k][:, base + i : base + i + 1], shape) for i in range(SLAB)]
            for k in range(SLAB)
        ]
        for k in range(SLAB):
            scale = lax.rsqrt(entry[k][k])
            left[k] = left[k] * scale
            right[k] = right[k] * jnp.concatenate([scale] * 2, axis=1)
            factor = {i: entry[k][i] * scale for i in range(k + 1, SLAB)}
            for i in range(k + 1, SLAB):
                for j in range(i, SLAB):
                    entry[i][j] = entry[i][j] - factor[i] * factor[j]
                left[i] = left[i] - factor[i] * left[k]
                right[i] = right[i] - jnp.concatenate([factor[i]] * 2, axis=1) * right[k]
            out_refs[0][base + k : base + k + 1, :] = right[k][:, :rank]
            out_refs[1][base + k : base + k + 1, :] = right[k][:, rank:]
            line_scr[k : k + 1, :rank] = left[k]
            line_scr[k : k + 1, rank:] = right[k]
        after = base + SLAB
        if after < rank:
            line = line_scr[...]
            high = line.astype(BF16).astype(F32)
            rest = line - high
            mid = rest.astype(BF16).astype(F32)
            low = rest - mid
            first = jnp.concatenate([high, high, mid, high, low, mid], axis=0).astype(BF16)
            second = jnp.concatenate([high, mid, high, low, high, mid], axis=0).astype(BF16)
            drop = lax.dot_general(
                first[:, :rank], second, (((0,), (0,)), ((), ())), preferred_element_type=F32
            )
            work[after:, :] = work[after:, :] - drop[after:, :]


def choose_kernel(own_ref, got_ref, out_ref):
    second = lax.rem(lax.axis_index("fib"), 2) == 1

    @pl.when(second)
    def _():
        out_ref[...] = own_ref[...]

    @pl.when(jnp.logical_not(second))
    def _():
        out_ref[...] = got_ref[...]


def swapped(value, bits, step=1):
    apart = [bit for at, bit in enumerate(reversed(bits)) if step >> at & 1]
    peers = {axis: sum(mask for name, mask in apart if name == axis) for axis in ("fib", "pln")}
    owners, planes = lax.axis_size("fib"), lax.axis_size("pln")
    pairs = []
    for i in range(owners * planes):
        fib, pln = divmod(i, planes)
        to = (fib ^ peers["fib"]) * planes + (pln ^ peers["pln"])
        pairs.append((i, to if fib % 2 else i))
    return lax.ppermute(value, ("fib", "pln"), pairs)


def masks(axis, low, high):
    out = []
    while low < high:
        out.append((axis, low))
        low *= 2
    return out


def per_device(nodal_values, interp_matrix, count_table, slot_order, start_basis):
    nodes = nodal_values[0, 0]
    table = jnp.transpose(count_table, (2, 0, 1))
    owners = lax.axis_size("fib")
    planes = lax.axis_size("pln")
    window = table.shape[0]
    capacity = nodes.shape[0] // window
    points = interp_matrix.shape[1]
    elements = slot_order.shape[2]
    length, rank = start_basis.shape
    tile = points * elements // length
    core_swap = [(i, i ^ 1) for i in range(owners)]

    order_first = lax.ppermute(slot_order[0], "fib", core_swap)
    near, far, last = pl.pallas_call(
        functools.partial(interp_kernel, owners),
        out_shape=[jax.ShapeDtypeStruct((n * capacity, points), F32) for n in (2, 2, 1)],
        in_specs=[SMEM, VMEM, VMEM],
        out_specs=[VMEM] * 3,
        scratch_shapes=[pltpu.VMEM((nodes.shape[0] + SLAB, points), F32)],
        compiler_params=BIG,
        name="interp",
    )(table, nodes, interp_matrix)
    far_got = lax.ppermute(far, "fib", [(i, (i + 2) % owners if i % 2 else i) for i in range(owners)])
    onward = [(i, i - 1 if i % 2 else (i + 3) % owners) for i in range(owners)]
    last_got = lax.ppermute(last, "fib", onward)
    near_got = lax.ppermute(near, "fib", core_swap)
    pick = pl.pallas_call(
        functools.partial(pick_kernel, capacity, elements // owners),
        out_shape=jax.ShapeDtypeStruct((2 * elements, capacity * window), F32),
        in_specs=[SMEM, VMEM, VMEM],
        out_specs=VMEM,
        compiler_params=BIG,
        name="pick",
    )(table, order_first, slot_order[0])
    bricks = pl.pallas_call(
        order_kernel,
        out_shape=[jax.ShapeDtypeStruct((elements, points), F32)] * 2,
        in_specs=[VMEM] * 5,
        out_specs=[VMEM] * 2,
        compiler_params=BIG,
        name="order",
    )(pick, near, near_got, far_got, last_got)

    blocks = owners // 2
    chips = masks("fib", 2, owners)[::-1]
    both = jnp.concatenate([b.reshape(blocks, 2 * length // owners, tile) for b in bricks], axis=1)
    got = {step: swapped(both[step], chips, step) for step in range(blocks - 1, 0, -1)}
    got[0] = both[0]
    parts = [got[step] for step in range(blocks)]
    if length // owners % SLAB:
        at = lax.axis_index("fib") // 2 ^ jnp.arange(blocks)
        whole = jnp.stack(parts)[at].reshape(blocks, 2, 2, length // owners, tile)
        parts = [whole.transpose(0, 1, 3, 2, 4).reshape(length, 2 * tile)]

    mid = masks("fib", 2, 4) + masks("pln", 1, planes)
    distant = masks("fib", 4, owners)
    count = 2 ** len(mid)
    chunk = jax.ShapeDtypeStruct((length // count, rank), F32)
    *chunks, field = pl.pallas_call(
        functools.partial(image_kernel, mid),
        out_shape=[chunk] * count + [jax.ShapeDtypeStruct((length, 2 * tile), F32)],
        in_specs=[VMEM] * (len(parts) + 1),
        out_specs=[VMEM] * (count + 1),
        scratch_shapes=[pltpu.VMEM((length, rank), F32)],
        compiler_params=BIG,
        name="image",
    )(*parts, start_basis)
    total = chunks[0]
    for arrived in [swapped(chunks[step], mid, step) for step in range(count - 1, 0, -1)]:
        total = total + arrived
    share = total
    for arrived in [swapped(share, distant, step) for step in range(2 ** len(distant) - 1, 0, -1)]:
        total = total + arrived
    chunks = [total] + [swapped(total, mid, step) for step in range(1, count)]
    first, second = pl.pallas_call(
        functools.partial(factor_kernel, mid),
        out_shape=[jax.ShapeDtypeStruct((rank, tile), F32)] * 2,
        in_specs=[VMEM] * (1 + count),
        out_specs=[VMEM] * 2,
        scratch_shapes=[
            pltpu.VMEM((length, rank), F32),
            pltpu.VMEM((rank, rank + 2 * tile), F32),
            pltpu.VMEM((SLAB, rank + 2 * tile), F32),
        ],
        compiler_params=BIG,
        name="factor",
    )(field, *chunks)
    core_values = pl.pallas_call(
        choose_kernel,
        out_shape=jax.ShapeDtypeStruct((rank, tile), F32),
        in_specs=[VMEM] * 2,
        out_specs=VMEM,
        name="choose",
    )(second, lax.ppermute(first, "fib", core_swap))
    return core_values[None, None]


def solution(mesh):
    placed = (P("pln", "fib", None, None), P(), P("pln", None, None), P("pln", "fib", None), P())
    return jax.shard_map(
        per_device,
        mesh=mesh,
        in_specs=placed,
        out_specs=P("pln", "fib", None, None),
        check_vma=False,
    )
```

```python
import functools

import jax
import jax.numpy as jnp
from jax import lax
from jax.experimental import pallas as pl
from jax.experimental.pallas import tpu as pltpu
from jax.sharding import PartitionSpec as P

F32 = jnp.float32
BF16 = jnp.bfloat16
SLAB = 8
VMEM = pl.BlockSpec(memory_space=pltpu.VMEM)
SMEM = pl.BlockSpec(memory_space=pltpu.SMEM)
BIG = pltpu.CompilerParams(vmem_limit_bytes=32 * 1024 * 1024)


def halves(value):
    high = value.astype(BF16)
    return high, (value - high.astype(F32)).astype(BF16)


def dot3(left, right, contract):
    dims = (contract, ((), ()))
    lh, ll = left
    rh, rl = right
    out = lax.dot_general(lh, rl, dims, preferred_element_type=F32)
    out += lax.dot_general(ll, rh, dims, preferred_element_type=F32)
    return out + lax.dot_general(lh, rh, dims, preferred_element_type=F32)


def interp_kernel(owners, table_ref, node_ref, interp_ref, zero_ref, one_ref, send_ref, grid_scr):
    rows = zero_ref.shape[0]
    slots = node_ref.shape[0]
    own = lax.axis_index("fib")
    grid_scr[:slots, :] = dot3(halves(node_ref[...]), halves(interp_ref[...]), ((1,), (0,)))
    zero_ref[...] = grid_scr[:rows, :]
    start = table_ref[0, 0, own]
    for distance in range(1, 3):
        shift = lax.rem(start, SLAB)
        at = pl.multiple_of(start - shift, SLAB)
        wide = grid_scr[pl.ds(at, rows + SLAB), :]
        piece = pltpu.roll(wide, lax.rem(rows + SLAB - shift, rows + SLAB), 0)[:rows, :]
        if distance == 1:
            one_ref[...] = piece
            send_ref[:rows, :] = piece
        else:
            send_ref[rows:, :] = piece
        start = start + table_ref[distance, 0, lax.rem(own + distance, owners)]

    @pl.when(lax.rem(own, 2) == 0)
    def _():
        send_ref[:rows, :] = send_ref[rows:, :]


def pick_kernel(rows, per_tile, table_ref, order_ref, order_next_ref, out_ref):
    elements = order_ref.shape[1]
    slots = out_ref.shape[1]
    chip = lax.div(lax.axis_index("fib"), 2)
    rank_at = lax.broadcasted_iota(jnp.int32, (elements, slots), 0)
    slot_at = lax.broadcasted_iota(jnp.int32, (elements, slots), 1)
    row = lax.broadcasted_iota(jnp.int32, (elements, elements), 0)
    for core, order in enumerate((order_ref, order_next_ref)):
        from_slot = jnp.zeros((elements, slots), jnp.bool_)
        start = 0
        for distance in range(slots // rows - 1, -1, -1):
            count = table_ref[distance, 0, 2 * chip + core]
            inside = (rank_at >= start) & (rank_at < start + count)
            from_slot = from_slot | (inside & (slot_at - distance * rows == rank_at - start))
            start = start + count
        place = order[...]
        tile = lax.div(place, jnp.full_like(place, per_tile))
        place = place - tile * per_tile + (tile ^ (2 * chip)) * per_tile
        place = jnp.broadcast_to(place, (elements, elements))
        to_place = jnp.where(place == row, 1.0, 0.0).astype(BF16)
        out_ref[core * elements : (core + 1) * elements, :] = jnp.dot(
            to_place, jnp.where(from_slot, 1.0, 0.0).astype(BF16), preferred_element_type=F32
        )


def order_kernel(pick_ref, zero_ref, one_ref, next_zero_ref, back_ref, back_two_ref, *outs):
    rows = zero_ref.shape[0]
    elements = outs[0].shape[0]
    sources = (
        (zero_ref[...], back_ref[:rows, :], back_two_ref[...]),
        (next_zero_ref[...], one_ref[...], back_ref[rows:, :]),
    )
    for core, pieces in enumerate(sources):
        pick = pick_ref[core * elements : (core + 1) * elements, :].astype(BF16)
        line = jnp.concatenate(pieces, axis=0)
        high = line.astype(BF16)
        rest = line - high.astype(F32)
        mid = rest.astype(BF16)
        low = (rest - mid.astype(F32)).astype(BF16)
        out = jnp.dot(pick, low, preferred_element_type=F32)
        out += jnp.dot(pick, mid, preferred_element_type=F32)
        outs[core][...] = out + jnp.dot(pick, high, preferred_element_type=F32)


def bit_place(order):
    index = 0
    for axis, mask in order:
        index = index * 2 + lax.rem(lax.div(lax.axis_index(axis), mask), 2)
    return index


def image_kernel(mid, *refs):
    field_ref, image_scr = refs[-2:]
    count = 2 ** len(mid)
    outs = refs[-2 - count : -2]
    *block_refs, start_ref = refs[: -2 - count]
    length, width = field_ref.shape
    tile = width // 2
    chip = lax.div(lax.axis_index("fib"), 2)
    each = length // (2 * len(block_refs))
    if len(block_refs) == 1:
        field_ref[...] = block_refs[0][...]
        block_refs = []
    for step, block in enumerate(block_refs):
        for owner in range(2):
            at = pl.multiple_of((2 * (chip ^ step) + owner) * each, each)
            for core in range(2):
                part = (2 * owner + core) * each
                field_ref[pl.ds(at, each), core * tile : (core + 1) * tile] = block[part : part + each, :]
    field = halves(field_ref[...])
    mixed = dot3(field, halves(start_ref[...]), ((0,), (0,)))
    image_scr[...] = dot3(field, halves(mixed), ((1,), (0,)))
    place = bit_place(mid)
    for step, out in enumerate(outs):
        rows = out.shape[0]
        at = pl.multiple_of((place ^ step) * rows, rows)
        out[...] = image_scr[pl.ds(at, rows), :]


def factor_kernel(mid, field_ref, *refs):
    chunk_refs, out_refs, image_scr, work, line_scr = refs[:-5], refs[-5:-3], refs[-3], refs[-2], refs[-1]
    rank = image_scr.shape[1]
    place = bit_place(mid)
    for step, chunk in enumerate(chunk_refs):
        rows = chunk.shape[0]
        at = pl.multiple_of((place ^ step) * rows, rows)
        image_scr[pl.ds(at, rows), :] = chunk[...]
    image = halves(image_scr[...])
    work[:, :rank] = dot3(image, image, ((0,), (0,)))
    work[:, rank:] = dot3(image, halves(field_ref[...]), ((0,), (0,)))
    shape = (1, rank)
    for base in range(0, rank, SLAB):
        left = [work[base + k : base + k + 1, :rank] for k in range(SLAB)]
        right = [work[base + k : base + k + 1, rank:] for k in range(SLAB)]
        entry = [
            [jnp.broadcast_to(left[k][:, base + i : base + i + 1], shape) for i in range(SLAB)]
            for k in range(SLAB)
        ]
        for k in range(SLAB):
            scale = lax.rsqrt(entry[k][k])
            left[k] = left[k] * scale
            right[k] = right[k] * jnp.concatenate([scale] * 2, axis=1)
            factor = {i: entry[k][i] * scale for i in range(k + 1, SLAB)}
            for i in range(k + 1, SLAB):
                for j in range(i, SLAB):
                    entry[i][j] = entry[i][j] - factor[i] * factor[j]
                left[i] = left[i] - factor[i] * left[k]
                right[i] = right[i] - jnp.concatenate([factor[i]] * 2, axis=1) * right[k]
            out_refs[0][base + k : base + k + 1, :] = right[k][:, :rank]
            out_refs[1][base + k : base + k + 1, :] = right[k][:, rank:]
            line_scr[k : k + 1, :rank] = left[k]
            line_scr[k : k + 1, rank:] = right[k]
        after = base + SLAB
        if after < rank:
            line = line_scr[...]
            high = line.astype(BF16).astype(F32)
            rest = line - high
            mid = rest.astype(BF16).astype(F32)
            low = rest - mid
            first = jnp.concatenate([high, high, mid, high, low, mid], axis=0).astype(BF16)
            second = jnp.concatenate([high, mid, high, low, high, mid], axis=0).astype(BF16)
            drop = lax.dot_general(
                first[:, :rank], second, (((0,), (0,)), ((), ())), preferred_element_type=F32
            )
            work[after:, :] = work[after:, :] - drop[after:, :]

    @pl.when(lax.rem(lax.axis_index("fib"), 2) == 1)
    def _():
        for out in out_refs:
            out[...] = jnp.zeros_like(out)


def crossed(value, bits, step, to_core):
    apart = [bit for at, bit in enumerate(reversed(bits)) if step >> at & 1]
    peers = {axis: sum(mask for name, mask in apart if name == axis) for axis in ("fib", "pln")}
    owners, planes = lax.axis_size("fib"), lax.axis_size("pln")
    pairs = []
    for i in range(owners * planes):
        fib, pln = divmod(i, planes)
        if fib % 2 != to_core:
            fib, pln = fib ^ peers["fib"], pln ^ peers["pln"]
        pairs.append((i, (fib ^ 1) * planes + pln))
    return lax.ppermute(value, ("fib", "pln"), pairs)


def masks(axis, low, high):
    out = []
    while low < high:
        out.append((axis, low))
        low *= 2
    return out


def per_device(nodal_values, interp_matrix, count_table, slot_order, start_basis):
    nodes = nodal_values[0, 0]
    table = jnp.transpose(count_table, (2, 0, 1))
    owners = lax.axis_size("fib")
    planes = lax.axis_size("pln")
    window = table.shape[0]
    capacity = nodes.shape[0] // window
    points = interp_matrix.shape[1]
    elements = slot_order.shape[2]
    length, rank = start_basis.shape
    tile = points * elements // length
    core_swap = [(i, i ^ 1) for i in range(owners)]
    forward = [(i, (i + 1) % owners) for i in range(owners)]

    order_next = lax.ppermute(slot_order[0], "fib", core_swap)
    zero, one, send = pl.pallas_call(
        functools.partial(interp_kernel, owners),
        out_shape=[jax.ShapeDtypeStruct((n * capacity, points), F32) for n in (1, 1, 2)],
        in_specs=[SMEM, VMEM, VMEM],
        out_specs=[VMEM] * 3,
        scratch_shapes=[pltpu.VMEM((nodes.shape[0] + SLAB, points), F32)],
        compiler_params=BIG,
        name="interp",
    )(table, nodes, interp_matrix)
    back = lax.ppermute(send, "fib", forward)
    next_zero = lax.ppermute(zero, "fib", core_swap)
    back_two = lax.ppermute(back[:capacity], "fib", forward)
    pick = pl.pallas_call(
        functools.partial(pick_kernel, capacity, elements // owners),
        out_shape=jax.ShapeDtypeStruct((2 * elements, capacity * window), F32),
        in_specs=[SMEM, VMEM, VMEM],
        out_specs=VMEM,
        compiler_params=BIG,
        name="pick",
    )(table, slot_order[0], order_next)
    bricks = pl.pallas_call(
        order_kernel,
        out_shape=[jax.ShapeDtypeStruct((elements, points), F32)] * 2,
        in_specs=[VMEM] * 6,
        out_specs=[VMEM] * 2,
        compiler_params=BIG,
        name="order",
    )(pick, zero, one, next_zero, back, back_two)

    blocks = owners // 2
    chips = masks("fib", 2, owners)[::-1]
    both = jnp.concatenate([b.reshape(blocks, 2 * length // owners, tile) for b in bricks], axis=1)
    got = {step: crossed(both[step], chips, step, 1) for step in range(blocks - 1, -1, -1)}
    parts = [got[step] for step in range(blocks)]
    if length // owners % SLAB:
        at = lax.axis_index("fib") // 2 ^ jnp.arange(blocks)
        whole = jnp.stack(parts)[at].reshape(blocks, 2, 2, length // owners, tile)
        parts = [whole.transpose(0, 1, 3, 2, 4).reshape(length, 2 * tile)]

    mid = masks("fib", 2, 4) + masks("pln", 1, planes)
    distant = masks("fib", 4, owners)
    count = 2 ** len(mid)
    chunk = jax.ShapeDtypeStruct((length // count, rank), F32)
    *chunks, field = pl.pallas_call(
        functools.partial(image_kernel, mid),
        out_shape=[chunk] * count + [jax.ShapeDtypeStruct((length, 2 * tile), F32)],
        in_specs=[VMEM] * (len(parts) + 1),
        out_specs=[VMEM] * (count + 1),
        scratch_shapes=[pltpu.VMEM((length, rank), F32)],
        compiler_params=BIG,
        name="image",
    )(*parts, start_basis)
    field = crossed(field, mid, 0, 0)
    total = sum(crossed(chunks[step], mid, step, 0) for step in range(count - 1, -1, -1))
    total = sum(crossed(total, distant, step, 1) for step in range(2 ** len(distant) - 1, -1, -1))
    chunks = [crossed(total, mid, step, 0) for step in range(count)]
    first, second = pl.pallas_call(
        functools.partial(factor_kernel, mid),
        out_shape=[jax.ShapeDtypeStruct((rank, tile), F32)] * 2,
        in_specs=[VMEM] * (1 + count),
        out_specs=[VMEM] * 2,
        scratch_shapes=[
            pltpu.VMEM((length, rank), F32),
            pltpu.VMEM((rank, rank + 2 * tile), F32),
            pltpu.VMEM((SLAB, rank + 2 * tile), F32),
        ],
        compiler_params=BIG,
        name="factor",
    )(field, *chunks)
    core_values = first + lax.ppermute(second, "fib", core_swap)
    return core_values[None, None]


def solution(mesh):
    placed = (P("pln", "fib", None, None), P(), P("pln", None, None), P("pln", "fib", None), P())
    return jax.shard_map(
        per_device,
        mesh=mesh,
        in_specs=placed,
        out_specs=P("pln", "fib", None, None),
        check_vma=False,
    )
```

```python
import functools

import jax
import jax.numpy as jnp
from jax import lax
from jax.experimental import pallas as pl
from jax.experimental.pallas import tpu as pltpu
from jax.sharding import PartitionSpec as P

F32 = jnp.float32
BF16 = jnp.bfloat16
SLAB = 8
KSTEP = 256
VMEM = pl.BlockSpec(memory_space=pltpu.VMEM)
SMEM = pl.BlockSpec(memory_space=pltpu.SMEM)
BIG = pltpu.CompilerParams(vmem_limit_bytes=32 * 1024 * 1024)


def halves(value):
    high = value.astype(BF16)
    return high, (value - high.astype(F32)).astype(BF16)


def dot3(left, right, contract):
    dims = (contract, ((), ()))
    lh, ll = left
    rh, rl = right
    out = lax.dot_general(lh, rl, dims, preferred_element_type=F32)
    out += lax.dot_general(ll, rh, dims, preferred_element_type=F32)
    return out + lax.dot_general(lh, rh, dims, preferred_element_type=F32)


def interp_kernel(owners, table_hbm, node_hbm, interp_hbm, swap_ref, one_ref, send_ref, zero_ref, *scratch):
    grid_scr, node_ref, interp_ref, table_ref, sems = scratch
    rows = zero_ref.shape[0]
    slots, depth = node_ref.shape
    own = lax.axis_index("fib")
    copies = [pltpu.make_async_copy(table_hbm, table_ref, sems.at[0])]
    for part in range(slots // rows):
        at = pl.ds(part * rows, rows)
        copies.append(pltpu.make_async_copy(node_hbm.at[at, :], node_ref.at[at, :], sems.at[len(copies)]))
    steps = [(at, min(KSTEP, depth - at)) for at in range(0, depth, KSTEP)]
    first = len(copies)
    for at, size in steps:
        part = pl.ds(at, size)
        copies.append(
            pltpu.make_async_copy(interp_hbm.at[part, :], interp_ref.at[part, :], sems.at[len(copies)])
        )
    for copy in copies:
        copy.start()
    for copy in copies[:first]:
        copy.wait()
    total = None
    for (at, size), copy in zip(steps, copies[first:]):
        copy.wait()
        part = dot3(
            halves(node_ref[:, at : at + size]), halves(interp_ref[at : at + size, :]), ((1,), (0,))
        )
        total = part if total is None else total + part
    grid_scr[:slots, :] = total
    zero_ref[...] = grid_scr[:rows, :]
    start = table_ref[0, 0, own]
    for distance in range(1, 3):
        shift = lax.rem(start, SLAB)
        at = pl.multiple_of(start - shift, SLAB)
        wide = grid_scr[pl.ds(at, rows + SLAB), :]
        piece = pltpu.roll(wide, lax.rem(rows + SLAB - shift, rows + SLAB), 0)[:rows, :]
        if distance == 1:
            one_ref[...] = piece
            send_ref[:rows, :] = piece
        else:
            send_ref[rows:, :] = piece
        start = start + table_ref[distance, 0, lax.rem(own + distance, owners)]
    second = lax.rem(own, 2) == 1

    @pl.when(second)
    def _():
        swap_ref[...] = zero_ref[...]

    @pl.when(jnp.logical_not(second))
    def _():
        swap_ref[...] = send_ref[rows:, :]


def pick_kernel(rows, per_tile, table_ref, order_ref, order_next_ref, out_ref):
    elements = order_ref.shape[1]
    slots = out_ref.shape[1]
    chip = lax.div(lax.axis_index("fib"), 2)
    rank_at = lax.broadcasted_iota(jnp.int32, (elements, slots), 0)
    slot_at = lax.broadcasted_iota(jnp.int32, (elements, slots), 1)
    row = lax.broadcasted_iota(jnp.int32, (elements, elements), 0)
    for core, order in enumerate((order_ref, order_next_ref)):
        from_slot = jnp.zeros((elements, slots), jnp.bool_)
        start = 0
        for distance in range(slots // rows - 1, -1, -1):
            count = table_ref[distance, 0, 2 * chip + core]
            inside = (rank_at >= start) & (rank_at < start + count)
            from_slot = from_slot | (inside & (slot_at - distance * rows == rank_at - start))
            start = start + count
        place = order[...]
        tile = lax.div(place, jnp.full_like(place, per_tile))
        place = place - tile * per_tile + (tile ^ (2 * chip)) * per_tile
        place = jnp.broadcast_to(place, (elements, elements))
        to_place = jnp.where(place == row, 1.0, 0.0).astype(BF16)
        out_ref[core * elements : (core + 1) * elements, :] = jnp.dot(
            to_place, jnp.where(from_slot, 1.0, 0.0).astype(BF16), preferred_element_type=F32
        )


def order_kernel(pick_ref, zero_ref, one_ref, next_zero_ref, back_ref, back_two_ref, *outs):
    rows = zero_ref.shape[0]
    elements = outs[0].shape[0]
    sources = (
        (zero_ref[...], back_ref[:rows, :], back_two_ref[...]),
        (next_zero_ref[...], one_ref[...], back_ref[rows:, :]),
    )
    for core, pieces in enumerate(sources):
        pick = pick_ref[core * elements : (core + 1) * elements, :].astype(BF16)
        line = jnp.concatenate(pieces, axis=0)
        high = line.astype(BF16)
        rest = line - high.astype(F32)
        mid = rest.astype(BF16)
        low = (rest - mid.astype(F32)).astype(BF16)
        out = jnp.dot(pick, low, preferred_element_type=F32)
        out += jnp.dot(pick, mid, preferred_element_type=F32)
        outs[core][...] = out + jnp.dot(pick, high, preferred_element_type=F32)


def bit_place(order):
    index = 0
    for axis, mask in order:
        index = index * 2 + lax.rem(lax.div(lax.axis_index(axis), mask), 2)
    return index


def image_kernel(mid, *refs):
    field_ref, image_scr = refs[-2:]
    count = 2 ** len(mid)
    outs = refs[-2 - count : -2]
    *block_refs, start_ref = refs[: -2 - count]
    length, width = field_ref.shape
    tile = width // 2
    chip = lax.div(lax.axis_index("fib"), 2)
    each = length // (2 * len(block_refs))
    if len(block_refs) == 1:
        field_ref[...] = block_refs[0][...]
        block_refs = []
    for step, block in enumerate(block_refs):
        for owner in range(2):
            at = pl.multiple_of((2 * (chip ^ step) + owner) * each, each)
            for core in range(2):
                part = (2 * owner + core) * each
                field_ref[pl.ds(at, each), core * tile : (core + 1) * tile] = block[part : part + each, :]
    field = halves(field_ref[...])
    mixed = dot3(field, halves(start_ref[...]), ((0,), (0,)))
    image_scr[...] = dot3(field, halves(mixed), ((1,), (0,)))
    place = bit_place(mid)
    for step, out in enumerate(outs):
        rows = out.shape[0]
        at = pl.multiple_of((place ^ step) * rows, rows)
        out[...] = image_scr[pl.ds(at, rows), :]


def factor_kernel(mid, field_ref, *refs):
    chunk_refs, out_refs, image_scr, work, line_scr = refs[:-5], refs[-5:-3], refs[-3], refs[-2], refs[-1]
    rank = image_scr.shape[1]
    place = bit_place(mid)
    for step, chunk in enumerate(chunk_refs):
        rows = chunk.shape[0]
        at = pl.multiple_of((place ^ step) * rows, rows)
        image_scr[pl.ds(at, rows), :] = chunk[...]
    image = halves(image_scr[...])
    work[:, :rank] = dot3(image, image, ((0,), (0,)))
    work[:, rank:] = dot3(image, halves(field_ref[...]), ((0,), (0,)))
    shape = (1, rank)
    for base in range(0, rank, SLAB):
        left = [work[base + k : base + k + 1, :rank] for k in range(SLAB)]
        right = [work[base + k : base + k + 1, rank:] for k in range(SLAB)]
        entry = [
            [jnp.broadcast_to(left[k][:, base + i : base + i + 1], shape) for i in range(SLAB)]
            for k in range(SLAB)
        ]
        for k in range(SLAB):
            scale = lax.rsqrt(entry[k][k])
            left[k] = left[k] * scale
            right[k] = right[k] * jnp.concatenate([scale] * 2, axis=1)
            factor = {i: entry[k][i] * scale for i in range(k + 1, SLAB)}
            for i in range(k + 1, SLAB):
                for j in range(i, SLAB):
                    entry[i][j] = entry[i][j] - factor[i] * factor[j]
                left[i] = left[i] - factor[i] * left[k]
                right[i] = right[i] - jnp.concatenate([factor[i]] * 2, axis=1) * right[k]
            out_refs[0][base + k : base + k + 1, :] = right[k][:, :rank]
            out_refs[1][base + k : base + k + 1, :] = right[k][:, rank:]
            line_scr[k : k + 1, :rank] = left[k]
            line_scr[k : k + 1, rank:] = right[k]
        after = base + SLAB
        if after < rank:
            line = line_scr[...]
            high = line.astype(BF16).astype(F32)
            rest = line - high
            mid = rest.astype(BF16).astype(F32)
            low = rest - mid
            first = jnp.concatenate([high, high, mid, high, low, mid], axis=0).astype(BF16)
            second = jnp.concatenate([high, mid, high, low, high, mid], axis=0).astype(BF16)
            drop = lax.dot_general(
                first[:, :rank], second, (((0,), (0,)), ((), ())), preferred_element_type=F32
            )
            work[after:, :] = work[after:, :] - drop[after:, :]

    @pl.when(lax.rem(lax.axis_index("fib"), 2) == 1)
    def _():
        for out in out_refs:
            out[...] = jnp.zeros_like(out)


def crossed(value, bits, step, to_core):
    apart = [bit for at, bit in enumerate(reversed(bits)) if step >> at & 1]
    peers = {axis: sum(mask for name, mask in apart if name == axis) for axis in ("fib", "pln")}
    owners, planes = lax.axis_size("fib"), lax.axis_size("pln")
    pairs = []
    for i in range(owners * planes):
        fib, pln = divmod(i, planes)
        if fib % 2 != to_core:
            fib, pln = fib ^ peers["fib"], pln ^ peers["pln"]
        pairs.append((i, (fib ^ 1) * planes + pln))
    return lax.ppermute(value, ("fib", "pln"), pairs)


def masks(axis, low, high):
    out = []
    while low < high:
        out.append((axis, low))
        low *= 2
    return out


def per_device(nodal_values, interp_matrix, count_table, slot_order, start_basis):
    nodes = nodal_values[0, 0]
    table = jnp.transpose(count_table, (2, 0, 1))
    owners = lax.axis_size("fib")
    planes = lax.axis_size("pln")
    window = table.shape[0]
    capacity = nodes.shape[0] // window
    points = interp_matrix.shape[1]
    elements = slot_order.shape[2]
    length, rank = start_basis.shape
    tile = points * elements // length
    core_swap = [(i, i ^ 1) for i in range(owners)]
    forward = [(i, (i + 1) % owners) for i in range(owners)]

    order_next = lax.ppermute(slot_order[0], "fib", core_swap)
    piece = jax.ShapeDtypeStruct((capacity, points), F32)
    copies = 1 + window + pl.cdiv(nodes.shape[1], KSTEP)
    swap, one, send, zero = pl.pallas_call(
        functools.partial(interp_kernel, owners),
        out_shape=[piece, piece, jax.ShapeDtypeStruct((2 * capacity, points), F32), piece],
        in_specs=[pl.BlockSpec(memory_space=pl.ANY)] * 3,
        out_specs=[VMEM] * 4,
        scratch_shapes=[
            pltpu.VMEM((nodes.shape[0] + SLAB, points), F32),
            pltpu.VMEM(nodes.shape, F32),
            pltpu.VMEM(interp_matrix.shape, F32),
            pltpu.SMEM(table.shape, jnp.int32),
            pltpu.SemaphoreType.DMA((copies,)),
        ],
        compiler_params=BIG,
        name="interp",
    )(*(pltpu.with_memory_space_constraint(x, pltpu.HBM) for x in (table, nodes, interp_matrix)))
    swapped = lax.ppermute(swap, "fib", core_swap)
    back = lax.ppermute(send, "fib", forward)
    back_two = lax.ppermute(swapped, "fib", forward)
    pick = pl.pallas_call(
        functools.partial(pick_kernel, capacity, elements // owners),
        out_shape=jax.ShapeDtypeStruct((2 * elements, capacity * window), F32),
        in_specs=[SMEM, VMEM, VMEM],
        out_specs=VMEM,
        compiler_params=BIG,
        name="pick",
    )(table, slot_order[0], order_next)
    bricks = pl.pallas_call(
        order_kernel,
        out_shape=[jax.ShapeDtypeStruct((elements, points), F32)] * 2,
        in_specs=[VMEM] * 6,
        out_specs=[VMEM] * 2,
        compiler_params=BIG,
        name="order",
    )(pick, zero, one, swapped, back, back_two)

    blocks = owners // 2
    chips = masks("fib", 2, owners)[::-1]
    both = jnp.concatenate([b.reshape(blocks, 2 * length // owners, tile) for b in bricks], axis=1)
    got = {step: crossed(both[step], chips, step, 1) for step in range(blocks - 1, -1, -1)}
    parts = [got[step] for step in range(blocks)]
    if length // owners % SLAB:
        at = lax.axis_index("fib") // 2 ^ jnp.arange(blocks)
        whole = jnp.stack(parts)[at].reshape(blocks, 2, 2, length // owners, tile)
        parts = [whole.transpose(0, 1, 3, 2, 4).reshape(length, 2 * tile)]

    mid = masks("fib", 2, 4) + masks("pln", 1, planes)
    distant = masks("fib", 4, owners)
    count = 2 ** len(mid)
    chunk = jax.ShapeDtypeStruct((length // count, rank), F32)
    *chunks, field = pl.pallas_call(
        functools.partial(image_kernel, mid),
        out_shape=[chunk] * count + [jax.ShapeDtypeStruct((length, 2 * tile), F32)],
        in_specs=[VMEM] * (len(parts) + 1),
        out_specs=[VMEM] * (count + 1),
        scratch_shapes=[pltpu.VMEM((length, rank), F32)],
        compiler_params=BIG,
        name="image",
    )(*parts, start_basis)
    field = crossed(field, mid, 0, 0)
    total = sum(crossed(chunks[step], mid, step, 0) for step in range(count - 1, -1, -1))
    total = sum(crossed(total, distant, step, 1) for step in range(2 ** len(distant) - 1, -1, -1))
    chunks = [crossed(total, mid, step, 0) for step in range(count)]
    first, second = pl.pallas_call(
        functools.partial(factor_kernel, mid),
        out_shape=[jax.ShapeDtypeStruct((rank, tile), F32)] * 2,
        in_specs=[VMEM] * (1 + count),
        out_specs=[VMEM] * 2,
        scratch_shapes=[
            pltpu.VMEM((length, rank), F32),
            pltpu.VMEM((rank, rank + 2 * tile), F32),
            pltpu.VMEM((SLAB, rank + 2 * tile), F32),
        ],
        compiler_params=BIG,
        name="factor",
    )(field, *chunks)
    core_values = first + lax.ppermute(second, "fib", core_swap)
    return core_values[None, None]


def solution(mesh):
    placed = (P("pln", "fib", None, None), P(), P("pln", None, None), P("pln", "fib", None), P())
    return jax.shard_map(
        per_device,
        mesh=mesh,
        in_specs=placed,
        out_specs=P("pln", "fib", None, None),
        check_vma=False,
    )
```

```python
import functools

import jax
import jax.numpy as jnp
from jax import lax
from jax.experimental import pallas as pl
from jax.experimental.pallas import tpu as pltpu
from jax.sharding import PartitionSpec as P

F32 = jnp.float32
BF16 = jnp.bfloat16
SLAB = 8
BLOCK = 16
KSTEP = 256
VMEM = pl.BlockSpec(memory_space=pltpu.VMEM)
SMEM = pl.BlockSpec(memory_space=pltpu.SMEM)
BIG = pltpu.CompilerParams(vmem_limit_bytes=32 * 1024 * 1024)


def halves(value):
    high = value.astype(BF16)
    return high, (value - high.astype(F32)).astype(BF16)


def dot3(left, right, contract):
    dims = (contract, ((), ()))
    lh, ll = left
    rh, rl = right
    out = lax.dot_general(lh, rl, dims, preferred_element_type=F32)
    out += lax.dot_general(ll, rh, dims, preferred_element_type=F32)
    return out + lax.dot_general(lh, rh, dims, preferred_element_type=F32)


def interp_kernel(owners, table_hbm, node_hbm, interp_hbm, swap_ref, one_ref, send_ref, zero_ref, *scratch):
    grid_scr, node_ref, interp_ref, table_ref, sems = scratch
    rows = zero_ref.shape[0]
    slots, depth = node_ref.shape
    own = lax.axis_index("fib")
    copies = [pltpu.make_async_copy(table_hbm, table_ref, sems.at[0])]
    for part in range(slots // rows):
        at = pl.ds(part * rows, rows)
        copies.append(pltpu.make_async_copy(node_hbm.at[at, :], node_ref.at[at, :], sems.at[len(copies)]))
    steps = [(at, min(KSTEP, depth - at)) for at in range(0, depth, KSTEP)]
    first = len(copies)
    for at, size in steps:
        part = pl.ds(at, size)
        copies.append(
            pltpu.make_async_copy(interp_hbm.at[part, :], interp_ref.at[part, :], sems.at[len(copies)])
        )
    for copy in copies:
        copy.start()
    for copy in copies[:first]:
        copy.wait()
    total = None
    for (at, size), copy in zip(steps, copies[first:]):
        copy.wait()
        part = dot3(
            halves(node_ref[:, at : at + size]), halves(interp_ref[at : at + size, :]), ((1,), (0,))
        )
        total = part if total is None else total + part
    grid_scr[:slots, :] = total
    zero_ref[...] = grid_scr[:rows, :]
    start = table_ref[0, 0, own]
    for distance in range(1, 3):
        shift = lax.rem(start, SLAB)
        at = pl.multiple_of(start - shift, SLAB)
        wide = grid_scr[pl.ds(at, rows + SLAB), :]
        piece = pltpu.roll(wide, lax.rem(rows + SLAB - shift, rows + SLAB), 0)[:rows, :]
        if distance == 1:
            one_ref[...] = piece
            send_ref[:rows, :] = piece
        else:
            send_ref[rows:, :] = piece
        start = start + table_ref[distance, 0, lax.rem(own + distance, owners)]
    second = lax.rem(own, 2) == 1

    @pl.when(second)
    def _():
        swap_ref[...] = zero_ref[...]

    @pl.when(jnp.logical_not(second))
    def _():
        swap_ref[...] = send_ref[rows:, :]


def pick_kernel(rows, per_tile, table_ref, order_ref, order_next_ref, out_ref):
    elements = order_ref.shape[1]
    slots = out_ref.shape[1]
    chip = lax.div(lax.axis_index("fib"), 2)
    rank_at = lax.broadcasted_iota(jnp.int32, (elements, slots), 0)
    slot_at = lax.broadcasted_iota(jnp.int32, (elements, slots), 1)
    row = lax.broadcasted_iota(jnp.int32, (elements, elements), 0)
    for core, order in enumerate((order_ref, order_next_ref)):
        from_slot = jnp.zeros((elements, slots), jnp.bool_)
        start = 0
        for distance in range(slots // rows - 1, -1, -1):
            count = table_ref[distance, 0, 2 * chip + core]
            inside = (rank_at >= start) & (rank_at < start + count)
            from_slot = from_slot | (inside & (slot_at - distance * rows == rank_at - start))
            start = start + count
        place = order[...]
        tile = lax.div(place, jnp.full_like(place, per_tile))
        place = place - tile * per_tile + (tile ^ (2 * chip)) * per_tile
        place = jnp.broadcast_to(place, (elements, elements))
        to_place = jnp.where(place == row, 1.0, 0.0).astype(BF16)
        out_ref[core * elements : (core + 1) * elements, :] = jnp.dot(
            to_place, jnp.where(from_slot, 1.0, 0.0).astype(BF16), preferred_element_type=F32
        )


def order_kernel(pick_ref, zero_ref, one_ref, next_zero_ref, back_ref, back_two_ref, *outs):
    rows = zero_ref.shape[0]
    elements = outs[0].shape[0]
    sources = (
        (zero_ref[...], back_ref[:rows, :], back_two_ref[...]),
        (next_zero_ref[...], one_ref[...], back_ref[rows:, :]),
    )
    for core, pieces in enumerate(sources):
        pick = pick_ref[core * elements : (core + 1) * elements, :].astype(BF16)
        line = jnp.concatenate(pieces, axis=0)
        high = line.astype(BF16)
        rest = line - high.astype(F32)
        mid = rest.astype(BF16)
        low = (rest - mid.astype(F32)).astype(BF16)
        out = jnp.dot(pick, low, preferred_element_type=F32)
        out += jnp.dot(pick, mid, preferred_element_type=F32)
        outs[core][...] = out + jnp.dot(pick, high, preferred_element_type=F32)


def bit_place(order):
    index = 0
    for axis, mask in order:
        index = index * 2 + lax.rem(lax.div(lax.axis_index(axis), mask), 2)
    return index


def image_kernel(mid, *refs):
    field_ref, image_scr = refs[-2:]
    count = 2 ** len(mid)
    outs = refs[-2 - count : -2]
    *block_refs, start_ref = refs[: -2 - count]
    length, width = field_ref.shape
    tile = width // 2
    chip = lax.div(lax.axis_index("fib"), 2)
    each = length // (2 * len(block_refs))
    if len(block_refs) == 1:
        field_ref[...] = block_refs[0][...]
        block_refs = []
    for step, block in enumerate(block_refs):
        for owner in range(2):
            at = pl.multiple_of((2 * (chip ^ step) + owner) * each, each)
            for core in range(2):
                part = (2 * owner + core) * each
                field_ref[pl.ds(at, each), core * tile : (core + 1) * tile] = block[part : part + each, :]
    field = halves(field_ref[...])
    mixed = dot3(field, halves(start_ref[...]), ((0,), (0,)))
    image_scr[...] = dot3(field, halves(mixed), ((1,), (0,)))
    place = bit_place(mid)
    for step, out in enumerate(outs):
        rows = out.shape[0]
        at = pl.multiple_of((place ^ step) * rows, rows)
        out[...] = image_scr[pl.ds(at, rows), :]


def factor_kernel(mid, field_ref, *refs):
    chunk_refs, out_refs, image_scr, work, line_scr = refs[:-5], refs[-5:-3], refs[-3], refs[-2], refs[-1]
    rank = image_scr.shape[1]
    place = bit_place(mid)
    for step, chunk in enumerate(chunk_refs):
        rows = chunk.shape[0]
        at = pl.multiple_of((place ^ step) * rows, rows)
        image_scr[pl.ds(at, rows), :] = chunk[...]
    image = halves(image_scr[...])
    work[:, :rank] = dot3(image, image, ((0,), (0,)))
    work[:, rank:] = dot3(image, halves(field_ref[...]), ((0,), (0,)))
    width = work.shape[1]

    def splat(row, lane):
        return jnp.broadcast_to(row[:, lane : lane + 1], (1, rank))

    def scaled(factor, row):
        return row * jnp.concatenate([factor] * (width // rank), axis=1)

    for base in range(0, rank, BLOCK):
        line = [work[base + k : base + k + 1, :] for k in range(BLOCK)]
        for slab in range(0, BLOCK, SLAB):
            ahead = base + slab
            entry = [[splat(line[slab + k], ahead + i) for i in range(SLAB)] for k in range(SLAB)]
            for k in range(SLAB):
                scale = lax.rsqrt(entry[k][k])
                line[slab + k] = scaled(scale, line[slab + k])
                factor = {i: entry[k][i] * scale for i in range(k + 1, SLAB)}
                for i in range(k + 1, SLAB):
                    for j in range(i, SLAB):
                        entry[i][j] = entry[i][j] - factor[i] * factor[j]
                    line[slab + i] = line[slab + i] - scaled(factor[i], line[slab + k])
                row = line[slab + k]
                for core, out in enumerate(out_refs):
                    out[ahead + k : ahead + k + 1, :] = row[:, (core + 1) * rank : (core + 2) * rank]
                line_scr[slab + k : slab + k + 1, :] = row
            for i in range(slab + SLAB, BLOCK):
                for k in range(slab, slab + SLAB):
                    line[i] = line[i] - scaled(splat(line[k], base + i), line[k])
        after = base + BLOCK
        if after < rank:
            rows = line_scr[...]
            high = rows.astype(BF16).astype(F32)
            rest = rows - high
            mid_part = rest.astype(BF16).astype(F32)
            low = rest - mid_part
            first = jnp.concatenate([x[:, :rank] for x in (high, high, mid_part, high, low, mid_part)], axis=0)
            second = jnp.concatenate([high, mid_part, high, low, high, mid_part], axis=0)
            drop = lax.dot_general(
                first.astype(BF16),
                second.astype(BF16),
                (((0,), (0,)), ((), ())),
                preferred_element_type=F32,
            )
            work[after:, :] = work[after:, :] - drop[after:, :]

    @pl.when(lax.rem(lax.axis_index("fib"), 2) == 1)
    def _():
        for out in out_refs:
            out[...] = jnp.zeros_like(out)


def crossed(value, bits, step, to_core):
    apart = [bit for at, bit in enumerate(reversed(bits)) if step >> at & 1]
    peers = {axis: sum(mask for name, mask in apart if name == axis) for axis in ("fib", "pln")}
    owners, planes = lax.axis_size("fib"), lax.axis_size("pln")
    pairs = []
    for i in range(owners * planes):
        fib, pln = divmod(i, planes)
        if fib % 2 != to_core:
            fib, pln = fib ^ peers["fib"], pln ^ peers["pln"]
        pairs.append((i, (fib ^ 1) * planes + pln))
    return lax.ppermute(value, ("fib", "pln"), pairs)


def masks(axis, low, high):
    out = []
    while low < high:
        out.append((axis, low))
        low *= 2
    return out


def per_device(nodal_values, interp_matrix, count_table, slot_order, start_basis):
    nodes = nodal_values[0, 0]
    table = jnp.transpose(count_table, (2, 0, 1))
    owners = lax.axis_size("fib")
    planes = lax.axis_size("pln")
    window = table.shape[0]
    capacity = nodes.shape[0] // window
    points = interp_matrix.shape[1]
    elements = slot_order.shape[2]
    length, rank = start_basis.shape
    tile = points * elements // length
    core_swap = [(i, i ^ 1) for i in range(owners)]
    forward = [(i, (i + 1) % owners) for i in range(owners)]

    order_next = lax.ppermute(slot_order[0], "fib", core_swap)
    piece = jax.ShapeDtypeStruct((capacity, points), F32)
    copies = 1 + window + pl.cdiv(nodes.shape[1], KSTEP)
    swap, one, send, zero = pl.pallas_call(
        functools.partial(interp_kernel, owners),
        out_shape=[piece, piece, jax.ShapeDtypeStruct((2 * capacity, points), F32), piece],
        in_specs=[pl.BlockSpec(memory_space=pl.ANY)] * 3,
        out_specs=[VMEM] * 4,
        scratch_shapes=[
            pltpu.VMEM((nodes.shape[0] + SLAB, points), F32),
            pltpu.VMEM(nodes.shape, F32),
            pltpu.VMEM(interp_matrix.shape, F32),
            pltpu.SMEM(table.shape, jnp.int32),
            pltpu.SemaphoreType.DMA((copies,)),
        ],
        compiler_params=BIG,
        name="interp",
    )(*(pltpu.with_memory_space_constraint(x, pltpu.HBM) for x in (table, nodes, interp_matrix)))
    swapped = lax.ppermute(swap, "fib", core_swap)
    back = lax.ppermute(send, "fib", forward)
    back_two = lax.ppermute(swapped, "fib", forward)
    pick = pl.pallas_call(
        functools.partial(pick_kernel, capacity, elements // owners),
        out_shape=jax.ShapeDtypeStruct((2 * elements, capacity * window), F32),
        in_specs=[SMEM, VMEM, VMEM],
        out_specs=VMEM,
        compiler_params=BIG,
        name="pick",
    )(table, slot_order[0], order_next)
    bricks = pl.pallas_call(
        order_kernel,
        out_shape=[jax.ShapeDtypeStruct((elements, points), F32)] * 2,
        in_specs=[VMEM] * 6,
        out_specs=[VMEM] * 2,
        compiler_params=BIG,
        name="order",
    )(pick, zero, one, swapped, back, back_two)

    blocks = owners // 2
    chips = masks("fib", 2, owners)[::-1]
    both = jnp.concatenate([b.reshape(blocks, 2 * length // owners, tile) for b in bricks], axis=1)
    got = {step: crossed(both[step], chips, step, 1) for step in range(blocks - 1, -1, -1)}
    parts = [got[step] for step in range(blocks)]
    if length // owners % SLAB:
        at = lax.axis_index("fib") // 2 ^ jnp.arange(blocks)
        whole = jnp.stack(parts)[at].reshape(blocks, 2, 2, length // owners, tile)
        parts = [whole.transpose(0, 1, 3, 2, 4).reshape(length, 2 * tile)]

    mid = masks("fib", 2, 4) + masks("pln", 1, planes)
    distant = masks("fib", 4, owners)
    count = 2 ** len(mid)
    chunk = jax.ShapeDtypeStruct((length // count, rank), F32)
    *chunks, field = pl.pallas_call(
        functools.partial(image_kernel, mid),
        out_shape=[chunk] * count + [jax.ShapeDtypeStruct((length, 2 * tile), F32)],
        in_specs=[VMEM] * (len(parts) + 1),
        out_specs=[VMEM] * (count + 1),
        scratch_shapes=[pltpu.VMEM((length, rank), F32)],
        compiler_params=BIG,
        name="image",
    )(*parts, start_basis)
    field = crossed(field, mid, 0, 0)
    total = sum(crossed(chunks[step], mid, step, 0) for step in range(count - 1, -1, -1))
    total = sum(crossed(total, distant, step, 1) for step in range(2 ** len(distant) - 1, -1, -1))
    chunks = [crossed(total, mid, step, 0) for step in range(count)]
    first, second = pl.pallas_call(
        functools.partial(factor_kernel, mid),
        out_shape=[jax.ShapeDtypeStruct((rank, tile), F32)] * 2,
        in_specs=[VMEM] * (1 + count),
        out_specs=[VMEM] * 2,
        scratch_shapes=[
            pltpu.VMEM((length, rank), F32),
            pltpu.VMEM((rank, rank + 2 * tile), F32),
            pltpu.VMEM((BLOCK, rank + 2 * tile), F32),
        ],
        compiler_params=BIG,
        name="factor",
    )(field, *chunks)
    core_values = first + lax.ppermute(second, "fib", core_swap)
    return core_values[None, None]


def solution(mesh):
    placed = (P("pln", "fib", None, None), P(), P("pln", None, None), P("pln", "fib", None), P())
    return jax.shard_map(
        per_device,
        mesh=mesh,
        in_specs=placed,
        out_specs=P("pln", "fib", None, None),
        check_vma=False,
    )
```

```python
import functools

import jax
import jax.numpy as jnp
from jax import lax
from jax.experimental import pallas as pl
from jax.experimental.pallas import tpu as pltpu
from jax.sharding import PartitionSpec as P

F32 = jnp.float32
BF16 = jnp.bfloat16
SLAB = 8
BLOCK = 16
KSTEP = 256
VMEM = pl.BlockSpec(memory_space=pltpu.VMEM)
SMEM = pl.BlockSpec(memory_space=pltpu.SMEM)
BIG = pltpu.CompilerParams(vmem_limit_bytes=32 * 1024 * 1024)


def halves(value):
    high = value.astype(BF16)
    return high, (value - high.astype(F32)).astype(BF16)


def dot3(left, right, contract):
    dims = (contract, ((), ()))
    lh, ll = left
    rh, rl = right
    (lk,), (rk,) = contract
    if lh.shape[lk] % 128 == 0:
        longer_left = jnp.concatenate([lh, ll, lh], axis=lk)
        longer_right = jnp.concatenate([rl, rh, rh], axis=rk)
        return lax.dot_general(longer_left, longer_right, dims, preferred_element_type=F32)
    out = lax.dot_general(lh, rl, dims, preferred_element_type=F32)
    out += lax.dot_general(ll, rh, dims, preferred_element_type=F32)
    return out + lax.dot_general(lh, rh, dims, preferred_element_type=F32)


def interp_kernel(owners, table_hbm, node_hbm, interp_hbm, swap_ref, one_ref, send_ref, zero_ref, *scratch):
    grid_scr, node_ref, interp_ref, table_ref, sems = scratch
    rows = zero_ref.shape[0]
    slots, depth = node_ref.shape
    own = lax.axis_index("fib")
    copies = [pltpu.make_async_copy(table_hbm, table_ref, sems.at[0])]
    for part in range(slots // rows):
        at = pl.ds(part * rows, rows)
        copies.append(pltpu.make_async_copy(node_hbm.at[at, :], node_ref.at[at, :], sems.at[len(copies)]))
    steps = [(at, min(KSTEP, depth - at)) for at in range(0, depth, KSTEP)]
    first = len(copies)
    for at, size in steps:
        part = pl.ds(at, size)
        copies.append(
            pltpu.make_async_copy(interp_hbm.at[part, :], interp_ref.at[part, :], sems.at[len(copies)])
        )
    for copy in copies:
        copy.start()
    for copy in copies[:first]:
        copy.wait()
    total = None
    for (at, size), copy in zip(steps, copies[first:]):
        copy.wait()
        part = dot3(
            halves(node_ref[:, at : at + size]), halves(interp_ref[at : at + size, :]), ((1,), (0,))
        )
        total = part if total is None else total + part
    grid_scr[:slots, :] = total
    zero_ref[...] = grid_scr[:rows, :]
    start = table_ref[0, 0, own]
    for distance in range(1, 3):
        shift = lax.rem(start, SLAB)
        at = pl.multiple_of(start - shift, SLAB)
        wide = grid_scr[pl.ds(at, rows + SLAB), :]
        piece = pltpu.roll(wide, lax.rem(rows + SLAB - shift, rows + SLAB), 0)[:rows, :]
        if distance == 1:
            one_ref[...] = piece
            send_ref[:rows, :] = piece
        else:
            send_ref[rows:, :] = piece
        start = start + table_ref[distance, 0, lax.rem(own + distance, owners)]
    second = lax.rem(own, 2) == 1

    @pl.when(second)
    def _():
        swap_ref[...] = zero_ref[...]

    @pl.when(jnp.logical_not(second))
    def _():
        swap_ref[...] = send_ref[rows:, :]


def pick_kernel(rows, per_tile, table_ref, order_ref, order_next_ref, start_ref, out_ref, high_ref, low_ref):
    elements = order_ref.shape[1]
    slots = out_ref.shape[1]
    chip = lax.div(lax.axis_index("fib"), 2)
    rank_at = lax.broadcasted_iota(jnp.int32, (elements, slots), 0)
    slot_at = lax.broadcasted_iota(jnp.int32, (elements, slots), 1)
    row = lax.broadcasted_iota(jnp.int32, (elements, elements), 0)
    for core, order in enumerate((order_ref, order_next_ref)):
        from_slot = jnp.zeros((elements, slots), jnp.bool_)
        start = 0
        for distance in range(slots // rows - 1, -1, -1):
            count = table_ref[distance, 0, 2 * chip + core]
            inside = (rank_at >= start) & (rank_at < start + count)
            from_slot = from_slot | (inside & (slot_at - distance * rows == rank_at - start))
            start = start + count
        place = order[...]
        tile = lax.div(place, jnp.full_like(place, per_tile))
        place = place - tile * per_tile + (tile ^ (2 * chip)) * per_tile
        place = jnp.broadcast_to(place, (elements, elements))
        to_place = jnp.where(place == row, 1.0, 0.0).astype(BF16)
        out_ref[core * elements : (core + 1) * elements, :] = jnp.dot(
            to_place, jnp.where(from_slot, 1.0, 0.0).astype(BF16), preferred_element_type=F32
        ).astype(BF16)
    high_ref[...], low_ref[...] = halves(start_ref[...].T)


def order_kernel(pick_ref, zero_ref, one_ref, next_zero_ref, back_ref, back_two_ref, *outs):
    rows = zero_ref.shape[0]
    elements = outs[0].shape[0]
    sources = (
        (zero_ref[...], back_ref[:rows, :], back_two_ref[...]),
        (next_zero_ref[...], one_ref[...], back_ref[rows:, :]),
    )
    for core, pieces in enumerate(sources):
        pick = pick_ref[core * elements : (core + 1) * elements, :]
        high, low = halves(jnp.concatenate(pieces, axis=0))
        out = jnp.dot(pick, low, preferred_element_type=F32)
        outs[core][...] = out + jnp.dot(pick, high, preferred_element_type=F32)


def bit_place(order):
    index = 0
    for axis, mask in order:
        index = index * 2 + lax.rem(lax.div(lax.axis_index(axis), mask), 2)
    return index


def image_kernel(mid, *refs):
    field_ref, image_scr = refs[-2:]
    count = 2 ** len(mid)
    outs = refs[-2 - count : -2]
    *block_refs, high_ref, low_ref = refs[: -2 - count]
    length, width = field_ref.shape
    tile = width // 2
    chip = lax.div(lax.axis_index("fib"), 2)
    each = length // (2 * len(block_refs))
    if len(block_refs) == 1:
        field_ref[...] = block_refs[0][...]
        block_refs = []
    for step, block in enumerate(block_refs):
        for owner in range(2):
            at = pl.multiple_of((2 * (chip ^ step) + owner) * each, each)
            for core in range(2):
                part = (2 * owner + core) * each
                field_ref[pl.ds(at, each), core * tile : (core + 1) * tile] = block[part : part + each, :]
    field = halves(field_ref[...])
    mixed = dot3((high_ref[...], low_ref[...]), field, ((1,), (0,)))
    image_scr[...] = dot3(field, halves(mixed), ((1,), (1,)))
    place = bit_place(mid)
    for step, out in enumerate(outs):
        rows = out.shape[0]
        at = pl.multiple_of((place ^ step) * rows, rows)
        out[...] = image_scr[pl.ds(at, rows), :]


def split_kernel(value_ref, high_ref, low_ref):
    high_ref[...], low_ref[...] = halves(value_ref[...])


def factor_kernel(mid, high_ref, low_ref, *refs):
    chunk_refs, out_refs, image_scr, work, line_scr = refs[:-5], refs[-5:-3], refs[-3], refs[-2], refs[-1]
    rank = image_scr.shape[1]
    place = bit_place(mid)
    for step, chunk in enumerate(chunk_refs):
        rows = chunk.shape[0]
        at = pl.multiple_of((place ^ step) * rows, rows)
        image_scr[pl.ds(at, rows), :] = chunk[...]
    image = halves(image_scr[...])
    work[:, :rank] = dot3(image, image, ((0,), (0,)))
    work[:, rank:] = dot3(image, (high_ref[...], low_ref[...]), ((0,), (0,)))
    width = work.shape[1]

    def splat(row, lane):
        return jnp.broadcast_to(row[:, lane : lane + 1], (1, rank))

    def scaled(factor, row):
        return row * jnp.concatenate([factor] * (width // rank), axis=1)

    for base in range(0, rank, BLOCK):
        line = [work[base + k : base + k + 1, :] for k in range(BLOCK)]
        for slab in range(0, BLOCK, SLAB):
            ahead = base + slab
            entry = [[splat(line[slab + k], ahead + i) for i in range(SLAB)] for k in range(SLAB)]
            for k in range(SLAB):
                scale = lax.rsqrt(entry[k][k])
                line[slab + k] = scaled(scale, line[slab + k])
                factor = {i: entry[k][i] * scale for i in range(k + 1, SLAB)}
                for i in range(k + 1, SLAB):
                    for j in range(i, SLAB):
                        entry[i][j] = entry[i][j] - factor[i] * factor[j]
                    line[slab + i] = line[slab + i] - scaled(factor[i], line[slab + k])
                row = line[slab + k]
                for core, out in enumerate(out_refs):
                    out[ahead + k : ahead + k + 1, :] = row[:, (core + 1) * rank : (core + 2) * rank]
                line_scr[slab + k : slab + k + 1, :] = row
            for i in range(slab + SLAB, BLOCK):
                for k in range(slab, slab + SLAB):
                    line[i] = line[i] - scaled(splat(line[k], base + i), line[k])
        after = base + BLOCK
        if after < rank:
            rows = line_scr[...]
            high = rows.astype(BF16).astype(F32)
            rest = rows - high
            mid_part = rest.astype(BF16).astype(F32)
            low = rest - mid_part
            first = jnp.concatenate([x[:, :rank] for x in (high, high, mid_part, high, low, mid_part)], axis=0)
            second = jnp.concatenate([high, mid_part, high, low, high, mid_part], axis=0)
            drop = lax.dot_general(
                first.astype(BF16),
                second.astype(BF16),
                (((0,), (0,)), ((), ())),
                preferred_element_type=F32,
            )
            work[after:, :] = work[after:, :] - drop[after:, :]

    @pl.when(lax.rem(lax.axis_index("fib"), 2) == 1)
    def _():
        for out in out_refs:
            out[...] = jnp.zeros_like(out)


def crossed(value, bits, step, to_core):
    apart = [bit for at, bit in enumerate(reversed(bits)) if step >> at & 1]
    peers = {axis: sum(mask for name, mask in apart if name == axis) for axis in ("fib", "pln")}
    owners, planes = lax.axis_size("fib"), lax.axis_size("pln")
    pairs = []
    for i in range(owners * planes):
        fib, pln = divmod(i, planes)
        if fib % 2 != to_core:
            fib, pln = fib ^ peers["fib"], pln ^ peers["pln"]
        pairs.append((i, (fib ^ 1) * planes + pln))
    return lax.ppermute(value, ("fib", "pln"), pairs)


def masks(axis, low, high):
    out = []
    while low < high:
        out.append((axis, low))
        low *= 2
    return out


def per_device(nodal_values, interp_matrix, count_table, slot_order, start_basis):
    nodes = nodal_values[0, 0]
    table = jnp.transpose(count_table, (2, 0, 1))
    owners = lax.axis_size("fib")
    planes = lax.axis_size("pln")
    window = table.shape[0]
    capacity = nodes.shape[0] // window
    points = interp_matrix.shape[1]
    elements = slot_order.shape[2]
    length, rank = start_basis.shape
    tile = points * elements // length
    core_swap = [(i, i ^ 1) for i in range(owners)]
    forward = [(i, (i + 1) % owners) for i in range(owners)]

    order_next = lax.ppermute(slot_order[0], "fib", core_swap)
    piece = jax.ShapeDtypeStruct((capacity, points), F32)
    copies = 1 + window + pl.cdiv(nodes.shape[1], KSTEP)
    swap, one, send, zero = pl.pallas_call(
        functools.partial(interp_kernel, owners),
        out_shape=[piece, piece, jax.ShapeDtypeStruct((2 * capacity, points), F32), piece],
        in_specs=[pl.BlockSpec(memory_space=pl.ANY)] * 3,
        out_specs=[VMEM] * 4,
        scratch_shapes=[
            pltpu.VMEM((nodes.shape[0] + SLAB, points), F32),
            pltpu.VMEM(nodes.shape, F32),
            pltpu.VMEM(interp_matrix.shape, F32),
            pltpu.SMEM(table.shape, jnp.int32),
            pltpu.SemaphoreType.DMA((copies,)),
        ],
        compiler_params=BIG,
        name="interp",
    )(*(pltpu.with_memory_space_constraint(x, pltpu.HBM) for x in (table, nodes, interp_matrix)))
    swapped = lax.ppermute(swap, "fib", core_swap)
    back = lax.ppermute(send, "fib", forward)
    back_two = lax.ppermute(swapped, "fib", forward)
    basis = jax.ShapeDtypeStruct((rank, length), BF16)
    pick, *basis_parts = pl.pallas_call(
        functools.partial(pick_kernel, capacity, elements // owners),
        out_shape=[jax.ShapeDtypeStruct((2 * elements, capacity * window), BF16), basis, basis],
        in_specs=[SMEM, VMEM, VMEM, VMEM],
        out_specs=[VMEM] * 3,
        compiler_params=BIG,
        name="pick",
    )(table, slot_order[0], order_next, start_basis)
    bricks = pl.pallas_call(
        order_kernel,
        out_shape=[jax.ShapeDtypeStruct((elements, points), F32)] * 2,
        in_specs=[VMEM] * 6,
        out_specs=[VMEM] * 2,
        compiler_params=BIG,
        name="order",
    )(pick, zero, one, swapped, back, back_two)

    blocks = owners // 2
    chips = masks("fib", 2, owners)[::-1]
    both = jnp.concatenate([b.reshape(blocks, 2 * length // owners, tile) for b in bricks], axis=1)
    got = {step: crossed(both[step], chips, step, 1) for step in range(blocks - 1, -1, -1)}
    parts = [got[step] for step in range(blocks)]
    if length // owners % SLAB:
        at = lax.axis_index("fib") // 2 ^ jnp.arange(blocks)
        whole = jnp.stack(parts)[at].reshape(blocks, 2, 2, length // owners, tile)
        parts = [whole.transpose(0, 1, 3, 2, 4).reshape(length, 2 * tile)]

    mid = masks("fib", 2, 4) + masks("pln", 1, planes)
    distant = masks("fib", 4, owners)
    count = 2 ** len(mid)
    chunk = jax.ShapeDtypeStruct((length // count, rank), F32)
    *chunks, field = pl.pallas_call(
        functools.partial(image_kernel, mid),
        out_shape=[chunk] * count + [jax.ShapeDtypeStruct((length, 2 * tile), F32)],
        in_specs=[VMEM] * (len(parts) + 2),
        out_specs=[VMEM] * (count + 1),
        scratch_shapes=[pltpu.VMEM((length, rank), F32)],
        compiler_params=BIG,
        name="image",
    )(*parts, *basis_parts)
    field_part = jax.ShapeDtypeStruct((length, 2 * tile), BF16)
    field_halves = pl.pallas_call(
        split_kernel,
        out_shape=[field_part] * 2,
        in_specs=[VMEM],
        out_specs=[VMEM] * 2,
        compiler_params=BIG,
        name="split",
    )(crossed(field, mid, 0, 0))
    total = sum(crossed(chunks[step], mid, step, 0) for step in range(count - 1, -1, -1))
    total = sum(crossed(total, distant, step, 1) for step in range(2 ** len(distant) - 1, -1, -1))
    chunks = [crossed(total, mid, step, 0) for step in range(count)]
    first, second = pl.pallas_call(
        functools.partial(factor_kernel, mid),
        out_shape=[jax.ShapeDtypeStruct((rank, tile), F32)] * 2,
        in_specs=[VMEM] * (2 + count),
        out_specs=[VMEM] * 2,
        scratch_shapes=[
            pltpu.VMEM((length, rank), F32),
            pltpu.VMEM((rank, rank + 2 * tile), F32),
            pltpu.VMEM((BLOCK, rank + 2 * tile), F32),
        ],
        compiler_params=BIG,
        name="factor",
    )(*field_halves, *chunks)
    core_values = first + lax.ppermute(second, "fib", core_swap)
    return core_values[None, None]


def solution(mesh):
    placed = (P("pln", "fib", None, None), P(), P("pln", None, None), P("pln", "fib", None), P())
    return jax.shard_map(
        per_device,
        mesh=mesh,
        in_specs=placed,
        out_specs=P("pln", "fib", None, None),
        check_vma=False,
    )
```

```python
import functools

import jax
import jax.numpy as jnp
from jax import lax
from jax.experimental import pallas as pl
from jax.experimental.pallas import tpu as pltpu
from jax.sharding import PartitionSpec as P

F32 = jnp.float32
BF16 = jnp.bfloat16
SLAB = 8
BLOCK = 16
KSTEP = 256
VMEM = pl.BlockSpec(memory_space=pltpu.VMEM)
SMEM = pl.BlockSpec(memory_space=pltpu.SMEM)
BIG = pltpu.CompilerParams(vmem_limit_bytes=32 * 1024 * 1024)


def halves(value):
    high = value.astype(BF16)
    return high, (value - high.astype(F32)).astype(BF16)


def dot3(left, right, contract):
    dims = (contract, ((), ()))
    lh, ll = left
    rh, rl = right
    (lk,), (rk,) = contract
    if lh.shape[lk] % 128 == 0:
        longer_left = jnp.concatenate([lh, ll, lh], axis=lk)
        longer_right = jnp.concatenate([rl, rh, rh], axis=rk)
        return lax.dot_general(longer_left, longer_right, dims, preferred_element_type=F32)
    out = lax.dot_general(lh, rl, dims, preferred_element_type=F32)
    out += lax.dot_general(ll, rh, dims, preferred_element_type=F32)
    return out + lax.dot_general(lh, rh, dims, preferred_element_type=F32)


def interp_kernel(owners, table_hbm, node_hbm, interp_hbm, swap_ref, one_ref, send_ref, zero_ref, *scratch):
    grid_scr, node_ref, interp_ref, table_ref, sems = scratch
    rows = zero_ref.shape[0]
    slots, depth = node_ref.shape
    own = lax.axis_index("fib")
    copies = [pltpu.make_async_copy(table_hbm, table_ref, sems.at[0])]
    for part in range(slots // rows):
        at = pl.ds(part * rows, rows)
        copies.append(pltpu.make_async_copy(node_hbm.at[at, :], node_ref.at[at, :], sems.at[len(copies)]))
    steps = [(at, min(KSTEP, depth - at)) for at in range(0, depth, KSTEP)]
    first = len(copies)
    for at, size in steps:
        part = pl.ds(at, size)
        copies.append(
            pltpu.make_async_copy(interp_hbm.at[part, :], interp_ref.at[part, :], sems.at[len(copies)])
        )
    for copy in copies:
        copy.start()
    for copy in copies[:first]:
        copy.wait()
    total = None
    for (at, size), copy in zip(steps, copies[first:]):
        copy.wait()
        part = dot3(
            halves(node_ref[:, at : at + size]), halves(interp_ref[at : at + size, :]), ((1,), (0,))
        )
        total = part if total is None else total + part
    grid_scr[:slots, :] = total
    zero_ref[...] = grid_scr[:rows, :]
    start = table_ref[0, 0, own]
    for distance in range(1, 3):
        shift = lax.rem(start, SLAB)
        at = pl.multiple_of(start - shift, SLAB)
        wide = grid_scr[pl.ds(at, rows + SLAB), :]
        piece = pltpu.roll(wide, lax.rem(rows + SLAB - shift, rows + SLAB), 0)[:rows, :]
        if distance == 1:
            one_ref[...] = piece
            send_ref[:rows, :] = piece
        else:
            send_ref[rows:, :] = piece
        start = start + table_ref[distance, 0, lax.rem(own + distance, owners)]
    second = lax.rem(own, 2) == 1

    @pl.when(second)
    def _():
        swap_ref[...] = zero_ref[...]

    @pl.when(jnp.logical_not(second))
    def _():
        swap_ref[...] = send_ref[rows:, :]


def pick_kernel(rows, per_tile, table_ref, order_ref, order_next_ref, start_ref, out_ref, high_ref, low_ref):
    elements = order_ref.shape[1]
    slots = out_ref.shape[1]
    chip = lax.div(lax.axis_index("fib"), 2)
    rank_at = lax.broadcasted_iota(jnp.int32, (elements, slots), 0)
    slot_at = lax.broadcasted_iota(jnp.int32, (elements, slots), 1)
    row = lax.broadcasted_iota(jnp.int32, (elements, elements), 0)
    for core, order in enumerate((order_ref, order_next_ref)):
        from_slot = jnp.zeros((elements, slots), jnp.bool_)
        start = 0
        for distance in range(slots // rows - 1, -1, -1):
            count = table_ref[distance, 0, 2 * chip + core]
            inside = (rank_at >= start) & (rank_at < start + count)
            from_slot = from_slot | (inside & (slot_at - distance * rows == rank_at - start))
            start = start + count
        place = order[...]
        tile = lax.div(place, jnp.full_like(place, per_tile))
        place = place - tile * per_tile + (tile ^ (2 * chip)) * per_tile
        place = jnp.broadcast_to(place, (elements, elements))
        to_place = jnp.where(place == row, 1.0, 0.0).astype(BF16)
        out_ref[core * elements : (core + 1) * elements, :] = jnp.dot(
            to_place, jnp.where(from_slot, 1.0, 0.0).astype(BF16), preferred_element_type=F32
        ).astype(BF16)
    high_ref[...], low_ref[...] = halves(start_ref[...].T)


def order_kernel(pick_ref, zero_ref, one_ref, next_zero_ref, back_ref, back_two_ref, *outs):
    rows = zero_ref.shape[0]
    elements = outs[0].shape[0]
    sources = (
        (zero_ref[...], back_ref[:rows, :], back_two_ref[...]),
        (next_zero_ref[...], one_ref[...], back_ref[rows:, :]),
    )
    for core, pieces in enumerate(sources):
        pick = pick_ref[core * elements : (core + 1) * elements, :]
        high, low = halves(jnp.concatenate(pieces, axis=0))
        out = jnp.dot(pick, low, preferred_element_type=F32)
        outs[core][...] = out + jnp.dot(pick, high, preferred_element_type=F32)


def bit_place(order):
    index = 0
    for axis, mask in order:
        index = index * 2 + lax.rem(lax.div(lax.axis_index(axis), mask), 2)
    return index


def image_kernel(mid, *refs):
    field_ref, image_scr = refs[-2:]
    count = 2 ** len(mid)
    outs = refs[-2 - count : -2]
    *block_refs, high_ref, low_ref = refs[: -2 - count]
    length, width = field_ref.shape
    tile = width // 2
    chip = lax.div(lax.axis_index("fib"), 2)
    each = length // (2 * len(block_refs))
    if len(block_refs) == 1:
        field_ref[...] = block_refs[0][...]
        block_refs = []
    for step, block in enumerate(block_refs):
        for owner in range(2):
            at = pl.multiple_of((2 * (chip ^ step) + owner) * each, each)
            for core in range(2):
                part = (2 * owner + core) * each
                field_ref[pl.ds(at, each), core * tile : (core + 1) * tile] = block[part : part + each, :]
    field = halves(field_ref[...])
    mixed = dot3((high_ref[...], low_ref[...]), field, ((1,), (0,)))
    image_scr[...] = dot3(field, halves(mixed), ((1,), (1,)))
    place = bit_place(mid)
    for step, out in enumerate(outs):
        rows = out.shape[0]
        at = pl.multiple_of((place ^ step) * rows, rows)
        out[...] = image_scr[pl.ds(at, rows), :]


def split_kernel(value_ref, high_ref, low_ref):
    high_ref[...], low_ref[...] = halves(value_ref[...])


def factor_kernel(mid, high_ref, low_ref, *refs):
    chunk_refs, out_refs, image_scr, work, line_scr = refs[:-5], refs[-5:-3], refs[-3], refs[-2], refs[-1]
    rank = image_scr.shape[1]
    place = bit_place(mid)
    for step, chunk in enumerate(chunk_refs):
        rows = chunk.shape[0]
        at = pl.multiple_of((place ^ step) * rows, rows)
        image_scr[pl.ds(at, rows), :] = chunk[...]
    image = image_scr[...]
    image = halves(image * lax.rsqrt(jnp.sum(image * image, axis=0, keepdims=True)))
    work[:, :rank] = dot3(image, image, ((0,), (0,)))
    work[:, rank:] = dot3(image, (high_ref[...], low_ref[...]), ((0,), (0,)))
    width = work.shape[1]

    def splat(row, lane):
        return jnp.broadcast_to(row[:, lane : lane + 1], (1, rank))

    def scaled(factor, row):
        return row * jnp.concatenate([factor] * (width // rank), axis=1)

    for base in range(0, rank, BLOCK):
        line = [work[base + k : base + k + 1, :] for k in range(BLOCK)]
        for slab in range(0, BLOCK, SLAB):
            ahead = base + slab
            entry = [[splat(line[slab + k], ahead + i) for i in range(SLAB)] for k in range(SLAB)]
            for k in range(0, SLAB, 2):
                p, q, r = entry[k][k], entry[k][k + 1], entry[k + 1][k + 1]
                root = lax.rsqrt(p)
                scales = (root, lax.rsqrt(p * r - q * q) * (p * root))
                for n, scale in zip((k, k + 1), scales):
                    row = scaled(scale, line[slab + n])
                    factor = {i: entry[n][i] * scale for i in range(n + 1, SLAB)}
                    for i in range(n + 1, SLAB):
                        for j in range(i, SLAB):
                            entry[i][j] = entry[i][j] - factor[i] * factor[j]
                        line[slab + i] = line[slab + i] - scaled(factor[i], row)
                    line[slab + n] = row
                    for core, out in enumerate(out_refs):
                        out[ahead + n : ahead + n + 1, :] = row[:, (core + 1) * rank : (core + 2) * rank]
                    line_scr[slab + n : slab + n + 1, :] = row
            for i in range(slab + SLAB, BLOCK):
                for k in range(slab, slab + SLAB):
                    line[i] = line[i] - scaled(splat(line[k], base + i), line[k])
        after = base + BLOCK
        if after < rank:
            rows = line_scr[...]
            high = rows.astype(BF16).astype(F32)
            rest = rows - high
            mid_part = rest.astype(BF16).astype(F32)
            low = rest - mid_part
            first = jnp.concatenate([x[:, :rank] for x in (high, high, mid_part, high, low, mid_part)], axis=0)
            second = jnp.concatenate([high, mid_part, high, low, high, mid_part], axis=0)
            drop = lax.dot_general(
                first.astype(BF16),
                second.astype(BF16),
                (((0,), (0,)), ((), ())),
                preferred_element_type=F32,
            )
            work[after:, :] = work[after:, :] - drop[after:, :]

    @pl.when(lax.rem(lax.axis_index("fib"), 2) == 1)
    def _():
        for out in out_refs:
            out[...] = jnp.zeros_like(out)


def crossed(value, bits, step, to_core):
    apart = [bit for at, bit in enumerate(reversed(bits)) if step >> at & 1]
    peers = {axis: sum(mask for name, mask in apart if name == axis) for axis in ("fib", "pln")}
    owners, planes = lax.axis_size("fib"), lax.axis_size("pln")
    pairs = []
    for i in range(owners * planes):
        fib, pln = divmod(i, planes)
        if fib % 2 != to_core:
            fib, pln = fib ^ peers["fib"], pln ^ peers["pln"]
        pairs.append((i, (fib ^ 1) * planes + pln))
    return lax.ppermute(value, ("fib", "pln"), pairs)


def masks(axis, low, high):
    out = []
    while low < high:
        out.append((axis, low))
        low *= 2
    return out


def per_device(nodal_values, interp_matrix, count_table, slot_order, start_basis):
    nodes = nodal_values[0, 0]
    table = jnp.transpose(count_table, (2, 0, 1))
    owners = lax.axis_size("fib")
    planes = lax.axis_size("pln")
    window = table.shape[0]
    capacity = nodes.shape[0] // window
    points = interp_matrix.shape[1]
    elements = slot_order.shape[2]
    length, rank = start_basis.shape
    tile = points * elements // length
    core_swap = [(i, i ^ 1) for i in range(owners)]
    forward = [(i, (i + 1) % owners) for i in range(owners)]

    order_next = lax.ppermute(slot_order[0], "fib", core_swap)
    piece = jax.ShapeDtypeStruct((capacity, points), F32)
    copies = 1 + window + pl.cdiv(nodes.shape[1], KSTEP)
    swap, one, send, zero = pl.pallas_call(
        functools.partial(interp_kernel, owners),
        out_shape=[piece, piece, jax.ShapeDtypeStruct((2 * capacity, points), F32), piece],
        in_specs=[pl.BlockSpec(memory_space=pl.ANY)] * 3,
        out_specs=[VMEM] * 4,
        scratch_shapes=[
            pltpu.VMEM((nodes.shape[0] + SLAB, points), F32),
            pltpu.VMEM(nodes.shape, F32),
            pltpu.VMEM(interp_matrix.shape, F32),
            pltpu.SMEM(table.shape, jnp.int32),
            pltpu.SemaphoreType.DMA((copies,)),
        ],
        compiler_params=BIG,
        name="interp",
    )(*(pltpu.with_memory_space_constraint(x, pltpu.HBM) for x in (table, nodes, interp_matrix)))
    swapped = lax.ppermute(swap, "fib", core_swap)
    back = lax.ppermute(send, "fib", forward)
    back_two = lax.ppermute(swapped, "fib", forward)
    basis = jax.ShapeDtypeStruct((rank, length), BF16)
    pick, *basis_parts = pl.pallas_call(
        functools.partial(pick_kernel, capacity, elements // owners),
        out_shape=[jax.ShapeDtypeStruct((2 * elements, capacity * window), BF16), basis, basis],
        in_specs=[SMEM, VMEM, VMEM, VMEM],
        out_specs=[VMEM] * 3,
        compiler_params=BIG,
        name="pick",
    )(table, slot_order[0], order_next, start_basis)
    bricks = pl.pallas_call(
        order_kernel,
        out_shape=[jax.ShapeDtypeStruct((elements, points), F32)] * 2,
        in_specs=[VMEM] * 6,
        out_specs=[VMEM] * 2,
        compiler_params=BIG,
        name="order",
    )(pick, zero, one, swapped, back, back_two)

    blocks = owners // 2
    chips = masks("fib", 2, owners)[::-1]
    both = jnp.concatenate([b.reshape(blocks, 2 * length // owners, tile) for b in bricks], axis=1)
    got = {step: crossed(both[step], chips, step, 1) for step in range(blocks - 1, -1, -1)}
    parts = [got[step] for step in range(blocks)]
    if length // owners % SLAB:
        at = lax.axis_index("fib") // 2 ^ jnp.arange(blocks)
        whole = jnp.stack(parts)[at].reshape(blocks, 2, 2, length // owners, tile)
        parts = [whole.transpose(0, 1, 3, 2, 4).reshape(length, 2 * tile)]

    mid = masks("fib", 2, 4) + masks("pln", 1, planes)
    distant = masks("fib", 4, owners)[::-1]
    count = 2 ** len(mid)
    chunk = jax.ShapeDtypeStruct((length // count, rank), F32)
    *chunks, field = pl.pallas_call(
        functools.partial(image_kernel, mid),
        out_shape=[chunk] * count + [jax.ShapeDtypeStruct((length, 2 * tile), F32)],
        in_specs=[VMEM] * (len(parts) + 2),
        out_specs=[VMEM] * (count + 1),
        scratch_shapes=[pltpu.VMEM((length, rank), F32)],
        compiler_params=BIG,
        name="image",
    )(*parts, *basis_parts)
    field_part = jax.ShapeDtypeStruct((length, 2 * tile), BF16)
    field_halves = pl.pallas_call(
        split_kernel,
        out_shape=[field_part] * 2,
        in_specs=[VMEM],
        out_specs=[VMEM] * 2,
        compiler_params=BIG,
        name="split",
    )(crossed(field, mid, 0, 0))
    total = sum(crossed(chunks[step], mid, step, 0) for step in range(count - 1, -1, -1))
    total = sum(crossed(total, distant, step, 1) for step in range(2 ** len(distant) - 1, -1, -1))
    chunks = [crossed(total, mid, step, 0) for step in range(count)]
    first, second = pl.pallas_call(
        functools.partial(factor_kernel, mid),
        out_shape=[jax.ShapeDtypeStruct((rank, tile), F32)] * 2,
        in_specs=[VMEM] * (2 + count),
        out_specs=[VMEM] * 2,
        scratch_shapes=[
            pltpu.VMEM((length, rank), F32),
            pltpu.VMEM((rank, rank + 2 * tile), F32),
            pltpu.VMEM((BLOCK, rank + 2 * tile), F32),
        ],
        compiler_params=BIG,
        name="factor",
    )(*field_halves, *chunks)
    core_values = first + lax.ppermute(second, "fib", core_swap)
    return core_values[None, None]


def solution(mesh):
    placed = (P("pln", "fib", None, None), P(), P("pln", None, None), P("pln", "fib", None), P())
    return jax.shard_map(
        per_device,
        mesh=mesh,
        in_specs=placed,
        out_specs=P("pln", "fib", None, None),
        check_vma=False,
    )
```

```python
import functools

import jax
import jax.numpy as jnp
from jax import lax
from jax.experimental import pallas as pl
from jax.experimental.pallas import tpu as pltpu
from jax.sharding import PartitionSpec as P

F32 = jnp.float32
BF16 = jnp.bfloat16
SLAB = 8
BLOCK = 16
KSTEP = 256
VMEM = pl.BlockSpec(memory_space=pltpu.VMEM)
SMEM = pl.BlockSpec(memory_space=pltpu.SMEM)
BIG = pltpu.CompilerParams(vmem_limit_bytes=32 * 1024 * 1024)


def halves(value):
    high = value.astype(BF16)
    return high, (value - high.astype(F32)).astype(BF16)


def dot3(left, right, contract):
    dims = (contract, ((), ()))
    lh, ll = left
    rh, rl = right
    (lk,), (rk,) = contract
    if lh.shape[lk] % 128 == 0:
        longer_left = jnp.concatenate([lh, ll, lh], axis=lk)
        longer_right = jnp.concatenate([rl, rh, rh], axis=rk)
        return lax.dot_general(longer_left, longer_right, dims, preferred_element_type=F32)
    out = lax.dot_general(lh, rl, dims, preferred_element_type=F32)
    out += lax.dot_general(ll, rh, dims, preferred_element_type=F32)
    return out + lax.dot_general(lh, rh, dims, preferred_element_type=F32)


def interp_kernel(owners, table_hbm, node_hbm, interp_hbm, zero_ref, one_ref, two_ref, *scratch):
    grid_scr, node_ref, interp_ref, table_ref, sems = scratch
    rows = zero_ref.shape[0]
    slots, depth = node_ref.shape
    own = lax.axis_index("fib")
    copies = [pltpu.make_async_copy(table_hbm, table_ref, sems.at[0])]
    for part in range(slots // rows):
        at = pl.ds(part * rows, rows)
        copies.append(pltpu.make_async_copy(node_hbm.at[at, :], node_ref.at[at, :], sems.at[len(copies)]))
    steps = [(at, min(KSTEP, depth - at)) for at in range(0, depth, KSTEP)]
    first = len(copies)
    for at, size in steps:
        part = pl.ds(at, size)
        copies.append(
            pltpu.make_async_copy(interp_hbm.at[part, :], interp_ref.at[part, :], sems.at[len(copies)])
        )
    for copy in copies:
        copy.start()
    for copy in copies[:first]:
        copy.wait()
    total = None
    for (at, size), copy in zip(steps, copies[first:]):
        copy.wait()
        part = dot3(
            halves(node_ref[:, at : at + size]), halves(interp_ref[at : at + size, :]), ((1,), (0,))
        )
        total = part if total is None else total + part
    grid_scr[:slots, :] = total
    zero_ref[...] = grid_scr[:rows, :]
    start = table_ref[0, 0, own]
    for distance in range(1, 3):
        shift = lax.rem(start, SLAB)
        at = pl.multiple_of(start - shift, SLAB)
        wide = grid_scr[pl.ds(at, rows + SLAB), :]
        piece = pltpu.roll(wide, lax.rem(rows + SLAB - shift, rows + SLAB), 0)[:rows, :]
        (one_ref, two_ref)[distance - 1][...] = piece
        start = start + table_ref[distance, 0, lax.rem(own + distance, owners)]


def pick_kernel(rows, per_tile, table_ref, order_ref, order_next_ref, start_ref, *refs):
    elements = order_ref.shape[1]
    *outs, high_ref, low_ref = refs
    slots = outs[0].shape[1]
    chip = lax.div(lax.axis_index("fib"), 2)
    rank_at = lax.broadcasted_iota(jnp.int32, (elements, slots), 0)
    slot_at = lax.broadcasted_iota(jnp.int32, (elements, slots), 1)
    row = lax.broadcasted_iota(jnp.int32, (elements, elements), 0)
    for core, order in enumerate((order_ref, order_next_ref)):
        from_slot = jnp.zeros((elements, slots), jnp.bool_)
        start = 0
        for distance in range(slots // rows - 1, -1, -1):
            count = table_ref[distance, 0, 2 * chip + core]
            inside = (rank_at >= start) & (rank_at < start + count)
            from_slot = from_slot | (inside & (slot_at - distance * rows == rank_at - start))
            start = start + count
        place = order[...]
        tile = lax.div(place, jnp.full_like(place, per_tile))
        place = place - tile * per_tile + (tile ^ (2 * chip)) * per_tile
        place = jnp.broadcast_to(place, (elements, elements))
        to_place = jnp.where(place == row, 1.0, 0.0).astype(BF16)
        outs[core][...] = jnp.dot(
            to_place, jnp.where(from_slot, 1.0, 0.0).astype(BF16), preferred_element_type=F32
        ).astype(BF16)
    high_ref[...], low_ref[...] = halves(start_ref[...].T)


def order_kernel(pick_ref, *refs):
    *pieces, out_ref = refs
    high, low = halves(jnp.concatenate([piece[...] for piece in pieces], axis=0))
    out = jnp.dot(pick_ref[...], low, preferred_element_type=F32)
    out_ref[...] = out + jnp.dot(pick_ref[...], high, preferred_element_type=F32)


def bit_place(order):
    index = 0
    for axis, mask in order:
        index = index * 2 + lax.rem(lax.div(lax.axis_index(axis), mask), 2)
    return index


def image_kernel(mid, *refs):
    field_ref, image_scr = refs[-2:]
    count = 2 ** len(mid)
    outs = refs[-2 - count : -2]
    *block_refs, high_ref, low_ref = refs[: -2 - count]
    length, width = field_ref.shape
    tile = width // 2
    chip = lax.div(lax.axis_index("fib"), 2)
    each = length // len(block_refs)
    if len(block_refs) == 1:
        field_ref[...] = block_refs[0][...]
        block_refs = []
    for n, block in enumerate(block_refs):
        owner, step = divmod(n, len(block_refs) // 2)
        at = pl.multiple_of((2 * (chip ^ step) + owner) * each, each)
        for core in range(2):
            field_ref[pl.ds(at, each), core * tile : (core + 1) * tile] = block[core * each : (core + 1) * each, :]
    field = halves(field_ref[...])
    mixed = dot3((high_ref[...], low_ref[...]), field, ((1,), (0,)))
    image_scr[...] = dot3(field, halves(mixed), ((1,), (1,)))
    place = bit_place(mid)
    for step, out in enumerate(outs):
        rows = out.shape[0]
        at = pl.multiple_of((place ^ step) * rows, rows)
        out[...] = image_scr[pl.ds(at, rows), :]


def split_kernel(value_ref, high_ref, low_ref):
    high_ref[...], low_ref[...] = halves(value_ref[...])


def factor_kernel(mid, high_ref, low_ref, *refs):
    chunk_refs, out_refs, image_scr, work, line_scr = refs[:-5], refs[-5:-3], refs[-3], refs[-2], refs[-1]
    rank = image_scr.shape[1]
    place = bit_place(mid)
    for step, chunk in enumerate(chunk_refs):
        rows = chunk.shape[0]
        at = pl.multiple_of((place ^ step) * rows, rows)
        image_scr[pl.ds(at, rows), :] = chunk[...]
    image = image_scr[...]
    image = halves(image * lax.rsqrt(jnp.sum(image * image, axis=0, keepdims=True)))
    work[:, :rank] = dot3(image, image, ((0,), (0,)))
    work[:, rank:] = dot3(image, (high_ref[...], low_ref[...]), ((0,), (0,)))
    width = work.shape[1]

    def splat(row, lane):
        return jnp.broadcast_to(row[:, lane : lane + 1], (1, rank))

    def scaled(factor, row):
        return row * jnp.concatenate([factor] * (width // rank), axis=1)

    for base in range(0, rank, BLOCK):
        line = [work[base + k : base + k + 1, :] for k in range(BLOCK)]
        for slab in range(0, BLOCK, SLAB):
            ahead = base + slab
            entry = [[splat(line[slab + k], ahead + i) for i in range(SLAB)] for k in range(SLAB)]
            for k in range(0, SLAB, 2):
                p, q, r = entry[k][k], entry[k][k + 1], entry[k + 1][k + 1]
                root = lax.rsqrt(p)
                scales = (root, lax.rsqrt(p * r - q * q) * (p * root))
                for n, scale in zip((k, k + 1), scales):
                    row = scaled(scale, line[slab + n])
                    factor = {i: entry[n][i] * scale for i in range(n + 1, SLAB)}
                    for i in range(n + 1, SLAB):
                        for j in range(i, SLAB):
                            entry[i][j] = entry[i][j] - factor[i] * factor[j]
                        line[slab + i] = line[slab + i] - scaled(factor[i], row)
                    line[slab + n] = row
                    for core, out in enumerate(out_refs):
                        out[ahead + n : ahead + n + 1, :] = row[:, (core + 1) * rank : (core + 2) * rank]
                    line_scr[slab + n : slab + n + 1, :] = row
            for i in range(slab + SLAB, BLOCK):
                for k in range(slab, slab + SLAB):
                    line[i] = line[i] - scaled(splat(line[k], base + i), line[k])
        after = base + BLOCK
        if after < rank:
            rows = line_scr[...]
            high = rows.astype(BF16).astype(F32)
            rest = rows - high
            mid_part = rest.astype(BF16).astype(F32)
            low = rest - mid_part
            first = jnp.concatenate([x[:, :rank] for x in (high, high, mid_part, high, low, mid_part)], axis=0)
            second = jnp.concatenate([high, mid_part, high, low, high, mid_part], axis=0)
            drop = lax.dot_general(
                first.astype(BF16),
                second.astype(BF16),
                (((0,), (0,)), ((), ())),
                preferred_element_type=F32,
            )
            work[after:, :] = work[after:, :] - drop[after:, :]

    @pl.when(lax.rem(lax.axis_index("fib"), 2) == 1)
    def _():
        for out in out_refs:
            out[...] = jnp.zeros_like(out)


def crossed(value, bits, step, to_core):
    apart = [bit for at, bit in enumerate(reversed(bits)) if step >> at & 1]
    peers = {axis: sum(mask for name, mask in apart if name == axis) for axis in ("fib", "pln")}
    owners, planes = lax.axis_size("fib"), lax.axis_size("pln")
    pairs = []
    for i in range(owners * planes):
        fib, pln = divmod(i, planes)
        if fib % 2 != to_core:
            fib, pln = fib ^ peers["fib"], pln ^ peers["pln"]
        pairs.append((i, (fib ^ 1) * planes + pln))
    return lax.ppermute(value, ("fib", "pln"), pairs)


def masks(axis, low, high):
    out = []
    while low < high:
        out.append((axis, low))
        low *= 2
    return out


def per_device(nodal_values, interp_matrix, count_table, slot_order, start_basis):
    nodes = nodal_values[0, 0]
    table = jnp.transpose(count_table, (2, 0, 1))
    owners = lax.axis_size("fib")
    planes = lax.axis_size("pln")
    window = table.shape[0]
    capacity = nodes.shape[0] // window
    points = interp_matrix.shape[1]
    elements = slot_order.shape[2]
    length, rank = start_basis.shape
    tile = points * elements // length
    core_swap = [(i, i ^ 1) for i in range(owners)]
    forward = [(i, (i + 1) % owners) for i in range(owners)]

    order_next = lax.ppermute(slot_order[0], "fib", core_swap)
    piece = jax.ShapeDtypeStruct((capacity, points), F32)
    copies = 1 + window + pl.cdiv(nodes.shape[1], KSTEP)
    zero, one, two = pl.pallas_call(
        functools.partial(interp_kernel, owners),
        out_shape=[piece] * 3,
        in_specs=[pl.BlockSpec(memory_space=pl.ANY)] * 3,
        out_specs=[VMEM] * 3,
        scratch_shapes=[
            pltpu.VMEM((nodes.shape[0] + SLAB, points), F32),
            pltpu.VMEM(nodes.shape, F32),
            pltpu.VMEM(interp_matrix.shape, F32),
            pltpu.SMEM(table.shape, jnp.int32),
            pltpu.SemaphoreType.DMA((copies,)),
        ],
        compiler_params=BIG,
        name="interp",
    )(*(pltpu.with_memory_space_constraint(x, pltpu.HBM) for x in (table, nodes, interp_matrix)))
    back = lax.ppermute(two, "fib", forward)
    next_zero = lax.ppermute(zero, "fib", core_swap)
    back_one = lax.ppermute(one, "fib", forward)
    back_two = lax.ppermute(back, "fib", forward)
    basis = jax.ShapeDtypeStruct((rank, length), BF16)
    first_pick, second_pick, *basis_parts = pl.pallas_call(
        functools.partial(pick_kernel, capacity, elements // owners),
        out_shape=[jax.ShapeDtypeStruct((elements, capacity * window), BF16)] * 2 + [basis] * 2,
        in_specs=[SMEM, VMEM, VMEM, VMEM],
        out_specs=[VMEM] * 4,
        compiler_params=BIG,
        name="pick",
    )(table, slot_order[0], order_next, start_basis)
    order = pl.pallas_call(
        order_kernel,
        out_shape=jax.ShapeDtypeStruct((elements, points), F32),
        in_specs=[VMEM] * (1 + window),
        out_specs=VMEM,
        compiler_params=BIG,
        name="order",
    )

    blocks = owners // 2
    chips = masks("fib", 2, owners)[::-1]
    parts = [None] * owners
    for owner, brick in (
        (1, order(second_pick, next_zero, one, back)),
        (0, order(first_pick, zero, back_one, back_two)),
    ):
        brick = brick.reshape(blocks, 2 * length // owners, tile)
        for step in range(blocks - 1, -1, -1):
            parts[owner * blocks + step] = crossed(brick[step], chips, step, 1)
    if length // owners % SLAB:
        at = lax.axis_index("fib") // 2 ^ jnp.arange(blocks)
        whole = jnp.stack(parts).reshape(2, blocks, 2, length // owners, tile)[:, at]
        parts = [whole.transpose(1, 0, 3, 2, 4).reshape(length, 2 * tile)]

    mid = masks("fib", 2, 4) + masks("pln", 1, planes)
    distant = masks("fib", 4, owners)[::-1]
    count = 2 ** len(mid)
    chunk = jax.ShapeDtypeStruct((length // count, rank), F32)
    *chunks, field = pl.pallas_call(
        functools.partial(image_kernel, mid),
        out_shape=[chunk] * count + [jax.ShapeDtypeStruct((length, 2 * tile), F32)],
        in_specs=[VMEM] * (len(parts) + 2),
        out_specs=[VMEM] * (count + 1),
        scratch_shapes=[pltpu.VMEM((length, rank), F32)],
        compiler_params=BIG,
        name="image",
    )(*parts, *basis_parts)
    field_part = jax.ShapeDtypeStruct((length, 2 * tile), BF16)
    field_halves = pl.pallas_call(
        split_kernel,
        out_shape=[field_part] * 2,
        in_specs=[VMEM],
        out_specs=[VMEM] * 2,
        compiler_params=BIG,
        name="split",
    )(crossed(field, mid, 0, 0))
    total = sum(crossed(chunks[step], mid, step, 0) for step in range(count - 1, -1, -1))
    total = sum(crossed(total, distant, step, 1) for step in range(2 ** len(distant) - 1, -1, -1))
    chunks = [crossed(total, mid, step, 0) for step in range(count)]
    first, second = pl.pallas_call(
        functools.partial(factor_kernel, mid),
        out_shape=[jax.ShapeDtypeStruct((rank, tile), F32)] * 2,
        in_specs=[VMEM] * (2 + count),
        out_specs=[VMEM] * 2,
        scratch_shapes=[
            pltpu.VMEM((length, rank), F32),
            pltpu.VMEM((rank, rank + 2 * tile), F32),
            pltpu.VMEM((BLOCK, rank + 2 * tile), F32),
        ],
        compiler_params=BIG,
        name="factor",
    )(*field_halves, *chunks)
    core_values = first + lax.ppermute(second, "fib", core_swap)
    return core_values[None, None]


def solution(mesh):
    placed = (P("pln", "fib", None, None), P(), P("pln", None, None), P("pln", "fib", None), P())
    return jax.shard_map(
        per_device,
        mesh=mesh,
        in_specs=placed,
        out_specs=P("pln", "fib", None, None),
        check_vma=False,
    )
```

```python
import functools

import jax
import jax.numpy as jnp
from jax import lax
from jax.experimental import pallas as pl
from jax.experimental.pallas import tpu as pltpu
from jax.sharding import PartitionSpec as P

F32 = jnp.float32
BF16 = jnp.bfloat16
SLAB = 8
BLOCK = 16
KSTEP = 256
VMEM = pl.BlockSpec(memory_space=pltpu.VMEM)
SMEM = pl.BlockSpec(memory_space=pltpu.SMEM)
BIG = pltpu.CompilerParams(vmem_limit_bytes=32 * 1024 * 1024)


def halves(value):
    high = value.astype(BF16)
    return high, (value - high.astype(F32)).astype(BF16)


def dot3(left, right, contract):
    dims = (contract, ((), ()))
    lh, ll = left
    rh, rl = right
    (lk,), (rk,) = contract
    if lh.shape[lk] % 128 == 0:
        longer_left = jnp.concatenate([lh, ll, lh], axis=lk)
        longer_right = jnp.concatenate([rl, rh, rh], axis=rk)
        return lax.dot_general(longer_left, longer_right, dims, preferred_element_type=F32)
    out = lax.dot_general(lh, rl, dims, preferred_element_type=F32)
    out += lax.dot_general(ll, rh, dims, preferred_element_type=F32)
    return out + lax.dot_general(lh, rh, dims, preferred_element_type=F32)


def interp_kernel(owners, table_hbm, node_hbm, interp_hbm, swap_ref, one_ref, send_ref, zero_ref, *scratch):
    grid_scr, node_ref, interp_ref, table_ref, sems = scratch
    rows = zero_ref.shape[0]
    slots, depth = node_ref.shape
    own = lax.axis_index("fib")
    copies = [pltpu.make_async_copy(table_hbm, table_ref, sems.at[0])]
    for part in range(slots // rows):
        at = pl.ds(part * rows, rows)
        copies.append(pltpu.make_async_copy(node_hbm.at[at, :], node_ref.at[at, :], sems.at[len(copies)]))
    steps = [(at, min(KSTEP, depth - at)) for at in range(0, depth, KSTEP)]
    first = len(copies)
    for at, size in steps:
        part = pl.ds(at, size)
        copies.append(
            pltpu.make_async_copy(interp_hbm.at[part, :], interp_ref.at[part, :], sems.at[len(copies)])
        )
    for copy in copies:
        copy.start()
    for copy in copies[:first]:
        copy.wait()
    total = None
    for (at, size), copy in zip(steps, copies[first:]):
        copy.wait()
        part = dot3(
            halves(node_ref[:, at : at + size]), halves(interp_ref[at : at + size, :]), ((1,), (0,))
        )
        total = part if total is None else total + part
    grid_scr[:slots, :] = total
    zero_ref[...] = grid_scr[:rows, :]
    start = table_ref[0, 0, own]
    for distance in range(1, 3):
        shift = lax.rem(start, SLAB)
        at = pl.multiple_of(start - shift, SLAB)
        wide = grid_scr[pl.ds(at, rows + SLAB), :]
        piece = pltpu.roll(wide, lax.rem(rows + SLAB - shift, rows + SLAB), 0)[:rows, :]
        if distance == 1:
            one_ref[...] = piece
            send_ref[:rows, :] = piece
        else:
            send_ref[rows:, :] = piece
        start = start + table_ref[distance, 0, lax.rem(own + distance, owners)]
    second = lax.rem(own, 2) == 1

    @pl.when(second)
    def _():
        swap_ref[...] = zero_ref[...]

    @pl.when(jnp.logical_not(second))
    def _():
        swap_ref[...] = send_ref[rows:, :]


def pick_kernel(rows, per_tile, table_ref, order_ref, order_next_ref, start_ref, out_ref, high_ref, low_ref):
    elements = order_ref.shape[1]
    slots = out_ref.shape[1]
    chip = lax.div(lax.axis_index("fib"), 2)
    rank_at = lax.broadcasted_iota(jnp.int32, (elements, slots), 0)
    slot_at = lax.broadcasted_iota(jnp.int32, (elements, slots), 1)
    row = lax.broadcasted_iota(jnp.int32, (elements, elements), 0)
    for core, order in enumerate((order_ref, order_next_ref)):
        from_slot = jnp.zeros((elements, slots), jnp.bool_)
        start = 0
        for distance in range(slots // rows - 1, -1, -1):
            count = table_ref[distance, 0, 2 * chip + core]
            inside = (rank_at >= start) & (rank_at < start + count)
            from_slot = from_slot | (inside & (slot_at - distance * rows == rank_at - start))
            start = start + count
        place = order[...]
        tile = lax.div(place, jnp.full_like(place, per_tile))
        place = place - tile * per_tile + (tile ^ (2 * chip)) * per_tile
        place = jnp.broadcast_to(place, (elements, elements))
        to_place = jnp.where(place == row, 1.0, 0.0).astype(BF16)
        out_ref[core * elements : (core + 1) * elements, :] = jnp.dot(
            to_place, jnp.where(from_slot, 1.0, 0.0).astype(BF16), preferred_element_type=F32
        ).astype(BF16)
    high_ref[...], low_ref[...] = halves(start_ref[...].T)


def order_kernel(pick_ref, zero_ref, one_ref, next_zero_ref, back_ref, back_two_ref, *outs):
    rows = zero_ref.shape[0]
    elements = outs[0].shape[0]
    sources = (
        (zero_ref[...], back_ref[:rows, :], back_two_ref[...]),
        (next_zero_ref[...], one_ref[...], back_ref[rows:, :]),
    )
    for core, pieces in enumerate(sources):
        pick = pick_ref[core * elements : (core + 1) * elements, :]
        high, low = halves(jnp.concatenate(pieces, axis=0))
        out = jnp.dot(pick, low, preferred_element_type=F32)
        outs[core][...] = out + jnp.dot(pick, high, preferred_element_type=F32)


def bit_place(order):
    index = 0
    for axis, mask in order:
        index = index * 2 + lax.rem(lax.div(lax.axis_index(axis), mask), 2)
    return index


def image_kernel(mid, *refs):
    field_ref, image_scr = refs[-2:]
    count = 2 ** len(mid)
    outs = refs[-2 - count : -2]
    *block_refs, high_ref, low_ref = refs[: -2 - count]
    length, width = field_ref.shape
    tile = width // 2
    chip = lax.div(lax.axis_index("fib"), 2)
    each = length // (2 * len(block_refs))
    if len(block_refs) == 1:
        field_ref[...] = block_refs[0][...]
        block_refs = []
    for step, block in enumerate(block_refs):
        for owner in range(2):
            at = pl.multiple_of((2 * (chip ^ step) + owner) * each, each)
            for core in range(2):
                part = (2 * owner + core) * each
                field_ref[pl.ds(at, each), core * tile : (core + 1) * tile] = block[part : part + each, :]
    field = halves(field_ref[...])
    mixed = dot3((high_ref[...], low_ref[...]), field, ((1,), (0,)))
    image_scr[...] = dot3(field, halves(mixed), ((1,), (1,)))
    place = bit_place(mid)
    for step, out in enumerate(outs):
        rows = out.shape[0]
        at = pl.multiple_of((place ^ step) * rows, rows)
        out[...] = image_scr[pl.ds(at, rows), :]


def split_kernel(value_ref, high_ref, low_ref):
    high_ref[...], low_ref[...] = halves(value_ref[...])


def factor_kernel(mid, high_ref, low_ref, *refs):
    chunk_refs, out_refs, image_scr, work, line_scr = refs[:-5], refs[-5:-3], refs[-3], refs[-2], refs[-1]
    rank = image_scr.shape[1]
    place = bit_place(mid)
    for step, chunk in enumerate(chunk_refs):
        rows = chunk.shape[0]
        at = pl.multiple_of((place ^ step) * rows, rows)
        image_scr[pl.ds(at, rows), :] = chunk[...]
    image = image_scr[...]
    image = halves(image * lax.rsqrt(jnp.sum(image * image, axis=0, keepdims=True)))
    work[:, :rank] = dot3(image, image, ((0,), (0,)))
    work[:, rank:] = dot3(image, (high_ref[...], low_ref[...]), ((0,), (0,)))
    width = work.shape[1]

    def splat(row, lane):
        return jnp.broadcast_to(row[:, lane : lane + 1], (1, rank))

    def scaled(factor, row):
        return row * jnp.concatenate([factor] * (width // rank), axis=1)

    for base in range(0, rank, BLOCK):
        line = [work[base + k : base + k + 1, :] for k in range(BLOCK)]
        for slab in range(0, BLOCK, SLAB):
            ahead = base + slab
            entry = [[splat(line[slab + k], ahead + i) for i in range(SLAB)] for k in range(SLAB)]
            for k in range(0, SLAB, 2):
                p, q, r = entry[k][k], entry[k][k + 1], entry[k + 1][k + 1]
                root = lax.rsqrt(p)
                scales = (root, lax.rsqrt(p * r - q * q) * (p * root))
                for n, scale in zip((k, k + 1), scales):
                    row = scaled(scale, line[slab + n])
                    factor = {i: entry[n][i] * scale for i in range(n + 1, SLAB)}
                    for i in range(n + 1, SLAB):
                        for j in range(i, SLAB):
                            entry[i][j] = entry[i][j] - factor[i] * factor[j]
                        line[slab + i] = line[slab + i] - scaled(factor[i], row)
                    line[slab + n] = row
                    for core, out in enumerate(out_refs):
                        out[ahead + n : ahead + n + 1, :] = row[:, (core + 1) * rank : (core + 2) * rank]
                    line_scr[slab + n : slab + n + 1, :] = row
            for i in range(slab + SLAB, BLOCK):
                for k in range(slab, slab + SLAB):
                    line[i] = line[i] - scaled(splat(line[k], base + i), line[k])
        after = base + BLOCK
        if after < rank:
            rows = line_scr[...]
            high = rows.astype(BF16).astype(F32)
            rest = rows - high
            mid_part = rest.astype(BF16).astype(F32)
            low = rest - mid_part
            first = jnp.concatenate([x[:, :rank] for x in (high, high, mid_part, high, low, mid_part)], axis=0)
            second = jnp.concatenate([high, mid_part, high, low, high, mid_part], axis=0)
            drop = lax.dot_general(
                first.astype(BF16),
                second.astype(BF16),
                (((0,), (0,)), ((), ())),
                preferred_element_type=F32,
            )
            work[after:, :] = work[after:, :] - drop[after:, :]

    @pl.when(lax.rem(lax.axis_index("fib"), 2) == 1)
    def _():
        for out in out_refs:
            out[...] = jnp.zeros_like(out)


def crossed(value, bits, step, to_core):
    apart = [bit for at, bit in enumerate(reversed(bits)) if step >> at & 1]
    peers = {axis: sum(mask for name, mask in apart if name == axis) for axis in ("fib", "pln")}
    owners, planes = lax.axis_size("fib"), lax.axis_size("pln")
    pairs = []
    for i in range(owners * planes):
        fib, pln = divmod(i, planes)
        if fib % 2 != to_core:
            fib, pln = fib ^ peers["fib"], pln ^ peers["pln"]
        pairs.append((i, (fib ^ 1) * planes + pln))
    return lax.ppermute(value, ("fib", "pln"), pairs)


def masks(axis, low, high):
    out = []
    while low < high:
        out.append((axis, low))
        low *= 2
    return out


def per_device(nodal_values, interp_matrix, count_table, slot_order, start_basis):
    nodes = nodal_values[0, 0]
    table = jnp.transpose(count_table, (2, 0, 1))
    owners = lax.axis_size("fib")
    planes = lax.axis_size("pln")
    window = table.shape[0]
    capacity = nodes.shape[0] // window
    points = interp_matrix.shape[1]
    elements = slot_order.shape[2]
    length, rank = start_basis.shape
    tile = points * elements // length
    core_swap = [(i, i ^ 1) for i in range(owners)]
    forward = [(i, (i + 1) % owners) for i in range(owners)]

    order_next = lax.ppermute(slot_order[0], "fib", core_swap)
    piece = jax.ShapeDtypeStruct((capacity, points), F32)
    copies = 1 + window + pl.cdiv(nodes.shape[1], KSTEP)
    swap, one, send, zero = pl.pallas_call(
        functools.partial(interp_kernel, owners),
        out_shape=[piece, piece, jax.ShapeDtypeStruct((2 * capacity, points), F32), piece],
        in_specs=[pl.BlockSpec(memory_space=pl.ANY)] * 3,
        out_specs=[VMEM] * 4,
        scratch_shapes=[
            pltpu.VMEM((nodes.shape[0] + SLAB, points), F32),
            pltpu.VMEM(nodes.shape, F32),
            pltpu.VMEM(interp_matrix.shape, F32),
            pltpu.SMEM(table.shape, jnp.int32),
            pltpu.SemaphoreType.DMA((copies,)),
        ],
        compiler_params=BIG,
        name="interp",
    )(*(pltpu.with_memory_space_constraint(x, pltpu.HBM) for x in (table, nodes, interp_matrix)))
    swapped = lax.ppermute(swap, "fib", core_swap)
    back = lax.ppermute(send, "fib", forward)
    back_two = lax.ppermute(swapped, "fib", forward)
    basis = jax.ShapeDtypeStruct((rank, length), BF16)
    pick, *basis_parts = pl.pallas_call(
        functools.partial(pick_kernel, capacity, elements // owners),
        out_shape=[jax.ShapeDtypeStruct((2 * elements, capacity * window), BF16), basis, basis],
        in_specs=[SMEM, VMEM, VMEM, VMEM],
        out_specs=[VMEM] * 3,
        compiler_params=BIG,
        name="pick",
    )(table, slot_order[0], order_next, start_basis)
    bricks = pl.pallas_call(
        order_kernel,
        out_shape=[jax.ShapeDtypeStruct((elements, points), F32)] * 2,
        in_specs=[VMEM] * 6,
        out_specs=[VMEM] * 2,
        compiler_params=BIG,
        name="order",
    )(pick, zero, one, swapped, back, back_two)

    blocks = owners // 2
    chips = masks("fib", 2, owners)[::-1]
    both = jnp.concatenate([b.reshape(blocks, 2 * length // owners, tile) for b in bricks], axis=1)
    got = {step: crossed(both[step], chips, step, 1) for step in range(blocks - 1, -1, -1)}
    parts = [got[step] for step in range(blocks)]
    if length // owners % SLAB:
        at = lax.axis_index("fib") // 2 ^ jnp.arange(blocks)
        whole = jnp.stack(parts)[at].reshape(blocks, 2, 2, length // owners, tile)
        parts = [whole.transpose(0, 1, 3, 2, 4).reshape(length, 2 * tile)]

    mid = masks("fib", 2, 4) + masks("pln", 1, planes)
    distant = masks("fib", 4, owners)[::-1]
    count = 2 ** len(mid)
    chunk = jax.ShapeDtypeStruct((length // count, rank), F32)
    *chunks, field = pl.pallas_call(
        functools.partial(image_kernel, mid),
        out_shape=[chunk] * count + [jax.ShapeDtypeStruct((length, 2 * tile), F32)],
        in_specs=[VMEM] * (len(parts) + 2),
        out_specs=[VMEM] * (count + 1),
        scratch_shapes=[pltpu.VMEM((length, rank), F32)],
        compiler_params=BIG,
        name="image",
    )(*parts, *basis_parts)
    total = sum(crossed(chunks[step], mid, step, 0) for step in range(count - 1, -1, -1))
    field, total = lax.optimization_barrier((field, total))
    field_part = jax.ShapeDtypeStruct((length, 2 * tile), BF16)
    field_halves = pl.pallas_call(
        split_kernel,
        out_shape=[field_part] * 2,
        in_specs=[VMEM],
        out_specs=[VMEM] * 2,
        compiler_params=BIG,
        name="split",
    )(crossed(field, mid, 0, 0))
    total = sum(crossed(total, distant, step, 1) for step in range(2 ** len(distant) - 1, -1, -1))
    chunks = [crossed(total, mid, step, 0) for step in range(count)]
    first, second = pl.pallas_call(
        functools.partial(factor_kernel, mid),
        out_shape=[jax.ShapeDtypeStruct((rank, tile), F32)] * 2,
        in_specs=[VMEM] * (2 + count),
        out_specs=[VMEM] * 2,
        scratch_shapes=[
            pltpu.VMEM((length, rank), F32),
            pltpu.VMEM((rank, rank + 2 * tile), F32),
            pltpu.VMEM((BLOCK, rank + 2 * tile), F32),
        ],
        compiler_params=BIG,
        name="factor",
    )(*field_halves, *chunks)
    core_values = first + lax.ppermute(second, "fib", core_swap)
    return core_values[None, None]


def solution(mesh):
    placed = (P("pln", "fib", None, None), P(), P("pln", None, None), P("pln", "fib", None), P())
    return jax.shard_map(
        per_device,
        mesh=mesh,
        in_specs=placed,
        out_specs=P("pln", "fib", None, None),
        check_vma=False,
    )
```

```python
import functools

import jax
import jax.numpy as jnp
from jax import lax
from jax.experimental import pallas as pl
from jax.experimental.pallas import tpu as pltpu
from jax.sharding import PartitionSpec as P

F32 = jnp.float32
BF16 = jnp.bfloat16
SLAB = 8
BLOCK = 16
KSTEP = 128
VMEM = pl.BlockSpec(memory_space=pltpu.VMEM)
SMEM = pl.BlockSpec(memory_space=pltpu.SMEM)
BIG = pltpu.CompilerParams(vmem_limit_bytes=32 * 1024 * 1024)


def halves(value):
    high = value.astype(BF16)
    return high, (value - high.astype(F32)).astype(BF16)


def dot3(left, right, contract):
    dims = (contract, ((), ()))
    lh, ll = left
    rh, rl = right
    (lk,), (rk,) = contract
    if lh.shape[lk] % 128 == 0:
        longer_left = jnp.concatenate([lh, ll, lh], axis=lk)
        longer_right = jnp.concatenate([rl, rh, rh], axis=rk)
        return lax.dot_general(longer_left, longer_right, dims, preferred_element_type=F32)
    out = lax.dot_general(lh, rl, dims, preferred_element_type=F32)
    out += lax.dot_general(ll, rh, dims, preferred_element_type=F32)
    return out + lax.dot_general(lh, rh, dims, preferred_element_type=F32)


def interp_kernel(owners, table_hbm, node_hbm, interp_hbm, swap_ref, one_ref, send_ref, zero_ref, *scratch):
    grid_scr, node_ref, interp_ref, table_ref, sems = scratch
    rows = zero_ref.shape[0]
    slots, depth = node_ref.shape
    own = lax.axis_index("fib")
    copies = [pltpu.make_async_copy(table_hbm, table_ref, sems.at[0])]
    for part in range(slots // rows):
        at = pl.ds(part * rows, rows)
        copies.append(pltpu.make_async_copy(node_hbm.at[at, :], node_ref.at[at, :], sems.at[len(copies)]))
    steps = [(at, min(KSTEP, depth - at)) for at in range(0, depth, KSTEP)]
    first = len(copies)
    for at, size in steps:
        part = pl.ds(at, size)
        copies.append(
            pltpu.make_async_copy(interp_hbm.at[part, :], interp_ref.at[part, :], sems.at[len(copies)])
        )
    for copy in copies:
        copy.start()
    for copy in copies[:first]:
        copy.wait()
    total = None
    for (at, size), copy in zip(steps, copies[first:]):
        copy.wait()
        part = dot3(
            halves(node_ref[:, at : at + size]), halves(interp_ref[at : at + size, :]), ((1,), (0,))
        )
        total = part if total is None else total + part
    grid_scr[:slots, :] = total
    zero_ref[...] = grid_scr[:rows, :]
    start = table_ref[0, 0, own]
    for distance in range(1, 3):
        shift = lax.rem(start, SLAB)
        at = pl.multiple_of(start - shift, SLAB)
        wide = grid_scr[pl.ds(at, rows + SLAB), :]
        piece = pltpu.roll(wide, lax.rem(rows + SLAB - shift, rows + SLAB), 0)[:rows, :]
        if distance == 1:
            one_ref[...] = piece
            send_ref[:rows, :] = piece
        else:
            send_ref[rows:, :] = piece
        start = start + table_ref[distance, 0, lax.rem(own + distance, owners)]
    second = lax.rem(own, 2) == 1

    @pl.when(second)
    def _():
        swap_ref[...] = zero_ref[...]

    @pl.when(jnp.logical_not(second))
    def _():
        swap_ref[...] = send_ref[rows:, :]


def pick_kernel(rows, per_tile, table_ref, order_ref, order_next_ref, start_ref, out_ref, high_ref, low_ref):
    elements = order_ref.shape[1]
    slots = out_ref.shape[1]
    chip = lax.div(lax.axis_index("fib"), 2)
    rank_at = lax.broadcasted_iota(jnp.int32, (elements, slots), 0)
    slot_at = lax.broadcasted_iota(jnp.int32, (elements, slots), 1)
    row = lax.broadcasted_iota(jnp.int32, (elements, elements), 0)
    for core, order in enumerate((order_ref, order_next_ref)):
        from_slot = jnp.zeros((elements, slots), jnp.bool_)
        start = 0
        for distance in range(slots // rows - 1, -1, -1):
            count = table_ref[distance, 0, 2 * chip + core]
            inside = (rank_at >= start) & (rank_at < start + count)
            from_slot = from_slot | (inside & (slot_at - distance * rows == rank_at - start))
            start = start + count
        place = order[...]
        tile = lax.div(place, jnp.full_like(place, per_tile))
        place = place - tile * per_tile + (tile ^ (2 * chip)) * per_tile
        place = jnp.broadcast_to(place, (elements, elements))
        to_place = jnp.where(place == row, 1.0, 0.0).astype(BF16)
        out_ref[core * elements : (core + 1) * elements, :] = jnp.dot(
            to_place, jnp.where(from_slot, 1.0, 0.0).astype(BF16), preferred_element_type=F32
        ).astype(BF16)
    high_ref[...], low_ref[...] = halves(start_ref[...].T)


def order_kernel(pick_ref, zero_ref, one_ref, next_zero_ref, back_ref, back_two_ref, *outs):
    rows = zero_ref.shape[0]
    elements = outs[0].shape[0]
    sources = (
        (zero_ref[...], back_ref[:rows, :], back_two_ref[...]),
        (next_zero_ref[...], one_ref[...], back_ref[rows:, :]),
    )
    for core, pieces in enumerate(sources):
        pick = pick_ref[core * elements : (core + 1) * elements, :]
        high, low = halves(jnp.concatenate(pieces, axis=0))
        out = jnp.dot(pick, low, preferred_element_type=F32)
        outs[core][...] = out + jnp.dot(pick, high, preferred_element_type=F32)


def bit_place(order):
    index = 0
    for axis, mask in order:
        index = index * 2 + lax.rem(lax.div(lax.axis_index(axis), mask), 2)
    return index


def image_kernel(mid, *refs):
    field_ref, image_scr = refs[-2:]
    count = 2 ** len(mid)
    outs = refs[-2 - count : -2]
    *block_refs, high_ref, low_ref = refs[: -2 - count]
    length, width = field_ref.shape
    tile = width // 2
    chip = lax.div(lax.axis_index("fib"), 2)
    each = length // (2 * len(block_refs))
    if len(block_refs) == 1:
        field_ref[...] = block_refs[0][...]
        block_refs = []
    for step, block in enumerate(block_refs):
        for owner in range(2):
            at = pl.multiple_of((2 * (chip ^ step) + owner) * each, each)
            for core in range(2):
                part = (2 * owner + core) * each
                field_ref[pl.ds(at, each), core * tile : (core + 1) * tile] = block[part : part + each, :]
    field = halves(field_ref[...])
    mixed = dot3((high_ref[...], low_ref[...]), field, ((1,), (0,)))
    image_scr[...] = dot3(field, halves(mixed), ((1,), (1,)))
    place = bit_place(mid)
    for step, out in enumerate(outs):
        rows = out.shape[0]
        at = pl.multiple_of((place ^ step) * rows, rows)
        out[...] = image_scr[pl.ds(at, rows), :]


def split_kernel(value_ref, high_ref, low_ref):
    high_ref[...], low_ref[...] = halves(value_ref[...])


def factor_kernel(mid, high_ref, low_ref, *refs):
    chunk_refs, out_refs, image_scr, work, line_scr = refs[:-5], refs[-5:-3], refs[-3], refs[-2], refs[-1]
    rank = image_scr.shape[1]
    place = bit_place(mid)
    for step, chunk in enumerate(chunk_refs):
        rows = chunk.shape[0]
        at = pl.multiple_of((place ^ step) * rows, rows)
        image_scr[pl.ds(at, rows), :] = chunk[...]
    image = image_scr[...]
    image = halves(image * lax.rsqrt(jnp.sum(image * image, axis=0, keepdims=True)))
    work[:, :rank] = dot3(image, image, ((0,), (0,)))
    work[:, rank:] = dot3(image, (high_ref[...], low_ref[...]), ((0,), (0,)))
    width = work.shape[1]

    def splat(row, lane):
        return jnp.broadcast_to(row[:, lane : lane + 1], (1, rank))

    def scaled(factor, row):
        return row * jnp.concatenate([factor] * (width // rank), axis=1)

    for base in range(0, rank, BLOCK):
        line = [work[base + k : base + k + 1, :] for k in range(BLOCK)]
        for slab in range(0, BLOCK, SLAB):
            ahead = base + slab
            entry = [[splat(line[slab + k], ahead + i) for i in range(SLAB)] for k in range(SLAB)]
            for k in range(0, SLAB, 2):
                p, q, r = entry[k][k], entry[k][k + 1], entry[k + 1][k + 1]
                root = lax.rsqrt(p)
                scales = (root, lax.rsqrt(p * r - q * q) * (p * root))
                for n, scale in zip((k, k + 1), scales):
                    row = scaled(scale, line[slab + n])
                    factor = {i: entry[n][i] * scale for i in range(n + 1, SLAB)}
                    for i in range(n + 1, SLAB):
                        for j in range(i, SLAB):
                            entry[i][j] = entry[i][j] - factor[i] * factor[j]
                        line[slab + i] = line[slab + i] - scaled(factor[i], row)
                    line[slab + n] = row
                    for core, out in enumerate(out_refs):
                        out[ahead + n : ahead + n + 1, :] = row[:, (core + 1) * rank : (core + 2) * rank]
                    line_scr[slab + n : slab + n + 1, :] = row
            for i in range(slab + SLAB, BLOCK):
                for k in range(slab, slab + SLAB):
                    line[i] = line[i] - scaled(splat(line[k], base + i), line[k])
        after = base + BLOCK
        if after < rank:
            rows = line_scr[...]
            high = rows.astype(BF16).astype(F32)
            low = rows - high
            first = jnp.concatenate([x[:, :rank] for x in (high, high, low)], axis=0)
            second = jnp.concatenate([high, low, high], axis=0)
            drop = lax.dot_general(
                first.astype(BF16),
                second.astype(BF16),
                (((0,), (0,)), ((), ())),
                preferred_element_type=F32,
            )
            work[after:, :] = work[after:, :] - drop[after:, :]

    @pl.when(lax.rem(lax.axis_index("fib"), 2) == 1)
    def _():
        for out in out_refs:
            out[...] = jnp.zeros_like(out)


def crossed(value, bits, step, to_core):
    apart = [bit for at, bit in enumerate(reversed(bits)) if step >> at & 1]
    peers = {axis: sum(mask for name, mask in apart if name == axis) for axis in ("fib", "pln")}
    owners, planes = lax.axis_size("fib"), lax.axis_size("pln")
    pairs = []
    for i in range(owners * planes):
        fib, pln = divmod(i, planes)
        if fib % 2 != to_core:
            fib, pln = fib ^ peers["fib"], pln ^ peers["pln"]
        pairs.append((i, (fib ^ 1) * planes + pln))
    return lax.ppermute(value, ("fib", "pln"), pairs)


def masks(axis, low, high):
    out = []
    while low < high:
        out.append((axis, low))
        low *= 2
    return out


def per_device(nodal_values, interp_matrix, count_table, slot_order, start_basis):
    nodes = nodal_values[0, 0]
    table = jnp.transpose(count_table, (2, 0, 1))
    owners = lax.axis_size("fib")
    planes = lax.axis_size("pln")
    window = table.shape[0]
    capacity = nodes.shape[0] // window
    points = interp_matrix.shape[1]
    elements = slot_order.shape[2]
    length, rank = start_basis.shape
    tile = points * elements // length
    core_swap = [(i, i ^ 1) for i in range(owners)]
    forward = [(i, (i + 1) % owners) for i in range(owners)]

    order_next = lax.ppermute(slot_order[0], "fib", core_swap)
    piece = jax.ShapeDtypeStruct((capacity, points), F32)
    copies = 1 + window + pl.cdiv(nodes.shape[1], KSTEP)
    swap, one, send, zero = pl.pallas_call(
        functools.partial(interp_kernel, owners),
        out_shape=[piece, piece, jax.ShapeDtypeStruct((2 * capacity, points), F32), piece],
        in_specs=[pl.BlockSpec(memory_space=pl.ANY)] * 3,
        out_specs=[VMEM] * 4,
        scratch_shapes=[
            pltpu.VMEM((nodes.shape[0] + SLAB, points), F32),
            pltpu.VMEM(nodes.shape, F32),
            pltpu.VMEM(interp_matrix.shape, F32),
            pltpu.SMEM(table.shape, jnp.int32),
            pltpu.SemaphoreType.DMA((copies,)),
        ],
        compiler_params=BIG,
        name="interp",
    )(*(pltpu.with_memory_space_constraint(x, pltpu.HBM) for x in (table, nodes, interp_matrix)))
    swapped = lax.ppermute(swap, "fib", core_swap)
    back = lax.ppermute(send, "fib", forward)
    back_two = lax.ppermute(swapped, "fib", forward)
    basis = jax.ShapeDtypeStruct((rank, length), BF16)
    pick, *basis_parts = pl.pallas_call(
        functools.partial(pick_kernel, capacity, elements // owners),
        out_shape=[jax.ShapeDtypeStruct((2 * elements, capacity * window), BF16), basis, basis],
        in_specs=[SMEM, VMEM, VMEM, VMEM],
        out_specs=[VMEM] * 3,
        compiler_params=BIG,
        name="pick",
    )(table, slot_order[0], order_next, start_basis)
    bricks = pl.pallas_call(
        order_kernel,
        out_shape=[jax.ShapeDtypeStruct((elements, points), F32)] * 2,
        in_specs=[VMEM] * 6,
        out_specs=[VMEM] * 2,
        compiler_params=BIG,
        name="order",
    )(pick, zero, one, swapped, back, back_two)

    blocks = owners // 2
    chips = masks("fib", 2, owners)[::-1]
    both = jnp.concatenate([b.reshape(blocks, 2 * length // owners, tile) for b in bricks], axis=1)
    got = {step: crossed(both[step], chips, step, 1) for step in range(blocks - 1, -1, -1)}
    parts = [got[step] for step in range(blocks)]
    if length // owners % SLAB:
        at = lax.axis_index("fib") // 2 ^ jnp.arange(blocks)
        whole = jnp.stack(parts)[at].reshape(blocks, 2, 2, length // owners, tile)
        parts = [whole.transpose(0, 1, 3, 2, 4).reshape(length, 2 * tile)]

    mid = masks("fib", 2, 4) + masks("pln", 1, planes)
    distant = masks("fib", 4, owners)[::-1]
    count = 2 ** len(mid)
    chunk = jax.ShapeDtypeStruct((length // count, rank), F32)
    *chunks, field = pl.pallas_call(
        functools.partial(image_kernel, mid),
        out_shape=[chunk] * count + [jax.ShapeDtypeStruct((length, 2 * tile), F32)],
        in_specs=[VMEM] * (len(parts) + 2),
        out_specs=[VMEM] * (count + 1),
        scratch_shapes=[pltpu.VMEM((length, rank), F32)],
        compiler_params=BIG,
        name="image",
    )(*parts, *basis_parts)
    total = sum(crossed(chunks[step], mid, step, 0) for step in range(count - 1, -1, -1))
    field, total = lax.optimization_barrier((field, total))
    field_part = jax.ShapeDtypeStruct((length, 2 * tile), BF16)
    field_halves = pl.pallas_call(
        split_kernel,
        out_shape=[field_part] * 2,
        in_specs=[VMEM],
        out_specs=[VMEM] * 2,
        compiler_params=BIG,
        name="split",
    )(crossed(field, mid, 0, 0))
    total = sum(crossed(total, distant, step, 1) for step in range(2 ** len(distant) - 1, -1, -1))
    chunks = [crossed(total, mid, step, 0) for step in range(count)]
    first, second = pl.pallas_call(
        functools.partial(factor_kernel, mid),
        out_shape=[jax.ShapeDtypeStruct((rank, tile), F32)] * 2,
        in_specs=[VMEM] * (2 + count),
        out_specs=[VMEM] * 2,
        scratch_shapes=[
            pltpu.VMEM((length, rank), F32),
            pltpu.VMEM((rank, rank + 2 * tile), F32),
            pltpu.VMEM((BLOCK, rank + 2 * tile), F32),
        ],
        compiler_params=BIG,
        name="factor",
    )(*field_halves, *chunks)
    core_values = first + lax.ppermute(second, "fib", core_swap)
    return core_values[None, None]


def solution(mesh):
    placed = (P("pln", "fib", None, None), P(), P("pln", None, None), P("pln", "fib", None), P())
    return jax.shard_map(
        per_device,
        mesh=mesh,
        in_specs=placed,
        out_specs=P("pln", "fib", None, None),
        check_vma=False,
    )
```
